32 devices in a mesh: dp: 8 (over z, core), seq: 4 (over y, x).
Axes of the slice: x: 2, y: 2, z: 4, core: 2. Of those that a mesh axis runs over, the one named last changes fastest.
Arguments:
- tokens: bfloat16 [32, 2048, 768], P('dp', 'seq'), may hold values from -6 to 6
- lengths: int32 [32], P('dp'), may hold values from 1024 to 2048, as said below
- cotangent: bfloat16 [32, 2048, 768], P('dp', 'seq'), may hold values from -6 to 6
- w_query: bfloat16 [768, 768], P(('dp', 'seq')), may hold values from -0.21875 to 0.21875
- b_query: bfloat16 [768], P(('dp', 'seq')), may hold values from -3 to 3
- w_key: bfloat16 [768, 768], P(('dp', 'seq')), may hold values from -0.21875 to 0.21875
- w_value: bfloat16 [768, 768], P(('dp', 'seq')), may hold values from -0.21875 to 0.21875
- b_value: bfloat16 [768], P(('dp', 'seq')), may hold values from -0.3125 to 0.3125
- w_out: bfloat16 [768, 768], P(('dp', 'seq')), may hold values from -3.5 to 3.5
- b_out: bfloat16 [768], P(('dp', 'seq')), may hold values from -3 to 3
- gain_one: bfloat16 [768], P(('dp', 'seq')), may hold values from 0.099609375 to 1.8984375
- shift_one: bfloat16 [768], P(('dp', 'seq')), may hold values from -1.75 to 1.75
- w_up: bfloat16 [768, 3072], P(('dp', 'seq')), may hold values from -0.21875 to 0.21875
- b_up: bfloat16 [3072], P(('dp', 'seq')), may hold values from -3 to 3
- w_down: bfloat16 [3072, 768], P(('dp', 'seq')), may hold values from -0.109375 to 0.109375
- b_down: bfloat16 [768], P(('dp', 'seq')), may hold values from -3 to 3
- gain_two: bfloat16 [768], P(('dp', 'seq')), may hold values from 0.099609375 to 1.8984375
- shift_two: bfloat16 [768], P(('dp', 'seq')), may hold values from -1.75 to 1.75
Outputs:
- output: bfloat16 [32, 2048, 768], P('dp', 'seq')
- grad_tokens: float32 [32, 2048, 768], P('dp', 'seq')
- grad_w_query: float32 [768, 768], P(('dp', 'seq'))
- grad_b_query: float32 [768], P(('dp', 'seq'))
- grad_w_key: float32 [768, 768], P(('dp', 'seq'))
- grad_w_value: float32 [768, 768], P(('dp', 'seq'))
- grad_b_value: float32 [768], P(('dp', 'seq'))
- grad_w_out: float32 [768, 768], P(('dp', 'seq'))
- output_bias_gradient: float32 [768], P(('dp', 'seq'))
- grad_gain_one: float32 [768], P(('dp', 'seq'))
- grad_shift_one: float32 [768], P(('dp', 'seq'))
- grad_w_up: float32 [768, 3072], P(('dp', 'seq'))
- grad_b_up: float32 [3072], P(('dp', 'seq'))
- grad_w_down: float32 [3072, 768], P(('dp', 'seq'))
- grad_b_down: float32 [768], P(('dp', 'seq'))
- grad_gain_two: float32 [768], P(('dp', 'seq'))
- grad_shift_two: float32 [768], P(('dp', 'seq'))
The draws below stay inside these ranges and needn't reach their ends.
Inputs may be any that keep to these rules, and one draw needn't show every extreme that they name: lengths[s] counts the valid tokens of sequence s from its start; in every draw some sequence is full and some has exactly half of its 2048 slots.
All inputs are finite; a program needn't handle non-finite values.
Results may differ from the reference program's by a relative error of at most 0.015.
Values may be sent and summed in bfloat16 or wider, within the bound.
No kernel may reach another device: no remote copies, remote signals or barrier semaphores. Data moves between devices by JAX's collectives and lax.ppermute only.
A program may use at most 768 MiB of HBM per device.

```python
import math
import jax
import jax.numpy as jnp
from jax import lax

D = 768
H = 12
HD = 64
FF = 3072
LEN = 2048
SEQS = 32


def draw_lengths(key, part):
    drawn_lengths = jax.random.randint(jax.random.fold_in(key, 1), (SEQS,), LEN // 2, LEN + 1, dtype=jnp.int32)
    longest = jax.random.randint(jax.random.fold_in(key, 2), (), 0, SEQS, dtype=jnp.int32)
    step_ahead = jax.random.randint(jax.random.fold_in(key, 3), (), 1, SEQS, dtype=jnp.int32)
    shortest = (longest + step_ahead) % SEQS
    drawn_lengths = drawn_lengths.at[longest].set(LEN)
    return drawn_lengths.at[shortest].set(LEN // 2)


def raised(values, key, source, target, shards_of, factor):
    def block_of(dim):
        return (jnp.arange(values.shape[dim]) // (values.shape[dim] // shards_of)).reshape((-1,) + (1,) * (values.ndim - 1 - dim))

    first = jax.random.permutation(key, shards_of)[block_of(target)]
    second = (block_of(target) + shards_of // 2) % shards_of
    return jnp.where((block_of(source) == first) | (block_of(source) == second), factor * values, values)


def steps_of(own_key, dims, pieces, least, largest):
    loudness, own = 1.0, jax.random.fold_in(own_key, 6)
    for dim, shards_of in pieces:
        heights = jnp.exp(jax.random.uniform(jax.random.fold_in(own, dim), (shards_of,), jnp.float32, least / len(pieces), largest / len(pieces)))
        loudness = loudness * jnp.repeat(heights, dims[dim] // shards_of).reshape([-1 if axis == dim else 1 for axis in range(len(dims))])
    return loudness


def centred(own_key, shape, scale, limit, pieces=(), held_as=jnp.bfloat16):
    values = scale * jax.random.normal(own_key, shape, jnp.float32)
    if pieces:
        values = values * steps_of(own_key, shape, pieces, -0.22, 0.18)
    return jnp.clip(values, -limit, limit).astype(held_as)


def gaussian_with(own_key, dims, scale, reach, cuts, heavy, held_as=jnp.bfloat16):
    array = scale * jax.random.normal(own_key, dims, jnp.float32)
    if cuts:
        array = array * steps_of(own_key, dims, cuts, -0.22, 0.18)
    return jnp.clip(raised(array, jax.random.fold_in(own_key, 3), *heavy), -reach, reach).astype(held_as)


def setup_inputs(seed: int = 0) -> dict:
    streams_of = jax.random.split(jax.random.key(seed), 19)
    tokens = gaussian_with(streams_of[0], (SEQS, LEN, D), 1.0, 6.0, ((0, 8), (1, 4)), (0, 2, 8, 2.0))
    lengths = draw_lengths(jax.random.fold_in(streams_of[18], 71), 0)
    cotangent = centred(streams_of[2], (SEQS, LEN, D), 1.0, 6.0, ((0, 8), (1, 4)))
    w_query = centred(streams_of[3], (D, D), D ** -0.5, 0.21875, ((0, 32),))
    b_query = centred(streams_of[4], (D,), 0.5, 3.0, ((0, 32),))
    w_key = centred(streams_of[5], (D, D), D ** -0.5, 0.21875, ((0, 32),))
    w_value = centred(streams_of[6], (D, D), D ** -0.5, 0.21875, ((0, 32),))
    b_value = centred(streams_of[7], (D,), 0.05, 0.3125, ((0, 32),))
    w_out = centred(streams_of[8], (D, D), (max(D // 256, 1)) ** -0.5, 3.5, ((0, 32),))
    b_out = centred(streams_of[9], (D,), 0.5, 3.0, ((0, 32),))
    gain_one = jnp.clip(1.0 + 0.18 * jax.random.normal(streams_of[10], (D,), jnp.float32), 0.099609375, 1.8984375).astype(jnp.bfloat16)
    shift_one = centred(streams_of[11], (D,), 0.3, 1.75, ((0, 32),))
    w_up = centred(streams_of[12], (D, FF), D ** -0.5, 0.21875, ((0, 32),))
    b_up = centred(streams_of[13], (FF,), 0.5, 3.0, ((0, 32),))
    w_down = centred(streams_of[14], (FF, D), FF ** -0.5, 0.109375, ((0, 32),))
    b_down = centred(streams_of[15], (D,), 0.5, 3.0, ((0, 32),))
    gain_two = jnp.clip(1.0 + 0.18 * jax.random.normal(streams_of[16], (D,), jnp.float32), 0.099609375, 1.8984375).astype(jnp.bfloat16)
    shift_two = centred(streams_of[17], (D,), 0.3, 1.75, ((0, 32),))
    return dict(tokens=tokens, lengths=lengths, cotangent=cotangent, w_query=w_query, b_query=b_query, w_key=w_key, w_value=w_value, b_value=b_value, w_out=w_out, b_out=b_out, gain_one=gain_one, shift_one=shift_one, w_up=w_up, b_up=b_up, w_down=w_down, b_down=b_down, gain_two=gain_two, shift_two=shift_two)


epsilon = 1e-06
largest_entry = lax.Precision.HIGHEST

@jax.custom_vjp
def low(v):
    return lax.optimization_barrier(v.astype(jnp.bfloat16)).astype(jnp.float32)

@jax.custom_vjp
def low_back(v):
    return v

def low_keep(v):
    return (low(v), None)

def low_pass(kept, grad):
    return (grad,)

def back_keep(v):
    return (v, None)

def back_low(kept, grad):
    return (low(grad),)
low.defvjp(low_keep, low_pass)
low_back.defvjp(back_keep, back_low)

def layer_norm(layer_input_rows, norm_gain, norm_shift):
    centre = layer_input_rows - lax.optimization_barrier(jnp.mean(layer_input_rows, -1, keepdims=True))
    spread = lax.optimization_barrier(jnp.mean(centre * centre, -1, keepdims=True))
    return centre * lax.rsqrt(spread + epsilon) * norm_gain + norm_shift

def project(layer_input_rows, weight_matrix):
    return jnp.einsum('hpz,zn->hpn', layer_input_rows, weight_matrix, precision=largest_entry)

def attend_sequence(queries, key_rows, value_rows, length):
    query_heads = queries.reshape(LEN, H, HD)
    key_heads = key_rows.reshape(LEN, H, HD)
    value_heads = value_rows.reshape(LEN, H, HD)
    raw_scores = jnp.einsum('qhd,khd->hqk', query_heads, key_heads, precision=largest_entry)
    scores = low_back(raw_scores) * HD ** (-0.5)
    visible = (jnp.arange(LEN, dtype=jnp.int32) < length)[None, None, :]
    scores = jnp.where(visible, scores, -1e+30)
    log_total = jax.nn.logsumexp(scores, axis=-1, keepdims=True)
    chances = low(jnp.exp(scores - log_total))
    mixed_heads = jnp.einsum('hqk,khd->qhd', chances, value_heads, precision=largest_entry)
    return mixed_heads.reshape(LEN, D)
checked_attend = jax.checkpoint(attend_sequence)

def attend_entry(entry):
    return checked_attend(entry[0], entry[1], entry[2], entry[3])

def forward(params, token_values, group_lengths):
    w_query, b_query, w_key, w_value, b_value, w_out, b_out, gain_one, shift_one, w_up, b_up, w_down, b_down, gain_two, shift_two = params
    queries = low(low_back(project(token_values, w_query) + b_query))
    key_rows = low(low_back(project(token_values, w_key)))
    value_rows = low(low_back(project(token_values, w_value) + b_value))
    mixed_rows = lax.map(attend_entry, (queries, key_rows, value_rows, group_lengths))
    mixed_low = low(low_back(mixed_rows))
    branch = low_back(project(mixed_low, w_out) + b_out)
    normed = layer_norm(token_values + branch, gain_one, shift_one)
    hidden = low_back(project(low(normed), w_up) + b_up)
    active = low(jax.nn.gelu(hidden, approximate=False))
    feed_out = low_back(project(active, w_down) + b_down)
    return layer_norm(normed + feed_out, gain_two, shift_two)

def reference(tokens, lengths, cotangent, w_query, b_query, w_key, w_value, b_value, w_out, b_out, gain_one, shift_one, w_up, b_up, w_down, b_down, gain_two, shift_two):
    params = tuple((weight.astype(jnp.float32) for weight in (w_query, b_query, w_key, w_value, b_value, w_out, b_out, gain_one, shift_one, w_up, b_up, w_down, b_down, gain_two, shift_two)))
    group_size = math.gcd(SEQS, max(1, 4096 // LEN))
    group_count = SEQS // group_size
    grouped_tokens = tokens.astype(jnp.float32).reshape(group_count, group_size, LEN, D)
    grouped_cots = cotangent.astype(jnp.float32).reshape(group_count, group_size, LEN, D)
    grouped_lengths = lengths.reshape(group_count, group_size)

    def run_group(running, entry):
        token_values, cot_values, group_lengths = entry
        live_rows = (jnp.arange(LEN, dtype=jnp.int32)[None, :] < group_lengths[:, None]).astype(jnp.float32)[:, :, None]

        def apply_layer(param_values, layer_input_rows):
            return forward(param_values, layer_input_rows, group_lengths)
        result, pullback = jax.vjp(apply_layer, params, token_values)
        param_grads, input_grads = pullback(cot_values * live_rows)
        running = tuple((total + grad for total, grad in zip(running, param_grads)))
        return (running, (result.astype(jnp.bfloat16), input_grads))
    zeros = tuple((jnp.zeros_like(weight) for weight in params))
    running, (results, input_grads) = lax.scan(run_group, zeros, (grouped_tokens, grouped_cots, grouped_lengths))
    output = results.reshape(SEQS, LEN, D)
    grad_tokens = input_grads.reshape(SEQS, LEN, D)
    return (output, grad_tokens, running[0], running[1], running[2], running[3], running[4], running[5], running[6], running[7], running[8], running[9], running[10], running[11], running[12], running[13], running[14])
```

```python
import functools

import jax
import jax.numpy as jnp
from jax import lax
from jax.experimental import pallas as pl
from jax.experimental.pallas import tpu as pltpu
from jax.sharding import PartitionSpec as P

H = 12
HD = 64
MB = 4


epsilon = 1e-06


def layer_norm(layer_input_rows, norm_gain, norm_shift):
    centre = layer_input_rows - jnp.mean(layer_input_rows, -1, keepdims=True)
    spread = jnp.mean(centre * centre, -1, keepdims=True)
    return centre * lax.rsqrt(spread + epsilon) * norm_gain + norm_shift


def gelu_exact(values):
    return jax.nn.gelu(values, approximate=False)


def matmul(former, latter):
    return jnp.dot(former, latter, preferred_element_type=jnp.float32)


def former_product(former, latter):
    return lax.dot_general(
        former, latter, (((0,), (0,)), ((), ())), preferred_element_type=jnp.float32
    )


def latter_product(former, latter):
    return lax.dot_general(
        former, latter, (((1,), (1,)), ((), ())), preferred_element_type=jnp.float32
    )


def widen(vector):
    return vector.astype(jnp.float32)


def general_body(
    tokens,
    lengths,
    cotangent,
    w_query,
    b_query,
    w_key,
    w_value,
    b_value,
    w_out,
    b_out,
    gain_one,
    shift_one,
    w_up,
    b_up,
    w_down,
    b_down,
    gain_two,
    shift_two,
):
    shards = (
        w_query,
        b_query,
        w_key,
        w_value,
        b_value,
        w_out,
        b_out,
        gain_one,
        shift_one,
        w_up,
        b_up,
        w_down,
        b_down,
        gain_two,
        shift_two,
    )
    per_batch = tokens.shape[0] // MB
    block_rows = tokens.shape[1]
    model_width = tokens.shape[2]
    head_count = H
    head_size = HD
    flat_rows = per_batch * block_rows
    full_length = block_rows * lax.axis_size("seq")
    offset = lax.axis_index("seq") * block_rows
    positions = jnp.arange(full_length, dtype=jnp.int32)
    own_positions = offset + jnp.arange(block_rows, dtype=jnp.int32)
    score_scale = head_size ** (-0.5)
    owners = lax.axis_size(("dp", "seq"))
    totals = [
        jnp.zeros((shard_piece.shape[0] * owners,) + shard_piece.shape[1:], jnp.float32)
        for shard_piece in shards
    ]
    outputs = []
    input_grads = []
    for micro_batch in range(MB):
        leading_row = micro_batch * per_batch
        own_tokens = tokens[leading_row : leading_row + per_batch]
        own_lengths = lengths[leading_row : leading_row + per_batch]
        own_cots = cotangent[leading_row : leading_row + per_batch]
        fore_weights = (
            lax.all_gather(shards[0], ("dp", "seq"), axis=0, tiled=True),
            lax.all_gather(shards[1], ("dp", "seq"), axis=0, tiled=True),
            lax.all_gather(shards[2], ("dp", "seq"), axis=0, tiled=True),
            lax.all_gather(shards[3], ("dp", "seq"), axis=0, tiled=True),
            lax.all_gather(shards[4], ("dp", "seq"), axis=0, tiled=True),
            lax.all_gather(shards[5], ("dp", "seq"), axis=0, tiled=True),
            lax.all_gather(shards[6], ("dp", "seq"), axis=0, tiled=True),
            lax.all_gather(shards[7], ("dp", "seq"), axis=0, tiled=True),
            lax.all_gather(shards[8], ("dp", "seq"), axis=0, tiled=True),
            lax.all_gather(shards[9], ("dp", "seq"), axis=0, tiled=True),
            lax.all_gather(shards[10], ("dp", "seq"), axis=0, tiled=True),
            lax.all_gather(shards[11], ("dp", "seq"), axis=0, tiled=True),
            lax.all_gather(shards[12], ("dp", "seq"), axis=0, tiled=True),
            lax.all_gather(shards[13], ("dp", "seq"), axis=0, tiled=True),
            lax.all_gather(shards[14], ("dp", "seq"), axis=0, tiled=True),
        )
        flat_tokens = own_tokens.reshape(flat_rows, model_width)
        query_low = (matmul(flat_tokens, fore_weights[0]) + widen(fore_weights[1])).astype(
            jnp.bfloat16
        )
        key_low = matmul(flat_tokens, fore_weights[2]).astype(jnp.bfloat16)
        value_low = (matmul(flat_tokens, fore_weights[3]) + widen(fore_weights[4])).astype(
            jnp.bfloat16
        )
        key_block = key_low.reshape(per_batch, block_rows, model_width)
        value_block = value_low.reshape(per_batch, block_rows, model_width)
        gathered_keys, gathered_values = (
            lax.all_gather(key_block, "seq", axis=1, tiled=True),
            lax.all_gather(value_block, "seq", axis=1, tiled=True),
        )
        query_heads = query_low.reshape(per_batch, block_rows, head_count, head_size)
        visible = (positions[None, :] < own_lengths[:, None])[:, None, None, :]

        def score_block(key_all):
            key_heads = key_all.reshape(per_batch, full_length, head_count, head_size)
            raw_scores = jnp.einsum(
                "pqhd,pkhd->phqk", query_heads, key_heads, preferred_element_type=jnp.float32
            )
            return jnp.where(visible, raw_scores * score_scale, -1e30)

        scores = score_block(gathered_keys)
        logarithm_totals = jax.nn.logsumexp(scores, axis=-1, keepdims=True)
        chances_low = jnp.exp(scores - logarithm_totals).astype(jnp.bfloat16)
        value_heads = gathered_values.reshape(per_batch, full_length, head_count, head_size)
        mixed_heads = jnp.einsum(
            "phqk,pkhd->pqhd", chances_low, value_heads, preferred_element_type=jnp.float32
        )
        mixed_low = mixed_heads.reshape(flat_rows, model_width).astype(jnp.bfloat16)
        branch = matmul(mixed_low, fore_weights[5]) + widen(fore_weights[6])
        resid_one = flat_tokens.astype(jnp.float32) + branch
        normed = layer_norm(resid_one, widen(fore_weights[7]), widen(fore_weights[8]))
        normed_low = normed.astype(jnp.bfloat16)
        hidden = matmul(normed_low, fore_weights[9]) + widen(fore_weights[10])
        active_low = gelu_exact(hidden).astype(jnp.bfloat16)
        feed_out = matmul(active_low, fore_weights[11]) + widen(fore_weights[12])
        resid_two = normed + feed_out
        result = layer_norm(resid_two, widen(fore_weights[13]), widen(fore_weights[14]))
        outputs.append(result.astype(jnp.bfloat16).reshape(per_batch, block_rows, model_width))
        back_weights = (
            lax.all_gather(shards[0], ("dp", "seq"), axis=0, tiled=True),
            lax.all_gather(shards[1], ("dp", "seq"), axis=0, tiled=True),
            lax.all_gather(shards[2], ("dp", "seq"), axis=0, tiled=True),
            lax.all_gather(shards[3], ("dp", "seq"), axis=0, tiled=True),
            lax.all_gather(shards[4], ("dp", "seq"), axis=0, tiled=True),
            lax.all_gather(shards[5], ("dp", "seq"), axis=0, tiled=True),
            lax.all_gather(shards[6], ("dp", "seq"), axis=0, tiled=True),
            lax.all_gather(shards[7], ("dp", "seq"), axis=0, tiled=True),
            lax.all_gather(shards[8], ("dp", "seq"), axis=0, tiled=True),
            lax.all_gather(shards[9], ("dp", "seq"), axis=0, tiled=True),
            lax.all_gather(shards[10], ("dp", "seq"), axis=0, tiled=True),
            lax.all_gather(shards[11], ("dp", "seq"), axis=0, tiled=True),
            lax.all_gather(shards[12], ("dp", "seq"), axis=0, tiled=True),
            lax.all_gather(shards[13], ("dp", "seq"), axis=0, tiled=True),
            lax.all_gather(shards[14], ("dp", "seq"), axis=0, tiled=True),
        )
        live_rows = (
            (own_positions[None, :] < own_lengths[:, None])
            .astype(jnp.float32)
            .reshape(flat_rows, 1)
        )
        incoming = own_cots.reshape(flat_rows, model_width).astype(jnp.float32) * live_rows
        _, second_pull = jax.vjp(
            layer_norm, resid_two, widen(back_weights[13]), widen(back_weights[14])
        )
        grad_two, grad_gain_two, grad_shift_two = second_pull(incoming)
        feed_low = grad_two.astype(jnp.bfloat16)
        totals[11] = totals[11] + former_product(active_low, feed_low)
        totals[12] = totals[12] + jnp.sum(feed_low.astype(jnp.float32), 0)
        grad_active = latter_product(feed_low, back_weights[11])
        _, gelu_pull = jax.vjp(gelu_exact, hidden)
        up_low = gelu_pull(grad_active)[0].astype(jnp.bfloat16)
        totals[9] = totals[9] + former_product(normed_low, up_low)
        totals[10] = totals[10] + jnp.sum(up_low.astype(jnp.float32), 0)
        grad_normed = latter_product(up_low, back_weights[9]) + grad_two
        _, first_pull = jax.vjp(
            layer_norm, resid_one, widen(back_weights[7]), widen(back_weights[8])
        )
        grad_one, grad_gain_one, grad_shift_one = first_pull(grad_normed)
        branch_low = grad_one.astype(jnp.bfloat16)
        totals[5] = totals[5] + former_product(mixed_low, branch_low)
        totals[6] = totals[6] + jnp.sum(branch_low.astype(jnp.float32), 0)
        dmix_low = latter_product(branch_low, back_weights[5]).astype(jnp.bfloat16)
        dmix_heads = dmix_low.reshape(per_batch, block_rows, head_count, head_size)
        back_keys, backward_value_rows = (gathered_keys, gathered_values)
        chances = jnp.exp(score_block(back_keys) - logarithm_totals)
        back_value_heads = backward_value_rows.reshape(
            per_batch, full_length, head_count, head_size
        )
        back_key_heads = back_keys.reshape(per_batch, full_length, head_count, head_size)
        grad_chances = jnp.einsum(
            "pqhd,pkhd->phqk", dmix_heads, back_value_heads, preferred_element_type=jnp.float32
        )
        row_inner = jnp.sum(grad_chances * chances, -1, keepdims=True)
        dscore_low = (score_scale * (chances * (grad_chances - row_inner))).astype(jnp.bfloat16)
        dquery_low = jnp.einsum(
            "phqk,pkhd->pqhd", dscore_low, back_key_heads, preferred_element_type=jnp.float32
        )
        dquery_low = dquery_low.reshape(flat_rows, model_width).astype(jnp.bfloat16)
        chance_low = chances.astype(jnp.bfloat16)
        value_terms = jnp.einsum(
            "phqk,pqhd->pkhd", chance_low, dmix_heads, preferred_element_type=jnp.float32
        )
        key_terms = jnp.einsum(
            "phqk,pqhd->pkhd", dscore_low, query_heads, preferred_element_type=jnp.float32
        )
        key_sums, value_sums = (
            lax.psum_scatter(
                key_terms.reshape(per_batch, full_length, model_width).astype(jnp.bfloat16),
                "seq",
                scatter_dimension=1,
                tiled=True,
            ).astype(jnp.float32),
            lax.psum_scatter(
                value_terms.reshape(per_batch, full_length, model_width).astype(jnp.bfloat16),
                "seq",
                scatter_dimension=1,
                tiled=True,
            ).astype(jnp.float32),
        )
        dkey_low = key_sums.reshape(flat_rows, model_width).astype(jnp.bfloat16)
        dvalue_low = value_sums.reshape(flat_rows, model_width).astype(jnp.bfloat16)
        totals[0] = totals[0] + former_product(flat_tokens, dquery_low)
        totals[1] = totals[1] + jnp.sum(dquery_low.astype(jnp.float32), 0)
        totals[2] = totals[2] + former_product(flat_tokens, dkey_low)
        totals[3] = totals[3] + former_product(flat_tokens, dvalue_low)
        totals[4] = totals[4] + jnp.sum(dvalue_low.astype(jnp.float32), 0)
        totals[7] = totals[7] + grad_gain_one
        totals[8] = totals[8] + grad_shift_one
        totals[13] = totals[13] + grad_gain_two
        totals[14] = totals[14] + grad_shift_two
        grad_input = (
            latter_product(dquery_low, back_weights[0])
            + latter_product(dkey_low, back_weights[2])
            + latter_product(dvalue_low, back_weights[3])
            + grad_one
        )
        input_grads.append(grad_input.reshape(per_batch, block_rows, model_width))
    owned = lax.psum_scatter(tuple(totals), ("dp", "seq"), scatter_dimension=0, tiled=True)
    output = jnp.concatenate(outputs, 0)
    grad_tokens = jnp.concatenate(input_grads, 0)
    return (
        output,
        grad_tokens,
        owned[0],
        owned[1],
        owned[2],
        owned[3],
        owned[4],
        owned[5],
        owned[6],
        owned[7],
        owned[8],
        owned[9],
        owned[10],
        owned[11],
        owned[12],
        owned[13],
        owned[14],
    )


LOG2E = 1.4426950408889634
PAD = 16
VMEM = 60 << 20
CHUNK = 512


def contract(former, latter, dim_former, dim_latter):
    return lax.dot_general(
        former,
        latter,
        (((dim_former,), (dim_latter,)), ((), ())),
        preferred_element_type=jnp.float32,
    )


def mix_kernel(scale, qt, kt, vt, bias, mixed, total, probs, keys, vals):
    size, slots = kt.shape[1], kt.shape[2]
    key = kt[0]
    keys[...] = jnp.concatenate([key, key, bias[...]], 0).T
    vals[...] = jnp.concatenate([vt[0], jnp.ones((PAD, slots), jnp.bfloat16)], 0)
    query = qt[0].astype(jnp.float32) * scale
    high = query.astype(jnp.bfloat16)
    low = (query - high.astype(jnp.float32)).astype(jnp.bfloat16)
    row = lax.broadcasted_iota(jnp.int32, (PAD, slots), 0)
    first = jnp.where(row == 0, 1.0, 0.0).astype(jnp.bfloat16)
    columns = jnp.concatenate([high, low, first], 0)

    def finish(sums):
        weight = sums[size : size + 1]
        mixed[0] = (sums[:size] / weight).astype(mixed.dtype)
        total[0] = weight
        return weight

    sums, top = None, None
    for at in range(0, slots, CHUNK):
        scores = contract(keys[at : at + CHUNK], columns, 1, 0)
        if top is None:
            top = jnp.max(scores[:256], 0, keepdims=True)
        part = jnp.exp2(scores - top).astype(jnp.bfloat16)
        probs[0, at : at + CHUNK] = part
        term = contract(vals[:, at : at + CHUNK], part, 1, 0)
        sums = term if sums is None else sums + term
    weight = finish(sums)

    @pl.when(jnp.logical_not(jnp.max(weight) < 2.0**60))
    def _():
        top = jnp.full((1, slots), -jnp.inf, jnp.float32)
        for at in range(0, slots, CHUNK):
            scores = contract(keys[at : at + CHUNK], columns, 1, 0)
            top = jnp.maximum(top, jnp.max(scores, 0, keepdims=True))
        sums = None
        for at in range(0, slots, CHUNK):
            scores = contract(keys[at : at + CHUNK], columns, 1, 0)
            part = jnp.exp2(scores - top).astype(jnp.bfloat16)
            probs[0, at : at + CHUNK] = part
            term = contract(vals[:, at : at + CHUNK], part, 1, 0)
            sums = term if sums is None else sums + term
        finish(sums)


def mix(qt, kt, vt, bias, scale):
    heads, size, slots = qt.shape
    whole = pl.BlockSpec((1, size, slots), lambda i: (i, 0, 0))
    return pl.pallas_call(
        functools.partial(mix_kernel, scale),
        grid=(heads,),
        in_specs=[whole, whole, whole, pl.BlockSpec((PAD, slots), lambda i: (0, 0))],
        out_specs=[
            whole,
            pl.BlockSpec((1, 1, slots), lambda i: (i, 0, 0)),
            pl.BlockSpec((1, slots, slots), lambda i: (i, 0, 0)),
        ],
        out_shape=[
            jax.ShapeDtypeStruct((heads, size, slots), jnp.bfloat16),
            jax.ShapeDtypeStruct((heads, 1, slots), jnp.float32),
            jax.ShapeDtypeStruct((heads, slots, slots), jnp.bfloat16),
        ],
        scratch_shapes=[
            pltpu.VMEM((slots, 2 * size + PAD), jnp.bfloat16),
            pltpu.VMEM((size + PAD, slots), jnp.bfloat16),
        ],
        compiler_params=pltpu.CompilerParams(vmem_limit_bytes=VMEM),
        name="mix",
    )(qt, kt, vt, bias)


def unmix_kernel(scale, probs, qt, kt, vt, gt, mt, total, dq, dk, dv, grads, inner, sums):
    step, last = pl.program_id(1), pl.num_programs(1) - 1

    @pl.when(step == 0)
    def _():
        scaled = (gt[0].astype(jnp.float32) / total[0]).astype(jnp.bfloat16)
        grads[...] = scaled
        inner[...] = jnp.sum(
            scaled.astype(jnp.float32) * mt[0].astype(jnp.float32), 0, keepdims=True
        )

    grad = grads[...]
    prob = probs[0]
    dprob = contract(vt[0], grad, 0, 0)
    dscore = (prob.astype(jnp.float32) * (dprob - inner[...])).astype(jnp.bfloat16)
    part = contract(kt[0], dscore, 1, 0)
    dv[0] = contract(prob, grad, 1, 1).T.astype(jnp.bfloat16)
    dk[0] = (contract(dscore, qt[0], 1, 1) * scale).T.astype(jnp.bfloat16)

    @pl.when(step == 0)
    def _():
        sums[...] = part

    @pl.when(step > 0)
    def _():
        sums[...] += part

    @pl.when(step == last)
    def _():
        dq[0] = (sums[...] * scale).astype(jnp.bfloat16)


def unmix(probs, qt, kt, vt, gt, mt, total, scale):
    heads, size, slots = qt.shape
    keys = slots // 2
    whole = pl.BlockSpec((1, size, slots), lambda i, j: (i, 0, 0))
    part = pl.BlockSpec((1, size, keys), lambda i, j: (i, 0, j))
    return pl.pallas_call(
        functools.partial(unmix_kernel, scale),
        grid=(heads, slots // keys),
        in_specs=[
            pl.BlockSpec((1, keys, slots), lambda i, j: (i, j, 0)),
            whole,
            part,
            part,
            whole,
            whole,
            pl.BlockSpec((1, 1, slots), lambda i, j: (i, 0, 0)),
        ],
        out_specs=[whole, part, part],
        out_shape=[jax.ShapeDtypeStruct((heads, size, slots), jnp.bfloat16)] * 3,
        scratch_shapes=[
            pltpu.VMEM((size, slots), jnp.bfloat16),
            pltpu.VMEM((1, slots), jnp.float32),
            pltpu.VMEM((size, slots), jnp.float32),
        ],
        compiler_params=pltpu.CompilerParams(vmem_limit_bytes=VMEM),
        name="unmix",
    )(probs, qt, kt, vt, gt, mt, total)


def swap(piece, step):
    size = lax.axis_size("seq")
    return lax.ppermute(piece, "seq", [(i, i ^ step) for i in range(size)])


def take(array, index):
    return lax.dynamic_index_in_dim(array, index, 0, keepdims=False)


def to_own(array):
    me = lax.axis_index("seq")
    pieces = [take(array, me)]
    pieces += [swap(take(array, me ^ step), step) for step in range(1, lax.axis_size("seq"))]
    return jnp.concatenate(pieces, 0)


def to_split(rows, own, blank):
    me = lax.axis_index("seq")
    size = lax.axis_size("seq")
    block = rows.shape[0] // size
    result = lax.dynamic_update_index_in_dim(blank, own.astype(blank.dtype), me, 0)
    for step in range(1, size):
        came = swap(rows[step * block : (step + 1) * block], step)
        result = lax.dynamic_update_index_in_dim(result, came.astype(blank.dtype), me ^ step, 0)
    return result


def whole_body(
    tokens,
    lengths,
    cotangent,
    w_query,
    b_query,
    w_key,
    w_value,
    b_value,
    w_out,
    b_out,
    gain_one,
    shift_one,
    w_up,
    b_up,
    w_down,
    b_down,
    gain_two,
    shift_two,
):
    count, block, width = tokens.shape
    slots = count * block
    wide = w_up.shape[1]
    rows = w_query.shape[0]
    axes = ("dp", "seq")
    me = lax.axis_index("seq")
    heads, size = H, HD
    scale = size ** (-0.5)
    times = wide // width

    vectors = [b_query, b_value, b_out, gain_one, shift_one, b_down, gain_two, shift_two]
    columns = [v.reshape(rows, 1) for v in vectors] + [b_up.reshape(rows, times)]
    columns = jnp.concatenate(columns, 1)
    columns = jnp.pad(columns, ((0, 0), (0, 128 - columns.shape[1])))
    first = jnp.concatenate([w_query, w_key, w_value, w_out, columns], 1)
    first = lax.all_gather(first, axes, axis=0, tiled=True)
    second = jnp.concatenate([w_up, w_down.reshape(rows, wide)], 1)
    second = lax.all_gather(second, axes, axis=0, tiled=True)

    x = to_own(tokens)
    cot = to_own(cotangent)
    length = take(lengths, me)
    order = me ^ jnp.arange(count, dtype=jnp.int32)
    place = (order[:, None] * block + jnp.arange(block, dtype=jnp.int32)[None, :]).reshape(slots)
    live = place < length
    bias = jnp.where(live, 0.0, -1e30).astype(jnp.bfloat16)
    bias = jnp.pad(bias[None, :], ((0, PAD - 1), (0, 0)))

    wq, wk, wv, wo = (first[:, i * width : (i + 1) * width] for i in range(4))
    vec = first[:, 4 * width :].astype(jnp.float32).T
    bq, bv, bo, g1, s1, bd, g2, s2 = (vec[i] for i in range(8))
    bu = vec[8 : 8 + times].T.reshape(wide)
    wu = second[:, :wide]
    wd = second[:, wide:].reshape(wide, width)

    def columns_of(weight):
        return contract(weight, x, 0, 1)

    def by_head(array):
        return array.astype(jnp.bfloat16).reshape(heads, size, slots)

    qt = by_head(columns_of(wq) + bq[:, None])
    kt = by_head(columns_of(wk))
    vt = by_head(columns_of(wv) + bv[:, None])
    mt, total, probs = mix(qt, kt, vt, bias, scale * LOG2E)
    mixed = mt.reshape(width, slots)
    resid_one = x.astype(jnp.float32) + contract(mixed, wo, 0, 0) + bo
    normed = layer_norm(resid_one, g1, s1)
    normed_low = normed.astype(jnp.bfloat16)
    hidden = matmul(normed_low, wu) + bu
    active_low = gelu_exact(hidden).astype(jnp.bfloat16)
    resid_two = normed + matmul(active_low, wd) + bd
    result = layer_norm(resid_two, g2, s2).astype(jnp.bfloat16)
    output = to_split(result, result[:block], jnp.zeros((count, block, width), jnp.bfloat16))

    incoming = cot.astype(jnp.float32) * live[:, None].astype(jnp.float32)
    _, second_pull = jax.vjp(layer_norm, resid_two, g2, s2)
    grad_two, d_g2, d_s2 = second_pull(incoming)
    feed_low = grad_two.astype(jnp.bfloat16)
    d_wd = former_product(active_low, feed_low)
    d_bd = jnp.sum(feed_low.astype(jnp.float32), 0)
    _, gelu_pull = jax.vjp(gelu_exact, hidden)
    up_low = gelu_pull(latter_product(feed_low, wd))[0].astype(jnp.bfloat16)
    d_wu = former_product(normed_low, up_low)
    d_bu = jnp.sum(up_low.astype(jnp.float32), 0)
    late = jnp.concatenate([d_wu, d_wd.reshape(width, wide)], 1).astype(jnp.bfloat16)
    late = lax.psum_scatter(late, axes, scatter_dimension=0, tiled=True).astype(jnp.float32)
    grad_normed = latter_product(up_low, wu) + grad_two
    _, first_pull = jax.vjp(layer_norm, resid_one, g1, s1)
    grad_one, d_g1, d_s1 = first_pull(grad_normed)
    branch_low = grad_one.astype(jnp.bfloat16)
    d_wo = matmul(mixed, branch_low)
    d_bo = jnp.sum(branch_low.astype(jnp.float32), 0)
    gt = by_head(latter_product(wo, branch_low))
    dq, dk, dv = unmix(probs, qt, kt, vt, gt, mt, total, scale)
    dq, dk, dv = (g.reshape(width, slots) for g in (dq, dk, dv))
    d_wq, d_wk, d_wv = (contract(x, g, 0, 1) for g in (dq, dk, dv))
    d_bq, d_bv = (jnp.sum(g.astype(jnp.float32), 1) for g in (dq, dv))
    grad_x = contract(dq, wq, 0, 1) + contract(dk, wk, 0, 1) + contract(dv, wv, 0, 1) + grad_one
    grad_tokens = to_split(
        grad_x.astype(jnp.bfloat16), grad_x[:block], jnp.zeros((count, block, width), jnp.float32)
    )

    columns = jnp.stack([d_bq, d_bv, d_bo, d_g1, d_s1, d_bd, d_g2, d_s2], 1)
    columns = jnp.concatenate([columns, d_bu.reshape(width, times)], 1)
    columns = jnp.pad(columns, ((0, 0), (0, 128 - columns.shape[1])))
    early = jnp.concatenate([d_wq, d_wk, d_wv, d_wo, columns], 1).astype(jnp.bfloat16)
    early = lax.psum_scatter(early, axes, scatter_dimension=0, tiled=True).astype(jnp.float32)
    o_wq, o_wk, o_wv, o_wo = (early[:, i * width : (i + 1) * width] for i in range(4))
    vec = early[:, 4 * width :]
    o_bq, o_bv, o_bo, o_g1, o_s1, o_bd, o_g2, o_s2 = (vec[:, i] for i in range(8))
    o_bu = vec[:, 8 : 8 + times].reshape(rows * times)
    o_wu = late[:, :wide]
    o_wd = late[:, wide:].reshape(rows * times, width)
    return (
        output,
        grad_tokens,
        o_wq,
        o_bq,
        o_wk,
        o_wv,
        o_bv,
        o_wo,
        o_bo,
        o_g1,
        o_s1,
        o_wu,
        o_bu,
        o_wd,
        o_bd,
        o_g2,
        o_s2,
    )


def body(*arrays):
    count = arrays[0].shape[0]
    fits = count == lax.axis_size("seq") and count & (count - 1) == 0
    return whole_body(*arrays) if fits else general_body(*arrays)


def solution(mesh):
    in_specs = (
        P("dp", "seq", None),
        P("dp"),
        P("dp", "seq", None),
        P(("dp", "seq"), None),
        P(("dp", "seq")),
        P(("dp", "seq"), None),
        P(("dp", "seq"), None),
        P(("dp", "seq")),
        P(("dp", "seq"), None),
        P(("dp", "seq")),
        P(("dp", "seq")),
        P(("dp", "seq")),
        P(("dp", "seq"), None),
        P(("dp", "seq")),
        P(("dp", "seq"), None),
        P(("dp", "seq")),
        P(("dp", "seq")),
        P(("dp", "seq")),
    )
    out_specs = (
        P("dp", "seq", None),
        P("dp", "seq", None),
        P(("dp", "seq"), None),
        P(("dp", "seq")),
        P(("dp", "seq"), None),
        P(("dp", "seq"), None),
        P(("dp", "seq")),
        P(("dp", "seq"), None),
        P(("dp", "seq")),
        P(("dp", "seq")),
        P(("dp", "seq")),
        P(("dp", "seq"), None),
        P(("dp", "seq")),
        P(("dp", "seq"), None),
        P(("dp", "seq")),
        P(("dp", "seq")),
        P(("dp", "seq")),
    )
    return jax.shard_map(body, mesh=mesh, in_specs=in_specs, out_specs=out_specs, check_vma=False)
```

```python
import functools

import jax
import jax.numpy as jnp
from jax import lax
from jax.experimental import pallas as pl
from jax.experimental.pallas import tpu as pltpu
from jax.sharding import PartitionSpec as P

H = 12
HD = 64
MB = 4


epsilon = 1e-06


def layer_norm(layer_input_rows, norm_gain, norm_shift):
    centre = layer_input_rows - jnp.mean(layer_input_rows, -1, keepdims=True)
    spread = jnp.mean(centre * centre, -1, keepdims=True)
    return centre * lax.rsqrt(spread + epsilon) * norm_gain + norm_shift


def gelu_exact(values):
    return jax.nn.gelu(values, approximate=False)


def matmul(former, latter):
    return jnp.dot(former, latter, preferred_element_type=jnp.float32)


def former_product(former, latter):
    return lax.dot_general(
        former, latter, (((0,), (0,)), ((), ())), preferred_element_type=jnp.float32
    )


def latter_product(former, latter):
    return lax.dot_general(
        former, latter, (((1,), (1,)), ((), ())), preferred_element_type=jnp.float32
    )


def widen(vector):
    return vector.astype(jnp.float32)


def general_body(
    tokens,
    lengths,
    cotangent,
    w_query,
    b_query,
    w_key,
    w_value,
    b_value,
    w_out,
    b_out,
    gain_one,
    shift_one,
    w_up,
    b_up,
    w_down,
    b_down,
    gain_two,
    shift_two,
):
    shards = (
        w_query,
        b_query,
        w_key,
        w_value,
        b_value,
        w_out,
        b_out,
        gain_one,
        shift_one,
        w_up,
        b_up,
        w_down,
        b_down,
        gain_two,
        shift_two,
    )
    per_batch = tokens.shape[0] // MB
    block_rows = tokens.shape[1]
    model_width = tokens.shape[2]
    head_count = H
    head_size = HD
    flat_rows = per_batch * block_rows
    full_length = block_rows * lax.axis_size("seq")
    offset = lax.axis_index("seq") * block_rows
    positions = jnp.arange(full_length, dtype=jnp.int32)
    own_positions = offset + jnp.arange(block_rows, dtype=jnp.int32)
    score_scale = head_size ** (-0.5)
    owners = lax.axis_size(("dp", "seq"))
    totals = [
        jnp.zeros((shard_piece.shape[0] * owners,) + shard_piece.shape[1:], jnp.float32)
        for shard_piece in shards
    ]
    outputs = []
    input_grads = []
    for micro_batch in range(MB):
        leading_row = micro_batch * per_batch
        own_tokens = tokens[leading_row : leading_row + per_batch]
        own_lengths = lengths[leading_row : leading_row + per_batch]
        own_cots = cotangent[leading_row : leading_row + per_batch]
        fore_weights = (
            lax.all_gather(shards[0], ("dp", "seq"), axis=0, tiled=True),
            lax.all_gather(shards[1], ("dp", "seq"), axis=0, tiled=True),
            lax.all_gather(shards[2], ("dp", "seq"), axis=0, tiled=True),
            lax.all_gather(shards[3], ("dp", "seq"), axis=0, tiled=True),
            lax.all_gather(shards[4], ("dp", "seq"), axis=0, tiled=True),
            lax.all_gather(shards[5], ("dp", "seq"), axis=0, tiled=True),
            lax.all_gather(shards[6], ("dp", "seq"), axis=0, tiled=True),
            lax.all_gather(shards[7], ("dp", "seq"), axis=0, tiled=True),
            lax.all_gather(shards[8], ("dp", "seq"), axis=0, tiled=True),
            lax.all_gather(shards[9], ("dp", "seq"), axis=0, tiled=True),
            lax.all_gather(shards[10], ("dp", "seq"), axis=0, tiled=True),
            lax.all_gather(shards[11], ("dp", "seq"), axis=0, tiled=True),
            lax.all_gather(shards[12], ("dp", "seq"), axis=0, tiled=True),
            lax.all_gather(shards[13], ("dp", "seq"), axis=0, tiled=True),
            lax.all_gather(shards[14], ("dp", "seq"), axis=0, tiled=True),
        )
        flat_tokens = own_tokens.reshape(flat_rows, model_width)
        query_low = (matmul(flat_tokens, fore_weights[0]) + widen(fore_weights[1])).astype(
            jnp.bfloat16
        )
        key_low = matmul(flat_tokens, fore_weights[2]).astype(jnp.bfloat16)
        value_low = (matmul(flat_tokens, fore_weights[3]) + widen(fore_weights[4])).astype(
            jnp.bfloat16
        )
        key_block = key_low.reshape(per_batch, block_rows, model_width)
        value_block = value_low.reshape(per_batch, block_rows, model_width)
        gathered_keys, gathered_values = (
            lax.all_gather(key_block, "seq", axis=1, tiled=True),
            lax.all_gather(value_block, "seq", axis=1, tiled=True),
        )
        query_heads = query_low.reshape(per_batch, block_rows, head_count, head_size)
        visible = (positions[None, :] < own_lengths[:, None])[:, None, None, :]

        def score_block(key_all):
            key_heads = key_all.reshape(per_batch, full_length, head_count, head_size)
            raw_scores = jnp.einsum(
                "pqhd,pkhd->phqk", query_heads, key_heads, preferred_element_type=jnp.float32
            )
            return jnp.where(visible, raw_scores * score_scale, -1e30)

        scores = score_block(gathered_keys)
        logarithm_totals = jax.nn.logsumexp(scores, axis=-1, keepdims=True)
        chances_low = jnp.exp(scores - logarithm_totals).astype(jnp.bfloat16)
        value_heads = gathered_values.reshape(per_batch, full_length, head_count, head_size)
        mixed_heads = jnp.einsum(
            "phqk,pkhd->pqhd", chances_low, value_heads, preferred_element_type=jnp.float32
        )
        mixed_low = mixed_heads.reshape(flat_rows, model_width).astype(jnp.bfloat16)
        branch = matmul(mixed_low, fore_weights[5]) + widen(fore_weights[6])
        resid_one = flat_tokens.astype(jnp.float32) + branch
        normed = layer_norm(resid_one, widen(fore_weights[7]), widen(fore_weights[8]))
        normed_low = normed.astype(jnp.bfloat16)
        hidden = matmul(normed_low, fore_weights[9]) + widen(fore_weights[10])
        active_low = gelu_exact(hidden).astype(jnp.bfloat16)
        feed_out = matmul(active_low, fore_weights[11]) + widen(fore_weights[12])
        resid_two = normed + feed_out
        result = layer_norm(resid_two, widen(fore_weights[13]), widen(fore_weights[14]))
        outputs.append(result.astype(jnp.bfloat16).reshape(per_batch, block_rows, model_width))
        back_weights = (
            lax.all_gather(shards[0], ("dp", "seq"), axis=0, tiled=True),
            lax.all_gather(shards[1], ("dp", "seq"), axis=0, tiled=True),
            lax.all_gather(shards[2], ("dp", "seq"), axis=0, tiled=True),
            lax.all_gather(shards[3], ("dp", "seq"), axis=0, tiled=True),
            lax.all_gather(shards[4], ("dp", "seq"), axis=0, tiled=True),
            lax.all_gather(shards[5], ("dp", "seq"), axis=0, tiled=True),
            lax.all_gather(shards[6], ("dp", "seq"), axis=0, tiled=True),
            lax.all_gather(shards[7], ("dp", "seq"), axis=0, tiled=True),
            lax.all_gather(shards[8], ("dp", "seq"), axis=0, tiled=True),
            lax.all_gather(shards[9], ("dp", "seq"), axis=0, tiled=True),
            lax.all_gather(shards[10], ("dp", "seq"), axis=0, tiled=True),
            lax.all_gather(shards[11], ("dp", "seq"), axis=0, tiled=True),
            lax.all_gather(shards[12], ("dp", "seq"), axis=0, tiled=True),
            lax.all_gather(shards[13], ("dp", "seq"), axis=0, tiled=True),
            lax.all_gather(shards[14], ("dp", "seq"), axis=0, tiled=True),
        )
        live_rows = (
            (own_positions[None, :] < own_lengths[:, None])
            .astype(jnp.float32)
            .reshape(flat_rows, 1)
        )
        incoming = own_cots.reshape(flat_rows, model_width).astype(jnp.float32) * live_rows
        _, second_pull = jax.vjp(
            layer_norm, resid_two, widen(back_weights[13]), widen(back_weights[14])
        )
        grad_two, grad_gain_two, grad_shift_two = second_pull(incoming)
        feed_low = grad_two.astype(jnp.bfloat16)
        totals[11] = totals[11] + former_product(active_low, feed_low)
        totals[12] = totals[12] + jnp.sum(feed_low.astype(jnp.float32), 0)
        grad_active = latter_product(feed_low, back_weights[11])
        _, gelu_pull = jax.vjp(gelu_exact, hidden)
        up_low = gelu_pull(grad_active)[0].astype(jnp.bfloat16)
        totals[9] = totals[9] + former_product(normed_low, up_low)
        totals[10] = totals[10] + jnp.sum(up_low.astype(jnp.float32), 0)
        grad_normed = latter_product(up_low, back_weights[9]) + grad_two
        _, first_pull = jax.vjp(
            layer_norm, resid_one, widen(back_weights[7]), widen(back_weights[8])
        )
        grad_one, grad_gain_one, grad_shift_one = first_pull(grad_normed)
        branch_low = grad_one.astype(jnp.bfloat16)
        totals[5] = totals[5] + former_product(mixed_low, branch_low)
        totals[6] = totals[6] + jnp.sum(branch_low.astype(jnp.float32), 0)
        dmix_low = latter_product(branch_low, back_weights[5]).astype(jnp.bfloat16)
        dmix_heads = dmix_low.reshape(per_batch, block_rows, head_count, head_size)
        back_keys, backward_value_rows = (gathered_keys, gathered_values)
        chances = jnp.exp(score_block(back_keys) - logarithm_totals)
        back_value_heads = backward_value_rows.reshape(
            per_batch, full_length, head_count, head_size
        )
        back_key_heads = back_keys.reshape(per_batch, full_length, head_count, head_size)
        grad_chances = jnp.einsum(
            "pqhd,pkhd->phqk", dmix_heads, back_value_heads, preferred_element_type=jnp.float32
        )
        row_inner = jnp.sum(grad_chances * chances, -1, keepdims=True)
        dscore_low = (score_scale * (chances * (grad_chances - row_inner))).astype(jnp.bfloat16)
        dquery_low = jnp.einsum(
            "phqk,pkhd->pqhd", dscore_low, back_key_heads, preferred_element_type=jnp.float32
        )
        dquery_low = dquery_low.reshape(flat_rows, model_width).astype(jnp.bfloat16)
        chance_low = chances.astype(jnp.bfloat16)
        value_terms = jnp.einsum(
            "phqk,pqhd->pkhd", chance_low, dmix_heads, preferred_element_type=jnp.float32
        )
        key_terms = jnp.einsum(
            "phqk,pqhd->pkhd", dscore_low, query_heads, preferred_element_type=jnp.float32
        )
        key_sums, value_sums = (
            lax.psum_scatter(
                key_terms.reshape(per_batch, full_length, model_width).astype(jnp.bfloat16),
                "seq",
                scatter_dimension=1,
                tiled=True,
            ).astype(jnp.float32),
            lax.psum_scatter(
                value_terms.reshape(per_batch, full_length, model_width).astype(jnp.bfloat16),
                "seq",
                scatter_dimension=1,
                tiled=True,
            ).astype(jnp.float32),
        )
        dkey_low = key_sums.reshape(flat_rows, model_width).astype(jnp.bfloat16)
        dvalue_low = value_sums.reshape(flat_rows, model_width).astype(jnp.bfloat16)
        totals[0] = totals[0] + former_product(flat_tokens, dquery_low)
        totals[1] = totals[1] + jnp.sum(dquery_low.astype(jnp.float32), 0)
        totals[2] = totals[2] + former_product(flat_tokens, dkey_low)
        totals[3] = totals[3] + former_product(flat_tokens, dvalue_low)
        totals[4] = totals[4] + jnp.sum(dvalue_low.astype(jnp.float32), 0)
        totals[7] = totals[7] + grad_gain_one
        totals[8] = totals[8] + grad_shift_one
        totals[13] = totals[13] + grad_gain_two
        totals[14] = totals[14] + grad_shift_two
        grad_input = (
            latter_product(dquery_low, back_weights[0])
            + latter_product(dkey_low, back_weights[2])
            + latter_product(dvalue_low, back_weights[3])
            + grad_one
        )
        input_grads.append(grad_input.reshape(per_batch, block_rows, model_width))
    owned = lax.psum_scatter(tuple(totals), ("dp", "seq"), scatter_dimension=0, tiled=True)
    output = jnp.concatenate(outputs, 0)
    grad_tokens = jnp.concatenate(input_grads, 0)
    return (
        output,
        grad_tokens,
        owned[0],
        owned[1],
        owned[2],
        owned[3],
        owned[4],
        owned[5],
        owned[6],
        owned[7],
        owned[8],
        owned[9],
        owned[10],
        owned[11],
        owned[12],
        owned[13],
        owned[14],
    )


LOG2E = 1.4426950408889634
PAD = 16
VMEM = 60 << 20
RATE = 1e9


def cost(microseconds):
    return pl.CostEstimate(flops=int(microseconds * RATE), bytes_accessed=0, transcendentals=0)


def contract(former, latter, dim_former, dim_latter):
    return lax.dot_general(
        former,
        latter,
        (((dim_former,), (dim_latter,)), ((), ())),
        preferred_element_type=jnp.float32,
    )


def mix_kernel(scale, chunk, me, qt, kt, vt, bias, mixed, total, probs, keys, vals):
    size, slots = kt.shape[1], kt.shape[2]
    places = [
        pl.ds(pl.multiple_of((me[0] ^ b) * chunk, chunk), chunk) for b in range(slots // chunk)
    ]
    key = kt[0]
    keys[...] = jnp.concatenate([key, key, bias[...]], 0).T
    vals[...] = jnp.concatenate([vt[0], jnp.ones((PAD, slots), jnp.bfloat16)], 0)
    query = qt[0].astype(jnp.float32) * scale
    high = query.astype(jnp.bfloat16)
    low = (query - high.astype(jnp.float32)).astype(jnp.bfloat16)
    row = lax.broadcasted_iota(jnp.int32, (PAD, slots), 0)
    first = jnp.where(row == 0, 1.0, 0.0).astype(jnp.bfloat16)
    columns = jnp.concatenate([high, low, first], 0)

    def finish(sums):
        weight = sums[size : size + 1]
        mixed[0] = (sums[:size] / weight).astype(mixed.dtype)
        total[0] = weight
        return weight

    sums, top = None, None
    for at in places:
        scores = contract(keys[at], columns, 1, 0)
        if top is None:
            top = jnp.max(scores[: chunk // 2], 0, keepdims=True)
        part = jnp.exp2(scores - top).astype(jnp.bfloat16)
        probs[0, at] = part
        term = contract(vals[:, at], part, 1, 0)
        sums = term if sums is None else sums + term
    weight = finish(sums)

    @pl.when(jnp.logical_not(jnp.max(weight) < 2.0**60))
    def _():
        top = jnp.full((1, slots), -jnp.inf, jnp.float32)
        for at in places:
            scores = contract(keys[at], columns, 1, 0)
            top = jnp.maximum(top, jnp.max(scores, 0, keepdims=True))
        sums = None
        for at in places:
            scores = contract(keys[at], columns, 1, 0)
            part = jnp.exp2(scores - top).astype(jnp.bfloat16)
            probs[0, at] = part
            term = contract(vals[:, at], part, 1, 0)
            sums = term if sums is None else sums + term
        finish(sums)


def mix(me, qt, kt, vt, bias, scale, chunk):
    heads, size, slots = qt.shape
    whole = pl.BlockSpec((1, size, slots), lambda i: (i, 0, 0))
    return pl.pallas_call(
        functools.partial(mix_kernel, scale, chunk),
        grid=(heads,),
        in_specs=[
            pl.BlockSpec(memory_space=pltpu.SMEM),
            whole,
            whole,
            whole,
            pl.BlockSpec((PAD, slots), lambda i: (0, 0)),
        ],
        out_specs=[
            whole,
            pl.BlockSpec((1, 1, slots), lambda i: (i, 0, 0)),
            pl.BlockSpec((1, slots, slots), lambda i: (i, 0, 0)),
        ],
        out_shape=[
            jax.ShapeDtypeStruct((heads, size, slots), jnp.bfloat16),
            jax.ShapeDtypeStruct((heads, 1, slots), jnp.float32),
            jax.ShapeDtypeStruct((heads, slots, slots), jnp.bfloat16),
        ],
        scratch_shapes=[
            pltpu.VMEM((slots, 2 * size + PAD), jnp.bfloat16),
            pltpu.VMEM((size + PAD, slots), jnp.bfloat16),
        ],
        compiler_params=pltpu.CompilerParams(vmem_limit_bytes=VMEM),
        cost_estimate=cost(57),
        name="mix",
    )(me, qt, kt, vt, bias)


def unmix_kernel(scale, probs, qt, kt, vt, gt, mt, total, out, grads, inner, sums):
    step, last = pl.program_id(1), pl.num_programs(1) - 1
    keys = kt.shape[2]
    here = pl.ds(pl.multiple_of(step * keys, keys), keys)

    @pl.when(step == 0)
    def _():
        scaled = (gt[0].astype(jnp.float32) / total[0]).astype(jnp.bfloat16)
        grads[...] = scaled
        inner[...] = jnp.sum(
            scaled.astype(jnp.float32) * mt[0].astype(jnp.float32), 0, keepdims=True
        )

    grad = grads[...]
    prob = probs[0]
    dprob = contract(vt[0], grad, 0, 0)
    dscore = (prob.astype(jnp.float32) * (dprob - inner[...])).astype(jnp.bfloat16)
    part = contract(kt[0], dscore, 1, 0)
    out[2, 0, :, here] = contract(prob, grad, 1, 1).T.astype(jnp.bfloat16)
    out[1, 0, :, here] = (contract(dscore, qt[0], 1, 1) * scale).T.astype(jnp.bfloat16)

    @pl.when(step == 0)
    def _():
        sums[...] = part

    @pl.when(step > 0)
    def _():
        sums[...] += part

    @pl.when(step == last)
    def _():
        out[0, 0] = (sums[...] * scale).astype(jnp.bfloat16)


def unmix(probs, qt, kt, vt, gt, mt, total, scale):
    heads, size, slots = qt.shape
    keys = slots // 2
    whole = pl.BlockSpec((1, size, slots), lambda i, j: (i, 0, 0))
    part = pl.BlockSpec((1, size, keys), lambda i, j: (i, 0, j))
    return pl.pallas_call(
        functools.partial(unmix_kernel, scale),
        grid=(heads, slots // keys),
        in_specs=[
            pl.BlockSpec((1, keys, slots), lambda i, j: (i, j, 0)),
            whole,
            part,
            part,
            whole,
            whole,
            pl.BlockSpec((1, 1, slots), lambda i, j: (i, 0, 0)),
        ],
        out_specs=pl.BlockSpec((3, 1, size, slots), lambda i, j: (0, i, 0, 0)),
        out_shape=jax.ShapeDtypeStruct((3, heads, size, slots), jnp.bfloat16),
        scratch_shapes=[
            pltpu.VMEM((size, slots), jnp.bfloat16),
            pltpu.VMEM((1, slots), jnp.float32),
            pltpu.VMEM((size, slots), jnp.float32),
        ],
        compiler_params=pltpu.CompilerParams(vmem_limit_bytes=VMEM),
        cost_estimate=cost(110),
        name="unmix",
    )(probs, qt, kt, vt, gt, mt, total)


def swap(piece, step):
    size = lax.axis_size("seq")
    return lax.ppermute(piece, "seq", [(i, i ^ step) for i in range(size)])


def take(array, index):
    return lax.dynamic_index_in_dim(array, index, 0, keepdims=False)


def to_own(array):
    me = lax.axis_index("seq")
    pieces = [take(array, me)]
    return pieces + [swap(take(array, me ^ step), step) for step in range(1, lax.axis_size("seq"))]


def to_split(rows):
    size = lax.axis_size("seq")
    block = rows.shape[0] // size
    pieces = [rows[step * block : (step + 1) * block] for step in range(size)]
    return pieces[:1] + [swap(pieces[step], step) for step in range(1, size)]


def placed(pieces, dtype):
    me = lax.axis_index("seq")
    result = jnp.zeros((len(pieces),) + pieces[0].shape, dtype)
    for step, piece in enumerate(pieces):
        result = lax.dynamic_update_index_in_dim(result, piece.astype(dtype), me ^ step, 0)
    return result


def row_sums(array):
    return jnp.sum(array, 0, keepdims=True)


def project_kernel(count, *refs):
    pieces, (w, vec, x, qt, kt, vt) = refs[:count], refs[count:]
    width = x.shape[1]
    bias = vec[...]
    for i, piece in enumerate(pieces):

        @pl.when(pl.program_id(0) == i)
        def _(piece=piece):
            x[...] = piece[...]

    outs = matmul(x[...], w[...])
    for i, out in enumerate((qt, kt, vt)):
        part = outs[:, i * width : (i + 1) * width]
        if i != 1:
            part = part + bias[i // 2 : i // 2 + 1]
        out[...] = part.astype(jnp.bfloat16).T


def project(pieces, first, vec):
    rows, width = pieces[0].shape
    count = len(pieces)
    slots = count * rows
    flat = pl.BlockSpec((width, rows), lambda i: (0, i))
    one = pl.Buffered(1)
    return pl.pallas_call(
        functools.partial(project_kernel, count),
        grid=(count,),
        in_specs=[pl.BlockSpec((rows, width), lambda i: (0, 0), pipeline_mode=one)] * count
        + [
            pl.BlockSpec((width, 3 * width), lambda i: (0, 0), pipeline_mode=one),
            pl.BlockSpec(vec.shape, lambda i: (0, 0)),
        ],
        out_specs=[pl.BlockSpec((rows, width), lambda i: (i, 0))] + [flat] * 3,
        out_shape=[jax.ShapeDtypeStruct((slots, width), jnp.bfloat16)]
        + [jax.ShapeDtypeStruct((width, slots), jnp.bfloat16)] * 3,
        compiler_params=pltpu.CompilerParams(vmem_limit_bytes=VMEM),
        cost_estimate=cost(11),
        name="project",
    )(*pieces, first, vec)


def norm(rows):
    centre = rows - jnp.mean(rows, -1, keepdims=True)
    rstd = lax.rsqrt(jnp.mean(centre * centre, -1, keepdims=True) + epsilon)
    return centre * rstd, rstd


def norm_back(unit, rstd, grad):
    mean = jnp.mean(grad, -1, keepdims=True)
    inner = jnp.mean(grad * unit, -1, keepdims=True)
    return rstd * (grad - mean - unit * inner)


def feed_kernel(
    x, mt, cot, live, vec, bu, wo, wu, wd,
    output, grad_one, gt, left, right, sums, up_sums, slope,
):
    width = x.shape[1]
    wide = wu.shape[1]
    step = pl.program_id(0)
    bo, g1, s1, bd, g2, s2 = (vec[i : i + 1] for i in range(2, 8))
    mixed = mt[...].T
    left[:, wide + width :] = mixed
    resid = x[...].astype(jnp.float32) + matmul(mixed, wo[...]) + bo
    unit_one, rstd_one = norm(resid)
    normed = unit_one * g1 + s1
    low = normed.astype(jnp.bfloat16)
    left[:, :width] = low
    resid = normed + bd
    for at in range(0, wide, width):
        cut = slice(at, at + width)
        hidden = matmul(low, wu[:, cut]) + bu[:, cut]
        share = 0.5 + 0.5 * lax.erf(hidden * 0.7071067811865476)
        bell = jnp.exp2(hidden * hidden * -0.7213475204444817) * 0.3989422804014327
        slope[:, cut] = (share + hidden * bell).astype(jnp.bfloat16)
        active = (hidden * share).astype(jnp.bfloat16)
        left[:, width + at : 2 * width + at] = active
        resid = resid + matmul(active, wd[:, cut])
    unit_two, rstd_two = norm(resid)
    output[...] = (unit_two * g2 + s2).astype(jnp.bfloat16)
    incoming = cot[...].astype(jnp.float32) * live[...]
    grad_two = norm_back(unit_two, rstd_two, incoming * g2)
    feed = grad_two.astype(jnp.bfloat16)
    right[:, wide : wide + width] = feed
    grad = grad_two
    up_rows = []
    for at in range(0, wide, width):
        cut = slice(at, at + width)
        part = contract(feed, wd[:, cut], 1, 1) * slope[:, cut].astype(jnp.float32)
        part = part.astype(jnp.bfloat16)
        right[:, cut] = part
        up_rows.append(row_sums(part.astype(jnp.float32)))
        grad = grad + contract(part, wu[:, cut], 1, 1)
    first = norm_back(unit_one, rstd_one, grad * g1)
    grad_one[...] = first
    branch = first.astype(jnp.bfloat16)
    right[:, wide + width :] = branch
    gt[...] = contract(wo[...], branch, 1, 1).astype(jnp.bfloat16)
    rows = [
        row_sums(branch.astype(jnp.float32)),
        row_sums(grad * unit_one),
        row_sums(grad),
        row_sums(feed.astype(jnp.float32)),
        row_sums(incoming * unit_two),
        row_sums(incoming),
    ]
    rows = jnp.concatenate(rows + [jnp.zeros((2, width), jnp.float32)], 0)
    wide_rows = jnp.concatenate(up_rows, 1)

    @pl.when(step == 0)
    def _():
        sums[...] = rows
        up_sums[...] = wide_rows

    @pl.when(step > 0)
    def _():
        sums[...] += rows
        up_sums[...] += wide_rows


def feed(x, mt, cot, live, vec, bu, second, rows):
    slots, width = x.shape
    wide = bu.shape[1]
    one = pl.Buffered(1)
    flat = pl.BlockSpec((rows, width), lambda i: (i, 0))
    tall = pl.BlockSpec((width, rows), lambda i: (0, i))
    stack = wide + 2 * width
    broad = pl.BlockSpec((rows, stack), lambda i: (i, 0))
    low = jnp.bfloat16
    return pl.pallas_call(
        feed_kernel,
        grid=(slots // rows,),
        in_specs=[
            flat,
            tall,
            flat,
            pl.BlockSpec((rows, 1), lambda i: (i, 0)),
            pl.BlockSpec(vec.shape, lambda i: (0, 0)),
            pl.BlockSpec((1, wide), lambda i: (0, 0)),
            pl.BlockSpec((width, width), lambda i: (0, 2 * wide // width), pipeline_mode=one),
            pl.BlockSpec((width, wide), lambda i: (0, 0), pipeline_mode=one),
            pl.BlockSpec((width, wide), lambda i: (0, 1), pipeline_mode=one),
        ],
        out_specs=[
            flat,
            flat,
            tall,
            broad,
            broad,
            pl.BlockSpec((8, width), lambda i: (0, 0)),
            pl.BlockSpec((1, wide), lambda i: (0, 0)),
        ],
        out_shape=[
            jax.ShapeDtypeStruct((slots, width), low),
            jax.ShapeDtypeStruct((slots, width), jnp.float32),
            jax.ShapeDtypeStruct((width, slots), low),
            jax.ShapeDtypeStruct((slots, stack), low),
            jax.ShapeDtypeStruct((slots, stack), low),
            jax.ShapeDtypeStruct((8, width), jnp.float32),
            jax.ShapeDtypeStruct((1, wide), jnp.float32),
        ],
        scratch_shapes=[pltpu.VMEM((rows, wide), low)],
        compiler_params=pltpu.CompilerParams(vmem_limit_bytes=VMEM),
        cost_estimate=cost(70),
        name="feed",
    )(x, mt, cot, live, vec, bu, second, second, second)


def feed_weights_kernel(left, right, d_w):
    d_w[...] = contract(left[...], right[...], 0, 0).astype(d_w.dtype)


def feed_weights(left, right, width):
    slots, stack = left.shape
    parts = stack // width - 2
    return pl.pallas_call(
        feed_weights_kernel,
        grid=(2 * parts + 1,),
        in_specs=[
            pl.BlockSpec((slots, width), lambda i: (0, jnp.maximum(i - parts + 1, 0))),
            pl.BlockSpec(
                (slots, width), lambda i: (0, jnp.minimum(i, parts) + i // (2 * parts))
            ),
        ],
        out_specs=pl.BlockSpec((width, width), lambda i: (0, i)),
        out_shape=jax.ShapeDtypeStruct((width, (2 * parts + 1) * width), jnp.bfloat16),
        compiler_params=pltpu.CompilerParams(vmem_limit_bytes=VMEM),
        cost_estimate=cost(26),
        name="feed_weights",
    )(left, right)


def inputs_kernel(grads, weights, grad_one, low):
    low[...] = (contract(grads[...], weights[...], 0, 1) + grad_one[...]).astype(low.dtype)


def inputs(grads, first, grad_one, rows):
    depth, slots = grads.shape
    width = first.shape[0]
    flat = pl.BlockSpec((rows, width), lambda i: (i, 0))
    return pl.pallas_call(
        inputs_kernel,
        grid=(slots // rows,),
        in_specs=[
            pl.BlockSpec((depth, rows), lambda i: (0, i)),
            pl.BlockSpec((width, depth), lambda i: (0, 0), pipeline_mode=pl.Buffered(1)),
            flat,
        ],
        out_specs=flat,
        out_shape=jax.ShapeDtypeStruct((slots, width), jnp.bfloat16),
        compiler_params=pltpu.CompilerParams(vmem_limit_bytes=VMEM),
        cost_estimate=cost(12),
        name="inputs",
    )(grads, first, grad_one)


def input_weights_kernel(x, grads, rows, d_w, edges):
    step, last = pl.program_id(0), pl.num_programs(0) - 1
    width = x.shape[1]
    depth = 3 * width
    size = grads.shape[0]
    grad = grads[...]
    product = contract(x[...], grad, 0, 1).astype(d_w.dtype)
    edge = jnp.sum(grad.astype(jnp.float32), 1, keepdims=True)
    for i in range(depth // size):

        @pl.when(step == i)
        def _(i=i):
            d_w[:, i * size : (i + 1) * size] = product
            column, top = i * size // width, i * size % width
            edges[top : top + size, column : column + 1] = edge

    @pl.when(step == last)
    def _():
        known = rows[...]
        tall = jnp.concatenate([known, jnp.zeros((128 - known.shape[0], width), jnp.float32)], 0).T
        column = lax.broadcasted_iota(jnp.int32, (width, 128), 1)
        sums = edges[...]
        columns = jnp.where(column == 0, sums[:, :1], jnp.where(column == 1, sums[:, 2:3], tall))
        d_w[:, depth:] = columns.astype(d_w.dtype)


def input_weights(x, grads, rows, size):
    slots, width = x.shape
    depth = grads.shape[0]
    one = pl.Buffered(1)
    return pl.pallas_call(
        input_weights_kernel,
        grid=(depth // size,),
        in_specs=[
            pl.BlockSpec((slots, width), lambda i: (0, 0), pipeline_mode=one),
            pl.BlockSpec((size, slots), lambda i: (i, 0)),
            pl.BlockSpec(rows.shape, lambda i: (0, 0)),
        ],
        out_specs=pl.BlockSpec((width, depth + 128), lambda i: (0, 0)),
        out_shape=jax.ShapeDtypeStruct((width, depth + 128), jnp.bfloat16),
        scratch_shapes=[pltpu.VMEM((width, 128), jnp.float32)],
        compiler_params=pltpu.CompilerParams(vmem_limit_bytes=VMEM),
        cost_estimate=cost(12),
        name="input_weights",
    )(x, grads, rows)


def whole_body(
    tokens,
    lengths,
    cotangent,
    w_query,
    b_query,
    w_key,
    w_value,
    b_value,
    w_out,
    b_out,
    gain_one,
    shift_one,
    w_up,
    b_up,
    w_down,
    b_down,
    gain_two,
    shift_two,
):
    count, block, width = tokens.shape
    slots = count * block
    wide = w_up.shape[1]
    rows = w_query.shape[0]
    axes = ("dp", "seq")
    me = lax.axis_index("seq")
    heads, size = H, HD
    scale = size ** (-0.5)
    times = wide // width

    vectors = [b_query, b_value, b_out, gain_one, shift_one, b_down, gain_two, shift_two, b_up]
    vec = jnp.concatenate(vectors)
    known = vec.shape[0]
    vec = jnp.pad(vec, (0, 1024 - known)).reshape(8, 128)
    first = jnp.concatenate([w_query, w_key, w_value], 1)
    first = lax.all_gather(first, "seq", axis=0, tiled=True)
    first = lax.all_gather(first, "dp", axis=0, tiled=True)
    owners = width // rows
    mixed_up = w_up.reshape(rows, owners, times, rows).transpose(0, 2, 1, 3).reshape(rows, wide)
    downs = [w_down[i * rows : (i + 1) * rows] for i in range(times)]
    second = jnp.concatenate([mixed_up] + downs + [w_out], 1)

    pieces = to_own(tokens)
    vec = lax.all_gather(vec, axes, axis=0, tiled=True)
    vec, pieces = lax.optimization_barrier((vec, pieces))
    second, first, pieces = lax.optimization_barrier((second, first, pieces))
    second = lax.all_gather(second, axes, axis=0, tiled=True)
    length = take(lengths, me)
    order = me ^ jnp.arange(count, dtype=jnp.int32)
    place = (order[:, None] * block + jnp.arange(block, dtype=jnp.int32)[None, :]).reshape(slots)
    live = place < length
    bias = jnp.where(live, 0.0, -1e30).astype(jnp.bfloat16)
    bias = jnp.pad(bias[None, :], ((0, PAD - 1), (0, 0)))
    live = live[:, None].astype(jnp.float32)

    vec = vec.reshape(owners, 1024)[:, :known]
    vec = vec.astype(jnp.float32).reshape(owners, 8 + times, rows).transpose(1, 0, 2)
    vec = vec.reshape(8 + times, width)
    bu = vec[8:].reshape(1, wide)
    vec = vec[:8]

    def by_head(array):
        return array.reshape(heads, size, slots)

    x, qt, kt, vt = project(pieces, first, vec)
    qt, cotangent = lax.optimization_barrier((qt, cotangent))
    cot = jnp.concatenate(to_own(cotangent), 0)
    qt, kt, vt = (by_head(a) for a in (qt, kt, vt))
    mt, total, probs = mix(me.reshape(1), qt, kt, vt, bias, scale * LOG2E, block)
    result, grad_one, gt, left, right, sums, up_sums = feed(
        x, mt.reshape(width, slots), cot, live, vec, bu, second, block
    )
    late = feed_weights(left, right, width)
    gt, late = lax.optimization_barrier((gt, late))
    late = lax.psum_scatter(late, "dp", scatter_dimension=0, tiled=True)
    output = to_split(result)
    grads = unmix(probs, qt, kt, vt, by_head(gt), mt, total, scale)
    grads, output, late = lax.optimization_barrier((grads, output, late))
    late = lax.psum_scatter(late, "seq", scatter_dimension=0, tiled=True)
    output = placed(output, jnp.bfloat16)
    grads = grads.reshape(3 * width, slots)
    edges = jnp.concatenate(
        [jnp.zeros((2, width), jnp.float32), sums[:6], up_sums.reshape(times, width)], 0
    )
    early = input_weights(x, grads, edges, width // 2)
    grads, early = lax.optimization_barrier((grads, early))
    low = inputs(grads, first, grad_one, block)
    grad_tokens = placed(to_split(low), jnp.float32)
    early, late = lax.optimization_barrier((early, late))
    early = lax.psum_scatter(early, "dp", scatter_dimension=0, tiled=True)
    early = lax.psum_scatter(early, "seq", scatter_dimension=0, tiled=True).astype(jnp.float32)
    late = late.astype(jnp.float32)
    o_wq, o_wk, o_wv = (early[:, i * width : (i + 1) * width] for i in range(3))
    vec = early[:, 3 * width :]
    o_wu = late[:, :wide].reshape(rows, times, owners, rows).transpose(0, 2, 1, 3).reshape(rows, wide)
    o_wd = jnp.concatenate(
        [late[:, wide + i * width : wide + (i + 1) * width] for i in range(times)], 0
    )
    o_wo = late[:, 2 * wide :]
    o_bq, o_bv, o_bo, o_g1, o_s1, o_bd, o_g2, o_s2 = (vec[:, i] for i in range(8))
    o_bu = vec[:, 8 : 8 + times].T.reshape(rows * times)
    return (
        output,
        grad_tokens,
        o_wq,
        o_bq,
        o_wk,
        o_wv,
        o_bv,
        o_wo,
        o_bo,
        o_g1,
        o_s1,
        o_wu,
        o_bu,
        o_wd,
        o_bd,
        o_g2,
        o_s2,
    )


def body(*arrays):
    count = arrays[0].shape[0]
    fits = count == lax.axis_size("seq") and count & (count - 1) == 0
    return whole_body(*arrays) if fits else general_body(*arrays)


def solution(mesh):
    in_specs = (
        P("dp", "seq", None),
        P("dp"),
        P("dp", "seq", None),
        P(("dp", "seq"), None),
        P(("dp", "seq")),
        P(("dp", "seq"), None),
        P(("dp", "seq"), None),
        P(("dp", "seq")),
        P(("dp", "seq"), None),
        P(("dp", "seq")),
        P(("dp", "seq")),
        P(("dp", "seq")),
        P(("dp", "seq"), None),
        P(("dp", "seq")),
        P(("dp", "seq"), None),
        P(("dp", "seq")),
        P(("dp", "seq")),
        P(("dp", "seq")),
    )
    out_specs = (
        P("dp", "seq", None),
        P("dp", "seq", None),
        P(("dp", "seq"), None),
        P(("dp", "seq")),
        P(("dp", "seq"), None),
        P(("dp", "seq"), None),
        P(("dp", "seq")),
        P(("dp", "seq"), None),
        P(("dp", "seq")),
        P(("dp", "seq")),
        P(("dp", "seq")),
        P(("dp", "seq"), None),
        P(("dp", "seq")),
        P(("dp", "seq"), None),
        P(("dp", "seq")),
        P(("dp", "seq")),
        P(("dp", "seq")),
    )
    return jax.shard_map(body, mesh=mesh, in_specs=in_specs, out_specs=out_specs, check_vma=False)
```

```python
import functools

import jax
import jax.numpy as jnp
from jax import lax
from jax.experimental import pallas as pl
from jax.experimental.pallas import tpu as pltpu
from jax.sharding import PartitionSpec as P

H = 12
HD = 64
MB = 4


epsilon = 1e-06


def layer_norm(layer_input_rows, norm_gain, norm_shift):
    centre = layer_input_rows - jnp.mean(layer_input_rows, -1, keepdims=True)
    spread = jnp.mean(centre * centre, -1, keepdims=True)
    return centre * lax.rsqrt(spread + epsilon) * norm_gain + norm_shift


def gelu_exact(values):
    return jax.nn.gelu(values, approximate=False)


def matmul(former, latter):
    return jnp.dot(former, latter, preferred_element_type=jnp.float32)


def former_product(former, latter):
    return lax.dot_general(
        former, latter, (((0,), (0,)), ((), ())), preferred_element_type=jnp.float32
    )


def latter_product(former, latter):
    return lax.dot_general(
        former, latter, (((1,), (1,)), ((), ())), preferred_element_type=jnp.float32
    )


def widen(vector):
    return vector.astype(jnp.float32)


def general_body(
    tokens,
    lengths,
    cotangent,
    w_query,
    b_query,
    w_key,
    w_value,
    b_value,
    w_out,
    b_out,
    gain_one,
    shift_one,
    w_up,
    b_up,
    w_down,
    b_down,
    gain_two,
    shift_two,
):
    shards = (
        w_query,
        b_query,
        w_key,
        w_value,
        b_value,
        w_out,
        b_out,
        gain_one,
        shift_one,
        w_up,
        b_up,
        w_down,
        b_down,
        gain_two,
        shift_two,
    )
    per_batch = tokens.shape[0] // MB
    block_rows = tokens.shape[1]
    model_width = tokens.shape[2]
    head_count = H
    head_size = HD
    flat_rows = per_batch * block_rows
    full_length = block_rows * lax.axis_size("seq")
    offset = lax.axis_index("seq") * block_rows
    positions = jnp.arange(full_length, dtype=jnp.int32)
    own_positions = offset + jnp.arange(block_rows, dtype=jnp.int32)
    score_scale = head_size ** (-0.5)
    owners = lax.axis_size(("dp", "seq"))
    totals = [
        jnp.zeros((shard_piece.shape[0] * owners,) + shard_piece.shape[1:], jnp.float32)
        for shard_piece in shards
    ]
    outputs = []
    input_grads = []
    for micro_batch in range(MB):
        leading_row = micro_batch * per_batch
        own_tokens = tokens[leading_row : leading_row + per_batch]
        own_lengths = lengths[leading_row : leading_row + per_batch]
        own_cots = cotangent[leading_row : leading_row + per_batch]
        fore_weights = (
            lax.all_gather(shards[0], ("dp", "seq"), axis=0, tiled=True),
            lax.all_gather(shards[1], ("dp", "seq"), axis=0, tiled=True),
            lax.all_gather(shards[2], ("dp", "seq"), axis=0, tiled=True),
            lax.all_gather(shards[3], ("dp", "seq"), axis=0, tiled=True),
            lax.all_gather(shards[4], ("dp", "seq"), axis=0, tiled=True),
            lax.all_gather(shards[5], ("dp", "seq"), axis=0, tiled=True),
            lax.all_gather(shards[6], ("dp", "seq"), axis=0, tiled=True),
            lax.all_gather(shards[7], ("dp", "seq"), axis=0, tiled=True),
            lax.all_gather(shards[8], ("dp", "seq"), axis=0, tiled=True),
            lax.all_gather(shards[9], ("dp", "seq"), axis=0, tiled=True),
            lax.all_gather(shards[10], ("dp", "seq"), axis=0, tiled=True),
            lax.all_gather(shards[11], ("dp", "seq"), axis=0, tiled=True),
            lax.all_gather(shards[12], ("dp", "seq"), axis=0, tiled=True),
            lax.all_gather(shards[13], ("dp", "seq"), axis=0, tiled=True),
            lax.all_gather(shards[14], ("dp", "seq"), axis=0, tiled=True),
        )
        flat_tokens = own_tokens.reshape(flat_rows, model_width)
        query_low = (matmul(flat_tokens, fore_weights[0]) + widen(fore_weights[1])).astype(
            jnp.bfloat16
        )
        key_low = matmul(flat_tokens, fore_weights[2]).astype(jnp.bfloat16)
        value_low = (matmul(flat_tokens, fore_weights[3]) + widen(fore_weights[4])).astype(
            jnp.bfloat16
        )
        key_block = key_low.reshape(per_batch, block_rows, model_width)
        value_block = value_low.reshape(per_batch, block_rows, model_width)
        gathered_keys, gathered_values = (
            lax.all_gather(key_block, "seq", axis=1, tiled=True),
            lax.all_gather(value_block, "seq", axis=1, tiled=True),
        )
        query_heads = query_low.reshape(per_batch, block_rows, head_count, head_size)
        visible = (positions[None, :] < own_lengths[:, None])[:, None, None, :]

        def score_block(key_all):
            key_heads = key_all.reshape(per_batch, full_length, head_count, head_size)
            raw_scores = jnp.einsum(
                "pqhd,pkhd->phqk", query_heads, key_heads, preferred_element_type=jnp.float32
            )
            return jnp.where(visible, raw_scores * score_scale, -1e30)

        scores = score_block(gathered_keys)
        logarithm_totals = jax.nn.logsumexp(scores, axis=-1, keepdims=True)
        chances_low = jnp.exp(scores - logarithm_totals).astype(jnp.bfloat16)
        value_heads = gathered_values.reshape(per_batch, full_length, head_count, head_size)
        mixed_heads = jnp.einsum(
            "phqk,pkhd->pqhd", chances_low, value_heads, preferred_element_type=jnp.float32
        )
        mixed_low = mixed_heads.reshape(flat_rows, model_width).astype(jnp.bfloat16)
        branch = matmul(mixed_low, fore_weights[5]) + widen(fore_weights[6])
        resid_one = flat_tokens.astype(jnp.float32) + branch
        normed = layer_norm(resid_one, widen(fore_weights[7]), widen(fore_weights[8]))
        normed_low = normed.astype(jnp.bfloat16)
        hidden = matmul(normed_low, fore_weights[9]) + widen(fore_weights[10])
        active_low = gelu_exact(hidden).astype(jnp.bfloat16)
        feed_out = matmul(active_low, fore_weights[11]) + widen(fore_weights[12])
        resid_two = normed + feed_out
        result = layer_norm(resid_two, widen(fore_weights[13]), widen(fore_weights[14]))
        outputs.append(result.astype(jnp.bfloat16).reshape(per_batch, block_rows, model_width))
        back_weights = (
            lax.all_gather(shards[0], ("dp", "seq"), axis=0, tiled=True),
            lax.all_gather(shards[1], ("dp", "seq"), axis=0, tiled=True),
            lax.all_gather(shards[2], ("dp", "seq"), axis=0, tiled=True),
            lax.all_gather(shards[3], ("dp", "seq"), axis=0, tiled=True),
            lax.all_gather(shards[4], ("dp", "seq"), axis=0, tiled=True),
            lax.all_gather(shards[5], ("dp", "seq"), axis=0, tiled=True),
            lax.all_gather(shards[6], ("dp", "seq"), axis=0, tiled=True),
            lax.all_gather(shards[7], ("dp", "seq"), axis=0, tiled=True),
            lax.all_gather(shards[8], ("dp", "seq"), axis=0, tiled=True),
            lax.all_gather(shards[9], ("dp", "seq"), axis=0, tiled=True),
            lax.all_gather(shards[10], ("dp", "seq"), axis=0, tiled=True),
            lax.all_gather(shards[11], ("dp", "seq"), axis=0, tiled=True),
            lax.all_gather(shards[12], ("dp", "seq"), axis=0, tiled=True),
            lax.all_gather(shards[13], ("dp", "seq"), axis=0, tiled=True),
            lax.all_gather(shards[14], ("dp", "seq"), axis=0, tiled=True),
        )
        live_rows = (
            (own_positions[None, :] < own_lengths[:, None])
            .astype(jnp.float32)
            .reshape(flat_rows, 1)
        )
        incoming = own_cots.reshape(flat_rows, model_width).astype(jnp.float32) * live_rows
        _, second_pull = jax.vjp(
            layer_norm, resid_two, widen(back_weights[13]), widen(back_weights[14])
        )
        grad_two, grad_gain_two, grad_shift_two = second_pull(incoming)
        feed_low = grad_two.astype(jnp.bfloat16)
        totals[11] = totals[11] + former_product(active_low, feed_low)
        totals[12] = totals[12] + jnp.sum(feed_low.astype(jnp.float32), 0)
        grad_active = latter_product(feed_low, back_weights[11])
        _, gelu_pull = jax.vjp(gelu_exact, hidden)
        up_low = gelu_pull(grad_active)[0].astype(jnp.bfloat16)
        totals[9] = totals[9] + former_product(normed_low, up_low)
        totals[10] = totals[10] + jnp.sum(up_low.astype(jnp.float32), 0)
        grad_normed = latter_product(up_low, back_weights[9]) + grad_two
        _, first_pull = jax.vjp(
            layer_norm, resid_one, widen(back_weights[7]), widen(back_weights[8])
        )
        grad_one, grad_gain_one, grad_shift_one = first_pull(grad_normed)
        branch_low = grad_one.astype(jnp.bfloat16)
        totals[5] = totals[5] + former_product(mixed_low, branch_low)
        totals[6] = totals[6] + jnp.sum(branch_low.astype(jnp.float32), 0)
        dmix_low = latter_product(branch_low, back_weights[5]).astype(jnp.bfloat16)
        dmix_heads = dmix_low.reshape(per_batch, block_rows, head_count, head_size)
        back_keys, backward_value_rows = (gathered_keys, gathered_values)
        chances = jnp.exp(score_block(back_keys) - logarithm_totals)
        back_value_heads = backward_value_rows.reshape(
            per_batch, full_length, head_count, head_size
        )
        back_key_heads = back_keys.reshape(per_batch, full_length, head_count, head_size)
        grad_chances = jnp.einsum(
            "pqhd,pkhd->phqk", dmix_heads, back_value_heads, preferred_element_type=jnp.float32
        )
        row_inner = jnp.sum(grad_chances * chances, -1, keepdims=True)
        dscore_low = (score_scale * (chances * (grad_chances - row_inner))).astype(jnp.bfloat16)
        dquery_low = jnp.einsum(
            "phqk,pkhd->pqhd", dscore_low, back_key_heads, preferred_element_type=jnp.float32
        )
        dquery_low = dquery_low.reshape(flat_rows, model_width).astype(jnp.bfloat16)
        chance_low = chances.astype(jnp.bfloat16)
        value_terms = jnp.einsum(
            "phqk,pqhd->pkhd", chance_low, dmix_heads, preferred_element_type=jnp.float32
        )
        key_terms = jnp.einsum(
            "phqk,pqhd->pkhd", dscore_low, query_heads, preferred_element_type=jnp.float32
        )
        key_sums, value_sums = (
            lax.psum_scatter(
                key_terms.reshape(per_batch, full_length, model_width).astype(jnp.bfloat16),
                "seq",
                scatter_dimension=1,
                tiled=True,
            ).astype(jnp.float32),
            lax.psum_scatter(
                value_terms.reshape(per_batch, full_length, model_width).astype(jnp.bfloat16),
                "seq",
                scatter_dimension=1,
                tiled=True,
            ).astype(jnp.float32),
        )
        dkey_low = key_sums.reshape(flat_rows, model_width).astype(jnp.bfloat16)
        dvalue_low = value_sums.reshape(flat_rows, model_width).astype(jnp.bfloat16)
        totals[0] = totals[0] + former_product(flat_tokens, dquery_low)
        totals[1] = totals[1] + jnp.sum(dquery_low.astype(jnp.float32), 0)
        totals[2] = totals[2] + former_product(flat_tokens, dkey_low)
        totals[3] = totals[3] + former_product(flat_tokens, dvalue_low)
        totals[4] = totals[4] + jnp.sum(dvalue_low.astype(jnp.float32), 0)
        totals[7] = totals[7] + grad_gain_one
        totals[8] = totals[8] + grad_shift_one
        totals[13] = totals[13] + grad_gain_two
        totals[14] = totals[14] + grad_shift_two
        grad_input = (
            latter_product(dquery_low, back_weights[0])
            + latter_product(dkey_low, back_weights[2])
            + latter_product(dvalue_low, back_weights[3])
            + grad_one
        )
        input_grads.append(grad_input.reshape(per_batch, block_rows, model_width))
    owned = lax.psum_scatter(tuple(totals), ("dp", "seq"), scatter_dimension=0, tiled=True)
    output = jnp.concatenate(outputs, 0)
    grad_tokens = jnp.concatenate(input_grads, 0)
    return (
        output,
        grad_tokens,
        owned[0],
        owned[1],
        owned[2],
        owned[3],
        owned[4],
        owned[5],
        owned[6],
        owned[7],
        owned[8],
        owned[9],
        owned[10],
        owned[11],
        owned[12],
        owned[13],
        owned[14],
    )


LOG2E = 1.4426950408889634
PAD = 16
VMEM = 60 << 20
RATE = 1e9


def cost(microseconds):
    return pl.CostEstimate(flops=int(microseconds * RATE), bytes_accessed=0, transcendentals=0)


def contract(former, latter, dim_former, dim_latter):
    return lax.dot_general(
        former,
        latter,
        (((dim_former,), (dim_latter,)), ((), ())),
        preferred_element_type=jnp.float32,
    )


def mix_kernel(scale, chunk, me, qt, kt, vt, bias, mixed, total, probs, keys, vals):
    size, slots = kt.shape[1], kt.shape[2]
    places = [
        pl.ds(pl.multiple_of((me[0] ^ b) * chunk, chunk), chunk) for b in range(slots // chunk)
    ]
    key = kt[0]
    keys[...] = jnp.concatenate([key, key, bias[...]], 0).T
    vals[...] = jnp.concatenate([vt[0], jnp.ones((PAD, slots), jnp.bfloat16)], 0)
    query = qt[0].astype(jnp.float32) * scale
    high = query.astype(jnp.bfloat16)
    low = (query - high.astype(jnp.float32)).astype(jnp.bfloat16)
    row = lax.broadcasted_iota(jnp.int32, (PAD, slots), 0)
    first = jnp.where(row == 0, 1.0, 0.0).astype(jnp.bfloat16)
    columns = jnp.concatenate([high, low, first], 0)

    def finish(sums):
        weight = sums[size : size + 1]
        mixed[0] = (sums[:size] / weight).astype(mixed.dtype)
        total[0] = weight
        return weight

    sums, top = None, None
    for at in places:
        scores = contract(keys[at], columns, 1, 0)
        if top is None:
            top = jnp.max(scores[: chunk // 2], 0, keepdims=True)
        part = jnp.exp2(scores - top).astype(jnp.bfloat16)
        probs[0, at] = part
        term = contract(vals[:, at], part, 1, 0)
        sums = term if sums is None else sums + term
    weight = finish(sums)

    @pl.when(jnp.logical_not(jnp.max(weight) < 2.0**60))
    def _():
        top = jnp.full((1, slots), -jnp.inf, jnp.float32)
        for at in places:
            scores = contract(keys[at], columns, 1, 0)
            top = jnp.maximum(top, jnp.max(scores, 0, keepdims=True))
        sums = None
        for at in places:
            scores = contract(keys[at], columns, 1, 0)
            part = jnp.exp2(scores - top).astype(jnp.bfloat16)
            probs[0, at] = part
            term = contract(vals[:, at], part, 1, 0)
            sums = term if sums is None else sums + term
        finish(sums)


def mix(me, qt, kt, vt, bias, scale, chunk):
    heads, size, slots = qt.shape
    whole = pl.BlockSpec((1, size, slots), lambda i: (i, 0, 0))
    return pl.pallas_call(
        functools.partial(mix_kernel, scale, chunk),
        grid=(heads,),
        in_specs=[
            pl.BlockSpec(memory_space=pltpu.SMEM),
            whole,
            whole,
            whole,
            pl.BlockSpec((PAD, slots), lambda i: (0, 0)),
        ],
        out_specs=[
            whole,
            pl.BlockSpec((1, 1, slots), lambda i: (i, 0, 0)),
            pl.BlockSpec((1, slots, slots), lambda i: (i, 0, 0)),
        ],
        out_shape=[
            jax.ShapeDtypeStruct((heads, size, slots), jnp.bfloat16),
            jax.ShapeDtypeStruct((heads, 1, slots), jnp.float32),
            jax.ShapeDtypeStruct((heads, slots, slots), jnp.bfloat16),
        ],
        scratch_shapes=[
            pltpu.VMEM((slots, 2 * size + PAD), jnp.bfloat16),
            pltpu.VMEM((size + PAD, slots), jnp.bfloat16),
        ],
        compiler_params=pltpu.CompilerParams(vmem_limit_bytes=VMEM),
        cost_estimate=cost(57),
        name="mix",
    )(me, qt, kt, vt, bias)


def unmix_kernel(scale, probs, qt, kt, vt, gt, mt, total, out, grads, inner, sums):
    step, last = pl.program_id(1), pl.num_programs(1) - 1
    keys = kt.shape[2]
    here = pl.ds(pl.multiple_of(step * keys, keys), keys)

    @pl.when(step == 0)
    def _():
        scaled = (gt[0].astype(jnp.float32) / total[0]).astype(jnp.bfloat16)
        grads[...] = scaled
        inner[...] = jnp.sum(
            scaled.astype(jnp.float32) * mt[0].astype(jnp.float32), 0, keepdims=True
        )

    grad = grads[...]
    prob = probs[0]
    dprob = contract(vt[0], grad, 0, 0)
    dscore = (prob.astype(jnp.float32) * (dprob - inner[...])).astype(jnp.bfloat16)
    part = contract(kt[0], dscore, 1, 0)
    out[2, 0, :, here] = contract(prob, grad, 1, 1).T.astype(jnp.bfloat16)
    out[1, 0, :, here] = (contract(dscore, qt[0], 1, 1) * scale).T.astype(jnp.bfloat16)

    @pl.when(step == 0)
    def _():
        sums[...] = part

    @pl.when(step > 0)
    def _():
        sums[...] += part

    @pl.when(step == last)
    def _():
        out[0, 0] = (sums[...] * scale).astype(jnp.bfloat16)


def unmix(probs, qt, kt, vt, gt, mt, total, scale):
    heads, size, slots = qt.shape
    keys = slots // 2
    whole = pl.BlockSpec((1, size, slots), lambda i, j: (i, 0, 0))
    part = pl.BlockSpec((1, size, keys), lambda i, j: (i, 0, j))
    return pl.pallas_call(
        functools.partial(unmix_kernel, scale),
        grid=(heads, slots // keys),
        in_specs=[
            pl.BlockSpec((1, keys, slots), lambda i, j: (i, j, 0)),
            whole,
            part,
            part,
            whole,
            whole,
            pl.BlockSpec((1, 1, slots), lambda i, j: (i, 0, 0)),
        ],
        out_specs=pl.BlockSpec((3, 1, size, slots), lambda i, j: (0, i, 0, 0)),
        out_shape=jax.ShapeDtypeStruct((3, heads, size, slots), jnp.bfloat16),
        scratch_shapes=[
            pltpu.VMEM((size, slots), jnp.bfloat16),
            pltpu.VMEM((1, slots), jnp.float32),
            pltpu.VMEM((size, slots), jnp.float32),
        ],
        compiler_params=pltpu.CompilerParams(vmem_limit_bytes=VMEM),
        cost_estimate=cost(110),
        name="unmix",
    )(probs, qt, kt, vt, gt, mt, total)


def swap(piece, step):
    size = lax.axis_size("seq")
    return lax.ppermute(piece, "seq", [(i, i ^ step) for i in range(size)])


def take(array, index):
    return lax.dynamic_index_in_dim(array, index, 0, keepdims=False)


def to_own(array):
    me = lax.axis_index("seq")
    pieces = [take(array, me)]
    return pieces + [swap(take(array, me ^ step), step) for step in range(1, lax.axis_size("seq"))]


def to_split(rows):
    size = lax.axis_size("seq")
    block = rows.shape[0] // size
    pieces = [rows[step * block : (step + 1) * block] for step in range(size)]
    return pieces[:1] + [swap(pieces[step], step) for step in range(1, size)]


def scattered(rows):
    me = lax.axis_index("seq")
    size = lax.axis_size("seq")
    parts = rows.reshape(size, rows.shape[0] // size, rows.shape[1])
    total = take(parts, me).astype(jnp.float32)
    for step in range(1, size):
        total = total + swap(take(parts, me ^ step), step).astype(jnp.float32)
    return total


def placed(pieces, dtype):
    me = lax.axis_index("seq")
    result = jnp.zeros((len(pieces),) + pieces[0].shape, dtype)
    for step, piece in enumerate(pieces):
        result = lax.dynamic_update_index_in_dim(result, piece.astype(dtype), me ^ step, 0)
    return result


def row_sums(array):
    return jnp.sum(array, 0, keepdims=True)


def project_kernel(count, *refs):
    pieces, (w, vec, x, qt, kt, vt) = refs[:count], refs[count:]
    width = x.shape[1]
    bias = vec[...]
    for i, piece in enumerate(pieces):

        @pl.when(pl.program_id(0) == i)
        def _(piece=piece):
            x[...] = piece[...]

    outs = matmul(x[...], w[...])
    for i, out in enumerate((qt, kt, vt)):
        part = outs[:, i * width : (i + 1) * width]
        if i != 1:
            part = part + bias[i // 2 : i // 2 + 1]
        out[...] = part.astype(jnp.bfloat16).T


def project(pieces, first, vec):
    rows, width = pieces[0].shape
    count = len(pieces)
    slots = count * rows
    flat = pl.BlockSpec((width, rows), lambda i: (0, i))
    one = pl.Buffered(1)
    return pl.pallas_call(
        functools.partial(project_kernel, count),
        grid=(count,),
        in_specs=[pl.BlockSpec((rows, width), lambda i: (0, 0), pipeline_mode=one)] * count
        + [
            pl.BlockSpec((width, 3 * width), lambda i: (0, 0), pipeline_mode=one),
            pl.BlockSpec(vec.shape, lambda i: (0, 0)),
        ],
        out_specs=[pl.BlockSpec((rows, width), lambda i: (i, 0))] + [flat] * 3,
        out_shape=[jax.ShapeDtypeStruct((slots, width), jnp.bfloat16)]
        + [jax.ShapeDtypeStruct((width, slots), jnp.bfloat16)] * 3,
        compiler_params=pltpu.CompilerParams(vmem_limit_bytes=VMEM),
        cost_estimate=cost(11),
        name="project",
    )(*pieces, first, vec)


def norm(rows):
    centre = rows - jnp.mean(rows, -1, keepdims=True)
    rstd = lax.rsqrt(jnp.mean(centre * centre, -1, keepdims=True) + epsilon)
    return centre * rstd, rstd


def norm_back(unit, rstd, grad):
    mean = jnp.mean(grad, -1, keepdims=True)
    inner = jnp.mean(grad * unit, -1, keepdims=True)
    return rstd * (grad - mean - unit * inner)


def feed_kernel(
    x, mt, cot, live, vec, bu, wo, wu, wd,
    output, grad_one, gt, left, right, sums, up_sums, slope,
):
    width = x.shape[1]
    wide = wu.shape[1]
    step = pl.program_id(0)
    bo, g1, s1, bd, g2, s2 = (vec[i : i + 1] for i in range(2, 8))
    mixed = mt[...].T
    left[:, wide + width :] = mixed
    resid = x[...].astype(jnp.float32) + matmul(mixed, wo[...]) + bo
    unit_one, rstd_one = norm(resid)
    normed = unit_one * g1 + s1
    low = normed.astype(jnp.bfloat16)
    left[:, :width] = low
    resid = normed + bd
    for at in range(0, wide, width):
        cut = slice(at, at + width)
        hidden = matmul(low, wu[:, cut]) + bu[:, cut]
        share = 0.5 + 0.5 * lax.erf(hidden * 0.7071067811865476)
        bell = jnp.exp2(hidden * hidden * -0.7213475204444817) * 0.3989422804014327
        slope[:, cut] = (share + hidden * bell).astype(jnp.bfloat16)
        active = (hidden * share).astype(jnp.bfloat16)
        left[:, width + at : 2 * width + at] = active
        resid = resid + matmul(active, wd[:, cut])
    unit_two, rstd_two = norm(resid)
    output[...] = (unit_two * g2 + s2).astype(jnp.bfloat16)
    incoming = cot[...].astype(jnp.float32) * live[...]
    grad_two = norm_back(unit_two, rstd_two, incoming * g2)
    feed = grad_two.astype(jnp.bfloat16)
    right[:, wide : wide + width] = feed
    grad = grad_two
    up_rows = []
    for at in range(0, wide, width):
        cut = slice(at, at + width)
        part = contract(feed, wd[:, cut], 1, 1) * slope[:, cut].astype(jnp.float32)
        part = part.astype(jnp.bfloat16)
        right[:, cut] = part
        up_rows.append(row_sums(part.astype(jnp.float32)))
        grad = grad + contract(part, wu[:, cut], 1, 1)
    first = norm_back(unit_one, rstd_one, grad * g1)
    grad_one[...] = first
    branch = first.astype(jnp.bfloat16)
    right[:, wide + width :] = branch
    gt[...] = contract(wo[...], branch, 1, 1).astype(jnp.bfloat16)
    rows = [
        row_sums(branch.astype(jnp.float32)),
        row_sums(grad * unit_one),
        row_sums(grad),
        row_sums(feed.astype(jnp.float32)),
        row_sums(incoming * unit_two),
        row_sums(incoming),
    ]
    rows = jnp.concatenate(rows + [jnp.zeros((2, width), jnp.float32)], 0)
    wide_rows = jnp.concatenate(up_rows, 1)

    @pl.when(step == 0)
    def _():
        sums[...] = rows
        up_sums[...] = wide_rows

    @pl.when(step > 0)
    def _():
        sums[...] += rows
        up_sums[...] += wide_rows


def feed(x, mt, cot, live, vec, bu, second, rows):
    slots, width = x.shape
    wide = bu.shape[1]
    one = pl.Buffered(1)
    flat = pl.BlockSpec((rows, width), lambda i: (i, 0))
    tall = pl.BlockSpec((width, rows), lambda i: (0, i))
    stack = wide + 2 * width
    broad = pl.BlockSpec((rows, stack), lambda i: (i, 0))
    low = jnp.bfloat16
    return pl.pallas_call(
        feed_kernel,
        grid=(slots // rows,),
        in_specs=[
            flat,
            tall,
            flat,
            pl.BlockSpec((rows, 1), lambda i: (i, 0)),
            pl.BlockSpec(vec.shape, lambda i: (0, 0)),
            pl.BlockSpec((1, wide), lambda i: (0, 0)),
            pl.BlockSpec((width, width), lambda i: (0, 2 * wide // width), pipeline_mode=one),
            pl.BlockSpec((width, wide), lambda i: (0, 0), pipeline_mode=one),
            pl.BlockSpec((width, wide), lambda i: (0, 1), pipeline_mode=one),
        ],
        out_specs=[
            flat,
            flat,
            tall,
            broad,
            broad,
            pl.BlockSpec((8, width), lambda i: (0, 0)),
            pl.BlockSpec((1, wide), lambda i: (0, 0)),
        ],
        out_shape=[
            jax.ShapeDtypeStruct((slots, width), low),
            jax.ShapeDtypeStruct((slots, width), jnp.float32),
            jax.ShapeDtypeStruct((width, slots), low),
            jax.ShapeDtypeStruct((slots, stack), low),
            jax.ShapeDtypeStruct((slots, stack), low),
            jax.ShapeDtypeStruct((8, width), jnp.float32),
            jax.ShapeDtypeStruct((1, wide), jnp.float32),
        ],
        scratch_shapes=[pltpu.VMEM((rows, wide), low)],
        compiler_params=pltpu.CompilerParams(vmem_limit_bytes=VMEM),
        cost_estimate=cost(70),
        name="feed",
    )(x, mt, cot, live, vec, bu, second, second, second)


def feed_weights_kernel(left, right, d_w):
    d_w[...] = contract(left[...], right[...], 0, 0).astype(d_w.dtype)


def feed_weights(left, right, width):
    slots, stack = left.shape
    parts = stack // width - 2
    return pl.pallas_call(
        feed_weights_kernel,
        grid=(2 * parts + 1,),
        in_specs=[
            pl.BlockSpec((slots, width), lambda i: (0, jnp.maximum(i - parts + 1, 0))),
            pl.BlockSpec(
                (slots, width), lambda i: (0, jnp.minimum(i, parts) + i // (2 * parts))
            ),
        ],
        out_specs=pl.BlockSpec((width, width), lambda i: (0, i)),
        out_shape=jax.ShapeDtypeStruct((width, (2 * parts + 1) * width), jnp.bfloat16),
        compiler_params=pltpu.CompilerParams(vmem_limit_bytes=VMEM),
        cost_estimate=cost(26),
        name="feed_weights",
    )(left, right)


def inputs_kernel(grads, weights, grad_one, low):
    low[...] = (contract(grads[...], weights[...], 0, 1) + grad_one[...]).astype(low.dtype)


def inputs(grads, first, grad_one, rows):
    depth, slots = grads.shape
    width = first.shape[0]
    flat = pl.BlockSpec((rows, width), lambda i: (i, 0))
    return pl.pallas_call(
        inputs_kernel,
        grid=(slots // rows,),
        in_specs=[
            pl.BlockSpec((depth, rows), lambda i: (0, i)),
            pl.BlockSpec((width, depth), lambda i: (0, 0), pipeline_mode=pl.Buffered(1)),
            flat,
        ],
        out_specs=flat,
        out_shape=jax.ShapeDtypeStruct((slots, width), jnp.bfloat16),
        compiler_params=pltpu.CompilerParams(vmem_limit_bytes=VMEM),
        cost_estimate=cost(12),
        name="inputs",
    )(grads, first, grad_one)


def input_weights_kernel(x, grads, rows, d_w, edges):
    step, last = pl.program_id(0), pl.num_programs(0) - 1
    width = x.shape[1]
    depth = 3 * width
    size = grads.shape[0]
    grad = grads[...]
    product = contract(x[...], grad, 0, 1).astype(d_w.dtype)
    edge = jnp.sum(grad.astype(jnp.float32), 1, keepdims=True)
    for i in range(depth // size):

        @pl.when(step == i)
        def _(i=i):
            d_w[:, i * size : (i + 1) * size] = product
            column, top = i * size // width, i * size % width
            edges[top : top + size, column : column + 1] = edge

    @pl.when(step == last)
    def _():
        known = rows[...]
        tall = jnp.concatenate([known, jnp.zeros((128 - known.shape[0], width), jnp.float32)], 0).T
        column = lax.broadcasted_iota(jnp.int32, (width, 128), 1)
        sums = edges[...]
        columns = jnp.where(column == 0, sums[:, :1], jnp.where(column == 1, sums[:, 2:3], tall))
        d_w[:, depth:] = columns.astype(d_w.dtype)


def input_weights(x, grads, rows, size):
    slots, width = x.shape
    depth = grads.shape[0]
    one = pl.Buffered(1)
    return pl.pallas_call(
        input_weights_kernel,
        grid=(depth // size,),
        in_specs=[
            pl.BlockSpec((slots, width), lambda i: (0, 0), pipeline_mode=one),
            pl.BlockSpec((size, slots), lambda i: (i, 0)),
            pl.BlockSpec(rows.shape, lambda i: (0, 0)),
        ],
        out_specs=pl.BlockSpec((width, depth + 128), lambda i: (0, 0)),
        out_shape=jax.ShapeDtypeStruct((width, depth + 128), jnp.bfloat16),
        scratch_shapes=[pltpu.VMEM((width, 128), jnp.float32)],
        compiler_params=pltpu.CompilerParams(vmem_limit_bytes=VMEM),
        cost_estimate=cost(12),
        name="input_weights",
    )(x, grads, rows)


def whole_body(
    tokens,
    lengths,
    cotangent,
    w_query,
    b_query,
    w_key,
    w_value,
    b_value,
    w_out,
    b_out,
    gain_one,
    shift_one,
    w_up,
    b_up,
    w_down,
    b_down,
    gain_two,
    shift_two,
):
    count, block, width = tokens.shape
    slots = count * block
    wide = w_up.shape[1]
    rows = w_query.shape[0]
    axes = ("dp", "seq")
    me = lax.axis_index("seq")
    heads, size = H, HD
    scale = size ** (-0.5)
    times = wide // width

    vectors = [b_query, b_value, b_out, gain_one, shift_one, b_down, gain_two, shift_two, b_up]
    vec = jnp.concatenate(vectors).reshape(8 + times, rows)
    vec = contract(vec, jnp.eye(8 + times, 128, dtype=jnp.bfloat16), 0, 0).astype(jnp.bfloat16)
    first = jnp.concatenate([w_query, w_key, w_value, vec], 1)
    first = lax.all_gather(first, "seq", axis=0, tiled=True)
    first = lax.all_gather(first, "dp", axis=0, tiled=True)
    owners = width // rows
    mixed_up = w_up.reshape(rows, owners, times, rows).transpose(0, 2, 1, 3).reshape(rows, wide)
    downs = [w_down[i * rows : (i + 1) * rows] for i in range(times)]
    second = jnp.concatenate([mixed_up] + downs + [w_out], 1)

    pieces = to_own(tokens)
    second, first, pieces = lax.optimization_barrier((second, first, pieces))
    second = lax.all_gather(second, axes, axis=0, tiled=True)
    length = take(lengths, me)
    order = me ^ jnp.arange(count, dtype=jnp.int32)
    place = (order[:, None] * block + jnp.arange(block, dtype=jnp.int32)[None, :]).reshape(slots)
    live = place < length
    bias = jnp.where(live, 0.0, -1e30).astype(jnp.bfloat16)
    bias = jnp.pad(bias[None, :], ((0, PAD - 1), (0, 0)))
    live = live[:, None].astype(jnp.float32)

    vec = first[:, 3 * width :].T[: 8 + times].astype(jnp.float32)
    bu = vec[8:].reshape(1, wide)
    vec = vec[:8]

    def by_head(array):
        return array.reshape(heads, size, slots)

    x, qt, kt, vt = project(pieces, first, vec)
    qt, cotangent = lax.optimization_barrier((qt, cotangent))
    cot = jnp.concatenate(to_own(cotangent), 0)
    qt, kt, vt = (by_head(a) for a in (qt, kt, vt))
    mt, total, probs = mix(me.reshape(1), qt, kt, vt, bias, scale * LOG2E, block)
    result, grad_one, gt, left, right, sums, up_sums = feed(
        x, mt.reshape(width, slots), cot, live, vec, bu, second, block
    )
    late = feed_weights(left, right, width)
    gt, late = lax.optimization_barrier((gt, late))
    late = lax.psum_scatter(late, "dp", scatter_dimension=0, tiled=True)
    output = to_split(result)
    grads = unmix(probs, qt, kt, vt, by_head(gt), mt, total, scale)
    grads, output, late = lax.optimization_barrier((grads, output, late))
    output = placed(output, jnp.bfloat16)
    grads = grads.reshape(3 * width, slots)
    edges = jnp.concatenate(
        [jnp.zeros((2, width), jnp.float32), sums[:6], up_sums.reshape(times, width)], 0
    )
    late = scattered(late)
    early = input_weights(x, grads, edges, width // 2)
    early, late, grads = lax.optimization_barrier((early, late, grads))
    early = lax.psum_scatter(early, "dp", scatter_dimension=0, tiled=True)
    low = inputs(grads, first, grad_one, block)
    grad_tokens = to_split(low)
    early, grad_tokens = lax.optimization_barrier((early, grad_tokens))
    early = scattered(early)
    grad_tokens = placed(grad_tokens, jnp.float32)
    o_wq, o_wk, o_wv = (early[:, i * width : (i + 1) * width] for i in range(3))
    vec = early[:, 3 * width :]
    o_wu = late[:, :wide].reshape(rows, times, owners, rows).transpose(0, 2, 1, 3).reshape(rows, wide)
    o_wd = jnp.concatenate(
        [late[:, wide + i * width : wide + (i + 1) * width] for i in range(times)], 0
    )
    o_wo = late[:, 2 * wide :]
    o_bq, o_bv, o_bo, o_g1, o_s1, o_bd, o_g2, o_s2 = (vec[:, i] for i in range(8))
    o_bu = vec[:, 8 : 8 + times].T.reshape(rows * times)
    return (
        output,
        grad_tokens,
        o_wq,
        o_bq,
        o_wk,
        o_wv,
        o_bv,
        o_wo,
        o_bo,
        o_g1,
        o_s1,
        o_wu,
        o_bu,
        o_wd,
        o_bd,
        o_g2,
        o_s2,
    )


def body(*arrays):
    count = arrays[0].shape[0]
    fits = count == lax.axis_size("seq") and count & (count - 1) == 0
    return whole_body(*arrays) if fits else general_body(*arrays)


def solution(mesh):
    in_specs = (
        P("dp", "seq", None),
        P("dp"),
        P("dp", "seq", None),
        P(("dp", "seq"), None),
        P(("dp", "seq")),
        P(("dp", "seq"), None),
        P(("dp", "seq"), None),
        P(("dp", "seq")),
        P(("dp", "seq"), None),
        P(("dp", "seq")),
        P(("dp", "seq")),
        P(("dp", "seq")),
        P(("dp", "seq"), None),
        P(("dp", "seq")),
        P(("dp", "seq"), None),
        P(("dp", "seq")),
        P(("dp", "seq")),
        P(("dp", "seq")),
    )
    out_specs = (
        P("dp", "seq", None),
        P("dp", "seq", None),
        P(("dp", "seq"), None),
        P(("dp", "seq")),
        P(("dp", "seq"), None),
        P(("dp", "seq"), None),
        P(("dp", "seq")),
        P(("dp", "seq"), None),
        P(("dp", "seq")),
        P(("dp", "seq")),
        P(("dp", "seq")),
        P(("dp", "seq"), None),
        P(("dp", "seq")),
        P(("dp", "seq"), None),
        P(("dp", "seq")),
        P(("dp", "seq")),
        P(("dp", "seq")),
    )
    return jax.shard_map(body, mesh=mesh, in_specs=in_specs, out_specs=out_specs, check_vma=False)
```

```python
import functools

import jax
import jax.numpy as jnp
from jax import lax
from jax.experimental import pallas as pl
from jax.experimental.pallas import tpu as pltpu
from jax.sharding import PartitionSpec as P

H = 12
HD = 64
MB = 4


epsilon = 1e-06


def layer_norm(layer_input_rows, norm_gain, norm_shift):
    centre = layer_input_rows - jnp.mean(layer_input_rows, -1, keepdims=True)
    spread = jnp.mean(centre * centre, -1, keepdims=True)
    return centre * lax.rsqrt(spread + epsilon) * norm_gain + norm_shift


def gelu_exact(values):
    return jax.nn.gelu(values, approximate=False)


def matmul(former, latter):
    return jnp.dot(former, latter, preferred_element_type=jnp.float32)


def former_product(former, latter):
    return lax.dot_general(
        former, latter, (((0,), (0,)), ((), ())), preferred_element_type=jnp.float32
    )


def latter_product(former, latter):
    return lax.dot_general(
        former, latter, (((1,), (1,)), ((), ())), preferred_element_type=jnp.float32
    )


def widen(vector):
    return vector.astype(jnp.float32)


def general_body(
    tokens,
    lengths,
    cotangent,
    w_query,
    b_query,
    w_key,
    w_value,
    b_value,
    w_out,
    b_out,
    gain_one,
    shift_one,
    w_up,
    b_up,
    w_down,
    b_down,
    gain_two,
    shift_two,
):
    shards = (
        w_query,
        b_query,
        w_key,
        w_value,
        b_value,
        w_out,
        b_out,
        gain_one,
        shift_one,
        w_up,
        b_up,
        w_down,
        b_down,
        gain_two,
        shift_two,
    )
    per_batch = tokens.shape[0] // MB
    block_rows = tokens.shape[1]
    model_width = tokens.shape[2]
    head_count = H
    head_size = HD
    flat_rows = per_batch * block_rows
    full_length = block_rows * lax.axis_size("seq")
    offset = lax.axis_index("seq") * block_rows
    positions = jnp.arange(full_length, dtype=jnp.int32)
    own_positions = offset + jnp.arange(block_rows, dtype=jnp.int32)
    score_scale = head_size ** (-0.5)
    owners = lax.axis_size(("dp", "seq"))
    totals = [
        jnp.zeros((shard_piece.shape[0] * owners,) + shard_piece.shape[1:], jnp.float32)
        for shard_piece in shards
    ]
    outputs = []
    input_grads = []
    for micro_batch in range(MB):
        leading_row = micro_batch * per_batch
        own_tokens = tokens[leading_row : leading_row + per_batch]
        own_lengths = lengths[leading_row : leading_row + per_batch]
        own_cots = cotangent[leading_row : leading_row + per_batch]
        fore_weights = (
            lax.all_gather(shards[0], ("dp", "seq"), axis=0, tiled=True),
            lax.all_gather(shards[1], ("dp", "seq"), axis=0, tiled=True),
            lax.all_gather(shards[2], ("dp", "seq"), axis=0, tiled=True),
            lax.all_gather(shards[3], ("dp", "seq"), axis=0, tiled=True),
            lax.all_gather(shards[4], ("dp", "seq"), axis=0, tiled=True),
            lax.all_gather(shards[5], ("dp", "seq"), axis=0, tiled=True),
            lax.all_gather(shards[6], ("dp", "seq"), axis=0, tiled=True),
            lax.all_gather(shards[7], ("dp", "seq"), axis=0, tiled=True),
            lax.all_gather(shards[8], ("dp", "seq"), axis=0, tiled=True),
            lax.all_gather(shards[9], ("dp", "seq"), axis=0, tiled=True),
            lax.all_gather(shards[10], ("dp", "seq"), axis=0, tiled=True),
            lax.all_gather(shards[11], ("dp", "seq"), axis=0, tiled=True),
            lax.all_gather(shards[12], ("dp", "seq"), axis=0, tiled=True),
            lax.all_gather(shards[13], ("dp", "seq"), axis=0, tiled=True),
            lax.all_gather(shards[14], ("dp", "seq"), axis=0, tiled=True),
        )
        flat_tokens = own_tokens.reshape(flat_rows, model_width)
        query_low = (matmul(flat_tokens, fore_weights[0]) + widen(fore_weights[1])).astype(
            jnp.bfloat16
        )
        key_low = matmul(flat_tokens, fore_weights[2]).astype(jnp.bfloat16)
        value_low = (matmul(flat_tokens, fore_weights[3]) + widen(fore_weights[4])).astype(
            jnp.bfloat16
        )
        key_block = key_low.reshape(per_batch, block_rows, model_width)
        value_block = value_low.reshape(per_batch, block_rows, model_width)
        gathered_keys, gathered_values = (
            lax.all_gather(key_block, "seq", axis=1, tiled=True),
            lax.all_gather(value_block, "seq", axis=1, tiled=True),
        )
        query_heads = query_low.reshape(per_batch, block_rows, head_count, head_size)
        visible = (positions[None, :] < own_lengths[:, None])[:, None, None, :]

        def score_block(key_all):
            key_heads = key_all.reshape(per_batch, full_length, head_count, head_size)
            raw_scores = jnp.einsum(
                "pqhd,pkhd->phqk", query_heads, key_heads, preferred_element_type=jnp.float32
            )
            return jnp.where(visible, raw_scores * score_scale, -1e30)

        scores = score_block(gathered_keys)
        logarithm_totals = jax.nn.logsumexp(scores, axis=-1, keepdims=True)
        chances_low = jnp.exp(scores - logarithm_totals).astype(jnp.bfloat16)
        value_heads = gathered_values.reshape(per_batch, full_length, head_count, head_size)
        mixed_heads = jnp.einsum(
            "phqk,pkhd->pqhd", chances_low, value_heads, preferred_element_type=jnp.float32
        )
        mixed_low = mixed_heads.reshape(flat_rows, model_width).astype(jnp.bfloat16)
        branch = matmul(mixed_low, fore_weights[5]) + widen(fore_weights[6])
        resid_one = flat_tokens.astype(jnp.float32) + branch
        normed = layer_norm(resid_one, widen(fore_weights[7]), widen(fore_weights[8]))
        normed_low = normed.astype(jnp.bfloat16)
        hidden = matmul(normed_low, fore_weights[9]) + widen(fore_weights[10])
        active_low = gelu_exact(hidden).astype(jnp.bfloat16)
        feed_out = matmul(active_low, fore_weights[11]) + widen(fore_weights[12])
        resid_two = normed + feed_out
        result = layer_norm(resid_two, widen(fore_weights[13]), widen(fore_weights[14]))
        outputs.append(result.astype(jnp.bfloat16).reshape(per_batch, block_rows, model_width))
        back_weights = (
            lax.all_gather(shards[0], ("dp", "seq"), axis=0, tiled=True),
            lax.all_gather(shards[1], ("dp", "seq"), axis=0, tiled=True),
            lax.all_gather(shards[2], ("dp", "seq"), axis=0, tiled=True),
            lax.all_gather(shards[3], ("dp", "seq"), axis=0, tiled=True),
            lax.all_gather(shards[4], ("dp", "seq"), axis=0, tiled=True),
            lax.all_gather(shards[5], ("dp", "seq"), axis=0, tiled=True),
            lax.all_gather(shards[6], ("dp", "seq"), axis=0, tiled=True),
            lax.all_gather(shards[7], ("dp", "seq"), axis=0, tiled=True),
            lax.all_gather(shards[8], ("dp", "seq"), axis=0, tiled=True),
            lax.all_gather(shards[9], ("dp", "seq"), axis=0, tiled=True),
            lax.all_gather(shards[10], ("dp", "seq"), axis=0, tiled=True),
            lax.all_gather(shards[11], ("dp", "seq"), axis=0, tiled=True),
            lax.all_gather(shards[12], ("dp", "seq"), axis=0, tiled=True),
            lax.all_gather(shards[13], ("dp", "seq"), axis=0, tiled=True),
            lax.all_gather(shards[14], ("dp", "seq"), axis=0, tiled=True),
        )
        live_rows = (
            (own_positions[None, :] < own_lengths[:, None])
            .astype(jnp.float32)
            .reshape(flat_rows, 1)
        )
        incoming = own_cots.reshape(flat_rows, model_width).astype(jnp.float32) * live_rows
        _, second_pull = jax.vjp(
            layer_norm, resid_two, widen(back_weights[13]), widen(back_weights[14])
        )
        grad_two, grad_gain_two, grad_shift_two = second_pull(incoming)
        feed_low = grad_two.astype(jnp.bfloat16)
        totals[11] = totals[11] + former_product(active_low, feed_low)
        totals[12] = totals[12] + jnp.sum(feed_low.astype(jnp.float32), 0)
        grad_active = latter_product(feed_low, back_weights[11])
        _, gelu_pull = jax.vjp(gelu_exact, hidden)
        up_low = gelu_pull(grad_active)[0].astype(jnp.bfloat16)
        totals[9] = totals[9] + former_product(normed_low, up_low)
        totals[10] = totals[10] + jnp.sum(up_low.astype(jnp.float32), 0)
        grad_normed = latter_product(up_low, back_weights[9]) + grad_two
        _, first_pull = jax.vjp(
            layer_norm, resid_one, widen(back_weights[7]), widen(back_weights[8])
        )
        grad_one, grad_gain_one, grad_shift_one = first_pull(grad_normed)
        branch_low = grad_one.astype(jnp.bfloat16)
        totals[5] = totals[5] + former_product(mixed_low, branch_low)
        totals[6] = totals[6] + jnp.sum(branch_low.astype(jnp.float32), 0)
        dmix_low = latter_product(branch_low, back_weights[5]).astype(jnp.bfloat16)
        dmix_heads = dmix_low.reshape(per_batch, block_rows, head_count, head_size)
        back_keys, backward_value_rows = (gathered_keys, gathered_values)
        chances = jnp.exp(score_block(back_keys) - logarithm_totals)
        back_value_heads = backward_value_rows.reshape(
            per_batch, full_length, head_count, head_size
        )
        back_key_heads = back_keys.reshape(per_batch, full_length, head_count, head_size)
        grad_chances = jnp.einsum(
            "pqhd,pkhd->phqk", dmix_heads, back_value_heads, preferred_element_type=jnp.float32
        )
        row_inner = jnp.sum(grad_chances * chances, -1, keepdims=True)
        dscore_low = (score_scale * (chances * (grad_chances - row_inner))).astype(jnp.bfloat16)
        dquery_low = jnp.einsum(
            "phqk,pkhd->pqhd", dscore_low, back_key_heads, preferred_element_type=jnp.float32
        )
        dquery_low = dquery_low.reshape(flat_rows, model_width).astype(jnp.bfloat16)
        chance_low = chances.astype(jnp.bfloat16)
        value_terms = jnp.einsum(
            "phqk,pqhd->pkhd", chance_low, dmix_heads, preferred_element_type=jnp.float32
        )
        key_terms = jnp.einsum(
            "phqk,pqhd->pkhd", dscore_low, query_heads, preferred_element_type=jnp.float32
        )
        key_sums, value_sums = (
            lax.psum_scatter(
                key_terms.reshape(per_batch, full_length, model_width).astype(jnp.bfloat16),
                "seq",
                scatter_dimension=1,
                tiled=True,
            ).astype(jnp.float32),
            lax.psum_scatter(
                value_terms.reshape(per_batch, full_length, model_width).astype(jnp.bfloat16),
                "seq",
                scatter_dimension=1,
                tiled=True,
            ).astype(jnp.float32),
        )
        dkey_low = key_sums.reshape(flat_rows, model_width).astype(jnp.bfloat16)
        dvalue_low = value_sums.reshape(flat_rows, model_width).astype(jnp.bfloat16)
        totals[0] = totals[0] + former_product(flat_tokens, dquery_low)
        totals[1] = totals[1] + jnp.sum(dquery_low.astype(jnp.float32), 0)
        totals[2] = totals[2] + former_product(flat_tokens, dkey_low)
        totals[3] = totals[3] + former_product(flat_tokens, dvalue_low)
        totals[4] = totals[4] + jnp.sum(dvalue_low.astype(jnp.float32), 0)
        totals[7] = totals[7] + grad_gain_one
        totals[8] = totals[8] + grad_shift_one
        totals[13] = totals[13] + grad_gain_two
        totals[14] = totals[14] + grad_shift_two
        grad_input = (
            latter_product(dquery_low, back_weights[0])
            + latter_product(dkey_low, back_weights[2])
            + latter_product(dvalue_low, back_weights[3])
            + grad_one
        )
        input_grads.append(grad_input.reshape(per_batch, block_rows, model_width))
    owned = lax.psum_scatter(tuple(totals), ("dp", "seq"), scatter_dimension=0, tiled=True)
    output = jnp.concatenate(outputs, 0)
    grad_tokens = jnp.concatenate(input_grads, 0)
    return (
        output,
        grad_tokens,
        owned[0],
        owned[1],
        owned[2],
        owned[3],
        owned[4],
        owned[5],
        owned[6],
        owned[7],
        owned[8],
        owned[9],
        owned[10],
        owned[11],
        owned[12],
        owned[13],
        owned[14],
    )


LOG2E = 1.4426950408889634
PAD = 16
VMEM = 60 << 20
RATE = 1e9


def cost(microseconds):
    return pl.CostEstimate(flops=int(microseconds * RATE), bytes_accessed=0, transcendentals=0)


def contract(former, latter, dim_former, dim_latter):
    return lax.dot_general(
        former,
        latter,
        (((dim_former,), (dim_latter,)), ((), ())),
        preferred_element_type=jnp.float32,
    )


def mix_kernel(scale, chunk, qt, kt, vt, bias, mixed, total, probs, keys, vals):
    size, slots = kt.shape[1], kt.shape[2]
    places = [slice(at, at + chunk) for at in range(0, slots, chunk)]
    key = kt[0]
    keys[...] = jnp.concatenate([key, key, bias[...]], 0).T
    vals[...] = jnp.concatenate([vt[0], jnp.ones((PAD, slots), jnp.bfloat16)], 0)
    query = qt[0].astype(jnp.float32) * scale
    high = query.astype(jnp.bfloat16)
    low = (query - high.astype(jnp.float32)).astype(jnp.bfloat16)
    row = lax.broadcasted_iota(jnp.int32, (PAD, slots), 0)
    first = jnp.where(row == 0, 1.0, 0.0).astype(jnp.bfloat16)
    columns = jnp.concatenate([high, low, first], 0)

    def finish(sums):
        weight = sums[size : size + 1]
        mixed[0] = (sums[:size] / weight).astype(mixed.dtype)
        total[0] = weight
        return weight

    sums, top = None, None
    for at in places:
        scores = contract(keys[at], columns, 1, 0)
        if top is None:
            top = jnp.max(scores[: chunk // 2], 0, keepdims=True)
        part = jnp.exp2(scores - top).astype(jnp.bfloat16)
        probs[0, at] = part
        term = contract(vals[:, at], part, 1, 0)
        sums = term if sums is None else sums + term
    weight = finish(sums)

    @pl.when(jnp.logical_not(jnp.max(weight) < 2.0**60))
    def _():
        top = jnp.full((1, slots), -jnp.inf, jnp.float32)
        for at in places:
            scores = contract(keys[at], columns, 1, 0)
            top = jnp.maximum(top, jnp.max(scores, 0, keepdims=True))
        sums = None
        for at in places:
            scores = contract(keys[at], columns, 1, 0)
            part = jnp.exp2(scores - top).astype(jnp.bfloat16)
            probs[0, at] = part
            term = contract(vals[:, at], part, 1, 0)
            sums = term if sums is None else sums + term
        finish(sums)


def mix(qt, kt, vt, bias, scale, chunk):
    heads, size, slots = qt.shape
    whole = pl.BlockSpec((1, size, slots), lambda i: (i, 0, 0))
    return pl.pallas_call(
        functools.partial(mix_kernel, scale, chunk),
        grid=(heads,),
        in_specs=[
            whole,
            whole,
            whole,
            pl.BlockSpec((PAD, slots), lambda i: (0, 0)),
        ],
        out_specs=[
            whole,
            pl.BlockSpec((1, 1, slots), lambda i: (i, 0, 0)),
            pl.BlockSpec((1, slots, slots), lambda i: (i, 0, 0)),
        ],
        out_shape=[
            jax.ShapeDtypeStruct((heads, size, slots), jnp.bfloat16),
            jax.ShapeDtypeStruct((heads, 1, slots), jnp.float32),
            jax.ShapeDtypeStruct((heads, slots, slots), jnp.bfloat16),
        ],
        scratch_shapes=[
            pltpu.VMEM((slots, 2 * size + PAD), jnp.bfloat16),
            pltpu.VMEM((size + PAD, slots), jnp.bfloat16),
        ],
        compiler_params=pltpu.CompilerParams(vmem_limit_bytes=VMEM),
        cost_estimate=cost(57),
        name="mix",
    )(qt, kt, vt, bias)


def unmix_kernel(scale, probs, qt, kt, vt, gt, mt, total, out, grads, inner, sums):
    step, last = pl.program_id(1), pl.num_programs(1) - 1
    keys = kt.shape[2]
    here = pl.ds(pl.multiple_of(step * keys, keys), keys)

    @pl.when(step == 0)
    def _():
        scaled = (gt[0].astype(jnp.float32) / total[0]).astype(jnp.bfloat16)
        grads[...] = scaled
        inner[...] = jnp.sum(
            scaled.astype(jnp.float32) * mt[0].astype(jnp.float32), 0, keepdims=True
        )

    grad = grads[...]
    prob = probs[0]
    dprob = contract(vt[0], grad, 0, 0)
    dscore = (prob.astype(jnp.float32) * (dprob - inner[...])).astype(jnp.bfloat16)
    part = contract(kt[0], dscore, 1, 0)
    out[2, 0, :, here] = contract(prob, grad, 1, 1).T.astype(jnp.bfloat16)
    out[1, 0, :, here] = (contract(dscore, qt[0], 1, 1) * scale).T.astype(jnp.bfloat16)

    @pl.when(step == 0)
    def _():
        sums[...] = part

    @pl.when(step > 0)
    def _():
        sums[...] += part

    @pl.when(step == last)
    def _():
        out[0, 0] = (sums[...] * scale).astype(jnp.bfloat16)


def unmix(probs, qt, kt, vt, gt, mt, total, scale):
    heads, size, slots = qt.shape
    keys = slots // 2
    whole = pl.BlockSpec((1, size, slots), lambda i, j: (i, 0, 0))
    part = pl.BlockSpec((1, size, keys), lambda i, j: (i, 0, j))
    return pl.pallas_call(
        functools.partial(unmix_kernel, scale),
        grid=(heads, slots // keys),
        in_specs=[
            pl.BlockSpec((1, keys, slots), lambda i, j: (i, j, 0)),
            whole,
            part,
            part,
            whole,
            whole,
            pl.BlockSpec((1, 1, slots), lambda i, j: (i, 0, 0)),
        ],
        out_specs=pl.BlockSpec((3, 1, size, slots), lambda i, j: (0, i, 0, 0)),
        out_shape=jax.ShapeDtypeStruct((3, heads, size, slots), jnp.bfloat16),
        scratch_shapes=[
            pltpu.VMEM((size, slots), jnp.bfloat16),
            pltpu.VMEM((1, slots), jnp.float32),
            pltpu.VMEM((size, slots), jnp.float32),
        ],
        compiler_params=pltpu.CompilerParams(vmem_limit_bytes=VMEM),
        cost_estimate=cost(110),
        name="unmix",
    )(probs, qt, kt, vt, gt, mt, total)


def exchange(blocks):
    return lax.all_to_all(blocks, "seq", 0, 0, tiled=True)


def take(array, index):
    return lax.dynamic_index_in_dim(array, index, 0, keepdims=False)


def columns(*vectors):
    rows = vectors[0].shape[0]
    stack = jnp.concatenate(vectors).reshape(-1, rows)
    unit = jnp.eye(stack.shape[0], 128, dtype=stack.dtype)
    return contract(stack, unit, 0, 0).astype(stack.dtype)


def scattered(rows):
    size = lax.axis_size("seq")
    parts = exchange(rows.reshape(size, rows.shape[0] // size, rows.shape[1]))
    return jnp.sum(parts.astype(jnp.float32), 0)


def row_sums(array):
    return jnp.sum(array, 0, keepdims=True)


def project_kernel(x, w, vec, qt, kt, vt):
    width = x.shape[1]
    bias = vec[...]
    outs = matmul(x[...], w[...])
    for i, out in enumerate((qt, kt, vt)):
        part = outs[:, i * width : (i + 1) * width]
        if i != 1:
            part = part + bias[i // 2 : i // 2 + 1]
        out[...] = part.astype(jnp.bfloat16).T


def project(x, first, vec, rows):
    slots, width = x.shape
    flat = pl.BlockSpec((width, rows), lambda i: (0, i))
    one = pl.Buffered(1)
    return pl.pallas_call(
        project_kernel,
        grid=(slots // rows,),
        in_specs=[
            pl.BlockSpec((rows, width), lambda i: (i, 0)),
            pl.BlockSpec((width, 3 * width), lambda i: (0, 0), pipeline_mode=one),
            pl.BlockSpec(vec.shape, lambda i: (0, 0)),
        ],
        out_specs=[flat] * 3,
        out_shape=[jax.ShapeDtypeStruct((width, slots), jnp.bfloat16)] * 3,
        compiler_params=pltpu.CompilerParams(vmem_limit_bytes=VMEM),
        cost_estimate=cost(11),
        name="project",
    )(x, first, vec)


def norm(rows):
    centre = rows - jnp.mean(rows, -1, keepdims=True)
    rstd = lax.rsqrt(jnp.mean(centre * centre, -1, keepdims=True) + epsilon)
    return centre * rstd, rstd


def norm_back(unit, rstd, grad):
    mean = jnp.mean(grad, -1, keepdims=True)
    inner = jnp.mean(grad * unit, -1, keepdims=True)
    return rstd * (grad - mean - unit * inner)


def feed_kernel(
    x, mt, cot, live, vec, bu, wo, wu, wd,
    output, grad_one, gt, left, right, sums, up_sums, slope,
):
    width = x.shape[1]
    wide = wu.shape[1]
    step = pl.program_id(0)
    bo, g1, s1, bd, g2, s2 = (vec[i : i + 1] for i in range(6))
    mixed = mt[...].T
    left[:, wide + width :] = mixed
    resid = x[...].astype(jnp.float32) + matmul(mixed, wo[...]) + bo
    unit_one, rstd_one = norm(resid)
    normed = unit_one * g1 + s1
    low = normed.astype(jnp.bfloat16)
    left[:, :width] = low
    resid = normed + bd
    for at in range(0, wide, width):
        cut = slice(at, at + width)
        hidden = matmul(low, wu[:, cut]) + bu[:, cut]
        share = 0.5 + 0.5 * lax.erf(hidden * 0.7071067811865476)
        bell = jnp.exp2(hidden * hidden * -0.7213475204444817) * 0.3989422804014327
        slope[:, cut] = (share + hidden * bell).astype(jnp.bfloat16)
        active = (hidden * share).astype(jnp.bfloat16)
        left[:, width + at : 2 * width + at] = active
        resid = resid + matmul(active, wd[:, cut])
    unit_two, rstd_two = norm(resid)
    output[...] = (unit_two * g2 + s2).astype(jnp.bfloat16)
    incoming = cot[...].astype(jnp.float32) * live[...]
    grad_two = norm_back(unit_two, rstd_two, incoming * g2)
    feed = grad_two.astype(jnp.bfloat16)
    right[:, wide : wide + width] = feed
    grad = grad_two
    up_rows = []
    for at in range(0, wide, width):
        cut = slice(at, at + width)
        part = contract(feed, wd[:, cut], 1, 1) * slope[:, cut].astype(jnp.float32)
        part = part.astype(jnp.bfloat16)
        right[:, cut] = part
        up_rows.append(row_sums(part.astype(jnp.float32)))
        grad = grad + contract(part, wu[:, cut], 1, 1)
    first = norm_back(unit_one, rstd_one, grad * g1)
    grad_one[...] = first
    branch = first.astype(jnp.bfloat16)
    right[:, wide + width :] = branch
    gt[...] = contract(wo[...], branch, 1, 1).astype(jnp.bfloat16)
    rows = [
        row_sums(branch.astype(jnp.float32)),
        row_sums(grad * unit_one),
        row_sums(grad),
        row_sums(feed.astype(jnp.float32)),
        row_sums(incoming * unit_two),
        row_sums(incoming),
    ]
    rows = jnp.concatenate(rows + [jnp.zeros((2, width), jnp.float32)], 0)
    wide_rows = jnp.concatenate(up_rows, 1)

    @pl.when(step == 0)
    def _():
        sums[...] = rows
        up_sums[...] = wide_rows

    @pl.when(step > 0)
    def _():
        sums[...] += rows
        up_sums[...] += wide_rows


def feed(x, mt, cot, live, vec, bu, second, rows):
    slots, width = x.shape
    wide = bu.shape[1]
    one = pl.Buffered(1)
    flat = pl.BlockSpec((rows, width), lambda i: (i, 0))
    tall = pl.BlockSpec((width, rows), lambda i: (0, i))
    stack = wide + 2 * width
    broad = pl.BlockSpec((rows, stack), lambda i: (i, 0))
    low = jnp.bfloat16
    return pl.pallas_call(
        feed_kernel,
        grid=(slots // rows,),
        in_specs=[
            flat,
            tall,
            flat,
            pl.BlockSpec((rows, 1), lambda i: (i, 0)),
            pl.BlockSpec(vec.shape, lambda i: (0, 0)),
            pl.BlockSpec((1, wide), lambda i: (0, 0)),
            pl.BlockSpec((width, width), lambda i: (0, 2 * wide // width), pipeline_mode=one),
            pl.BlockSpec((width, wide), lambda i: (0, 0), pipeline_mode=one),
            pl.BlockSpec((width, wide), lambda i: (0, 1), pipeline_mode=one),
        ],
        out_specs=[
            flat,
            flat,
            tall,
            broad,
            broad,
            pl.BlockSpec((8, width), lambda i: (0, 0)),
            pl.BlockSpec((1, wide), lambda i: (0, 0)),
        ],
        out_shape=[
            jax.ShapeDtypeStruct((slots, width), low),
            jax.ShapeDtypeStruct((slots, width), jnp.float32),
            jax.ShapeDtypeStruct((width, slots), low),
            jax.ShapeDtypeStruct((slots, stack), low),
            jax.ShapeDtypeStruct((slots, stack), low),
            jax.ShapeDtypeStruct((8, width), jnp.float32),
            jax.ShapeDtypeStruct((1, wide), jnp.float32),
        ],
        scratch_shapes=[pltpu.VMEM((rows, wide), low)],
        compiler_params=pltpu.CompilerParams(vmem_limit_bytes=VMEM),
        cost_estimate=cost(70),
        name="feed",
    )(x, mt, cot, live, vec, bu, second, second, second)


def feed_weights_kernel(left, right, d_w):
    d_w[...] = contract(left[...], right[...], 0, 0).astype(d_w.dtype)


def feed_weights(left, right, width):
    slots, stack = left.shape
    parts = stack // width - 2
    return pl.pallas_call(
        feed_weights_kernel,
        grid=(2 * parts + 1,),
        in_specs=[
            pl.BlockSpec((slots, width), lambda i: (0, jnp.maximum(i - parts + 1, 0))),
            pl.BlockSpec(
                (slots, width), lambda i: (0, jnp.minimum(i, parts) + i // (2 * parts))
            ),
        ],
        out_specs=pl.BlockSpec((width, width), lambda i: (0, i)),
        out_shape=jax.ShapeDtypeStruct((width, (2 * parts + 1) * width), jnp.bfloat16),
        compiler_params=pltpu.CompilerParams(vmem_limit_bytes=VMEM),
        cost_estimate=cost(26),
        name="feed_weights",
    )(left, right)


def inputs_kernel(grads, weights, grad_one, low):
    low[...] = (contract(grads[...], weights[...], 0, 1) + grad_one[...]).astype(low.dtype)


def inputs(grads, first, grad_one, rows):
    depth, slots = grads.shape
    width = first.shape[0]
    flat = pl.BlockSpec((rows, width), lambda i: (i, 0))
    return pl.pallas_call(
        inputs_kernel,
        grid=(slots // rows,),
        in_specs=[
            pl.BlockSpec((depth, rows), lambda i: (0, i)),
            pl.BlockSpec((width, depth), lambda i: (0, 0), pipeline_mode=pl.Buffered(1)),
            flat,
        ],
        out_specs=flat,
        out_shape=jax.ShapeDtypeStruct((slots, width), jnp.bfloat16),
        compiler_params=pltpu.CompilerParams(vmem_limit_bytes=VMEM),
        cost_estimate=cost(12),
        name="inputs",
    )(grads, first, grad_one)


def input_weights_kernel(x, grads, rows, d_w, edges):
    step, last = pl.program_id(0), pl.num_programs(0) - 1
    width = x.shape[1]
    depth = 3 * width
    size = grads.shape[0]
    grad = grads[...]
    product = contract(x[...], grad, 0, 1).astype(d_w.dtype)
    edge = jnp.sum(grad.astype(jnp.float32), 1, keepdims=True)
    for i in range(depth // size):

        @pl.when(step == i)
        def _(i=i):
            d_w[:, i * size : (i + 1) * size] = product
            column, top = i * size // width, i * size % width
            edges[top : top + size, column : column + 1] = edge

    @pl.when(step == last)
    def _():
        known = rows[...]
        tall = jnp.concatenate([known, jnp.zeros((128 - known.shape[0], width), jnp.float32)], 0).T
        column = lax.broadcasted_iota(jnp.int32, (width, 128), 1)
        sums = edges[...]
        columns = jnp.where(column == 0, sums[:, :1], jnp.where(column == 1, sums[:, 2:3], tall))
        d_w[:, depth:] = columns.astype(d_w.dtype)


def input_weights(x, grads, rows, size):
    slots, width = x.shape
    depth = grads.shape[0]
    one = pl.Buffered(1)
    return pl.pallas_call(
        input_weights_kernel,
        grid=(depth // size,),
        in_specs=[
            pl.BlockSpec((slots, width), lambda i: (0, 0), pipeline_mode=one),
            pl.BlockSpec((size, slots), lambda i: (i, 0)),
            pl.BlockSpec(rows.shape, lambda i: (0, 0)),
        ],
        out_specs=pl.BlockSpec((width, depth + 128), lambda i: (0, 0)),
        out_shape=jax.ShapeDtypeStruct((width, depth + 128), jnp.bfloat16),
        scratch_shapes=[pltpu.VMEM((width, 128), jnp.float32)],
        compiler_params=pltpu.CompilerParams(vmem_limit_bytes=VMEM),
        cost_estimate=cost(12),
        name="input_weights",
    )(x, grads, rows)


def whole_body(
    tokens,
    lengths,
    cotangent,
    w_query,
    b_query,
    w_key,
    w_value,
    b_value,
    w_out,
    b_out,
    gain_one,
    shift_one,
    w_up,
    b_up,
    w_down,
    b_down,
    gain_two,
    shift_two,
):
    count, block, width = tokens.shape
    slots = count * block
    wide = w_up.shape[1]
    rows = w_query.shape[0]
    axes = ("dp", "seq")
    me = lax.axis_index("seq")
    heads, size = H, HD
    scale = size ** (-0.5)
    times = wide // width

    x = exchange(tokens).reshape(slots, width)

    first = jnp.concatenate([w_query, w_key, w_value, columns(b_query, b_value)], 1)
    first = lax.all_gather(first, "seq", axis=0, tiled=True)
    first = lax.all_gather(first, "dp", axis=0, tiled=True)
    owners = width // rows
    mixed_up = w_up.reshape(rows, owners, times, rows).transpose(0, 2, 1, 3).reshape(rows, wide)
    downs = [w_down[i * rows : (i + 1) * rows] for i in range(times)]
    vectors = columns(b_out, gain_one, shift_one, b_down, gain_two, shift_two, b_up)
    second = jnp.concatenate([mixed_up] + downs + [w_out, vectors], 1)

    second, first, x = lax.optimization_barrier((second, first, x))
    second = lax.all_gather(second, axes, axis=0, tiled=True)
    length = take(lengths, me)
    live = jnp.arange(slots, dtype=jnp.int32) < length
    bias = jnp.where(live, 0.0, -1e30).astype(jnp.bfloat16)
    bias = jnp.pad(bias[None, :], ((0, PAD - 1), (0, 0)))
    live = live[:, None].astype(jnp.float32)

    def by_head(array):
        return array.reshape(heads, size, slots)

    qt, kt, vt = project(x, first, first[:, 3 * width :].T[:8].astype(jnp.float32), block)
    qt, cotangent = lax.optimization_barrier((qt, cotangent))
    cot = exchange(cotangent).reshape(slots, width)
    qt, kt, vt = (by_head(a) for a in (qt, kt, vt))
    mt, total, probs = mix(qt, kt, vt, bias, scale * LOG2E, block)
    vec = second[:, 2 * wide + width :].T[: 6 + times].astype(jnp.float32)
    bu = vec[6:].reshape(1, wide)
    result, grad_one, gt, left, right, sums, up_sums = feed(
        x, mt.reshape(width, slots), cot, live, vec[:6], bu, second, block
    )
    late = feed_weights(left, right, width)
    gt, late = lax.optimization_barrier((gt, late))
    late = lax.psum_scatter(late, "dp", scatter_dimension=0, tiled=True)
    output = exchange(result.reshape(count, block, width))
    grads = unmix(probs, qt, kt, vt, by_head(gt), mt, total, scale)
    grads, output, late = lax.optimization_barrier((grads, output, late))
    grads = grads.reshape(3 * width, slots)
    edges = jnp.concatenate(
        [jnp.zeros((2, width), jnp.float32), sums[:6], up_sums.reshape(times, width)], 0
    )
    late = scattered(late)
    early = input_weights(x, grads, edges, width)
    early, late, grads = lax.optimization_barrier((early, late, grads))
    early = lax.psum_scatter(early, "dp", scatter_dimension=0, tiled=True)
    low = inputs(grads, first, grad_one, block)
    grad_tokens = exchange(low.reshape(count, block, width)).astype(jnp.float32)
    early = scattered(early)
    o_wq, o_wk, o_wv = (early[:, i * width : (i + 1) * width] for i in range(3))
    vec = early[:, 3 * width :]
    o_wu = late[:, :wide].reshape(rows, times, owners, rows).transpose(0, 2, 1, 3).reshape(rows, wide)
    o_wd = jnp.concatenate(
        [late[:, wide + i * width : wide + (i + 1) * width] for i in range(times)], 0
    )
    o_wo = late[:, 2 * wide :]
    o_bq, o_bv, o_bo, o_g1, o_s1, o_bd, o_g2, o_s2 = (vec[:, i] for i in range(8))
    o_bu = vec[:, 8 : 8 + times].T.reshape(rows * times)
    return (
        output,
        grad_tokens,
        o_wq,
        o_bq,
        o_wk,
        o_wv,
        o_bv,
        o_wo,
        o_bo,
        o_g1,
        o_s1,
        o_wu,
        o_bu,
        o_wd,
        o_bd,
        o_g2,
        o_s2,
    )


def body(*arrays):
    count = arrays[0].shape[0]
    fits = count == lax.axis_size("seq") and count & (count - 1) == 0
    return whole_body(*arrays) if fits else general_body(*arrays)


def solution(mesh):
    in_specs = (
        P("dp", "seq", None),
        P("dp"),
        P("dp", "seq", None),
        P(("dp", "seq"), None),
        P(("dp", "seq")),
        P(("dp", "seq"), None),
        P(("dp", "seq"), None),
        P(("dp", "seq")),
        P(("dp", "seq"), None),
        P(("dp", "seq")),
        P(("dp", "seq")),
        P(("dp", "seq")),
        P(("dp", "seq"), None),
        P(("dp", "seq")),
        P(("dp", "seq"), None),
        P(("dp", "seq")),
        P(("dp", "seq")),
        P(("dp", "seq")),
    )
    out_specs = (
        P("dp", "seq", None),
        P("dp", "seq", None),
        P(("dp", "seq"), None),
        P(("dp", "seq")),
        P(("dp", "seq"), None),
        P(("dp", "seq"), None),
        P(("dp", "seq")),
        P(("dp", "seq"), None),
        P(("dp", "seq")),
        P(("dp", "seq")),
        P(("dp", "seq")),
        P(("dp", "seq"), None),
        P(("dp", "seq")),
        P(("dp", "seq"), None),
        P(("dp", "seq")),
        P(("dp", "seq")),
        P(("dp", "seq")),
    )
    return jax.shard_map(body, mesh=mesh, in_specs=in_specs, out_specs=out_specs, check_vma=False)
```

```python
import functools

import jax
import jax.numpy as jnp
from jax import lax
from jax.experimental import pallas as pl
from jax.experimental.pallas import tpu as pltpu
from jax.sharding import PartitionSpec as P

H = 12
HD = 64
MB = 4


epsilon = 1e-06


def layer_norm(layer_input_rows, norm_gain, norm_shift):
    centre = layer_input_rows - jnp.mean(layer_input_rows, -1, keepdims=True)
    spread = jnp.mean(centre * centre, -1, keepdims=True)
    return centre * lax.rsqrt(spread + epsilon) * norm_gain + norm_shift


def gelu_exact(values):
    return jax.nn.gelu(values, approximate=False)


def matmul(former, latter):
    return jnp.dot(former, latter, preferred_element_type=jnp.float32)


def former_product(former, latter):
    return lax.dot_general(
        former, latter, (((0,), (0,)), ((), ())), preferred_element_type=jnp.float32
    )


def latter_product(former, latter):
    return lax.dot_general(
        former, latter, (((1,), (1,)), ((), ())), preferred_element_type=jnp.float32
    )


def widen(vector):
    return vector.astype(jnp.float32)


def general_body(
    tokens,
    lengths,
    cotangent,
    w_query,
    b_query,
    w_key,
    w_value,
    b_value,
    w_out,
    b_out,
    gain_one,
    shift_one,
    w_up,
    b_up,
    w_down,
    b_down,
    gain_two,
    shift_two,
):
    shards = (
        w_query,
        b_query,
        w_key,
        w_value,
        b_value,
        w_out,
        b_out,
        gain_one,
        shift_one,
        w_up,
        b_up,
        w_down,
        b_down,
        gain_two,
        shift_two,
    )
    per_batch = tokens.shape[0] // MB
    block_rows = tokens.shape[1]
    model_width = tokens.shape[2]
    head_count = H
    head_size = HD
    flat_rows = per_batch * block_rows
    full_length = block_rows * lax.axis_size("seq")
    offset = lax.axis_index("seq") * block_rows
    positions = jnp.arange(full_length, dtype=jnp.int32)
    own_positions = offset + jnp.arange(block_rows, dtype=jnp.int32)
    score_scale = head_size ** (-0.5)
    owners = lax.axis_size(("dp", "seq"))
    totals = [
        jnp.zeros((shard_piece.shape[0] * owners,) + shard_piece.shape[1:], jnp.float32)
        for shard_piece in shards
    ]
    outputs = []
    input_grads = []
    for micro_batch in range(MB):
        leading_row = micro_batch * per_batch
        own_tokens = tokens[leading_row : leading_row + per_batch]
        own_lengths = lengths[leading_row : leading_row + per_batch]
        own_cots = cotangent[leading_row : leading_row + per_batch]
        fore_weights = (
            lax.all_gather(shards[0], ("dp", "seq"), axis=0, tiled=True),
            lax.all_gather(shards[1], ("dp", "seq"), axis=0, tiled=True),
            lax.all_gather(shards[2], ("dp", "seq"), axis=0, tiled=True),
            lax.all_gather(shards[3], ("dp", "seq"), axis=0, tiled=True),
            lax.all_gather(shards[4], ("dp", "seq"), axis=0, tiled=True),
            lax.all_gather(shards[5], ("dp", "seq"), axis=0, tiled=True),
            lax.all_gather(shards[6], ("dp", "seq"), axis=0, tiled=True),
            lax.all_gather(shards[7], ("dp", "seq"), axis=0, tiled=True),
            lax.all_gather(shards[8], ("dp", "seq"), axis=0, tiled=True),
            lax.all_gather(shards[9], ("dp", "seq"), axis=0, tiled=True),
            lax.all_gather(shards[10], ("dp", "seq"), axis=0, tiled=True),
            lax.all_gather(shards[11], ("dp", "seq"), axis=0, tiled=True),
            lax.all_gather(shards[12], ("dp", "seq"), axis=0, tiled=True),
            lax.all_gather(shards[13], ("dp", "seq"), axis=0, tiled=True),
            lax.all_gather(shards[14], ("dp", "seq"), axis=0, tiled=True),
        )
        flat_tokens = own_tokens.reshape(flat_rows, model_width)
        query_low = (matmul(flat_tokens, fore_weights[0]) + widen(fore_weights[1])).astype(
            jnp.bfloat16
        )
        key_low = matmul(flat_tokens, fore_weights[2]).astype(jnp.bfloat16)
        value_low = (matmul(flat_tokens, fore_weights[3]) + widen(fore_weights[4])).astype(
            jnp.bfloat16
        )
        key_block = key_low.reshape(per_batch, block_rows, model_width)
        value_block = value_low.reshape(per_batch, block_rows, model_width)
        gathered_keys, gathered_values = (
            lax.all_gather(key_block, "seq", axis=1, tiled=True),
            lax.all_gather(value_block, "seq", axis=1, tiled=True),
        )
        query_heads = query_low.reshape(per_batch, block_rows, head_count, head_size)
        visible = (positions[None, :] < own_lengths[:, None])[:, None, None, :]

        def score_block(key_all):
            key_heads = key_all.reshape(per_batch, full_length, head_count, head_size)
            raw_scores = jnp.einsum(
                "pqhd,pkhd->phqk", query_heads, key_heads, preferred_element_type=jnp.float32
            )
            return jnp.where(visible, raw_scores * score_scale, -1e30)

        scores = score_block(gathered_keys)
        logarithm_totals = jax.nn.logsumexp(scores, axis=-1, keepdims=True)
        chances_low = jnp.exp(scores - logarithm_totals).astype(jnp.bfloat16)
        value_heads = gathered_values.reshape(per_batch, full_length, head_count, head_size)
        mixed_heads = jnp.einsum(
            "phqk,pkhd->pqhd", chances_low, value_heads, preferred_element_type=jnp.float32
        )
        mixed_low = mixed_heads.reshape(flat_rows, model_width).astype(jnp.bfloat16)
        branch = matmul(mixed_low, fore_weights[5]) + widen(fore_weights[6])
        resid_one = flat_tokens.astype(jnp.float32) + branch
        normed = layer_norm(resid_one, widen(fore_weights[7]), widen(fore_weights[8]))
        normed_low = normed.astype(jnp.bfloat16)
        hidden = matmul(normed_low, fore_weights[9]) + widen(fore_weights[10])
        active_low = gelu_exact(hidden).astype(jnp.bfloat16)
        feed_out = matmul(active_low, fore_weights[11]) + widen(fore_weights[12])
        resid_two = normed + feed_out
        result = layer_norm(resid_two, widen(fore_weights[13]), widen(fore_weights[14]))
        outputs.append(result.astype(jnp.bfloat16).reshape(per_batch, block_rows, model_width))
        back_weights = (
            lax.all_gather(shards[0], ("dp", "seq"), axis=0, tiled=True),
            lax.all_gather(shards[1], ("dp", "seq"), axis=0, tiled=True),
            lax.all_gather(shards[2], ("dp", "seq"), axis=0, tiled=True),
            lax.all_gather(shards[3], ("dp", "seq"), axis=0, tiled=True),
            lax.all_gather(shards[4], ("dp", "seq"), axis=0, tiled=True),
            lax.all_gather(shards[5], ("dp", "seq"), axis=0, tiled=True),
            lax.all_gather(shards[6], ("dp", "seq"), axis=0, tiled=True),
            lax.all_gather(shards[7], ("dp", "seq"), axis=0, tiled=True),
            lax.all_gather(shards[8], ("dp", "seq"), axis=0, tiled=True),
            lax.all_gather(shards[9], ("dp", "seq"), axis=0, tiled=True),
            lax.all_gather(shards[10], ("dp", "seq"), axis=0, tiled=True),
            lax.all_gather(shards[11], ("dp", "seq"), axis=0, tiled=True),
            lax.all_gather(shards[12], ("dp", "seq"), axis=0, tiled=True),
            lax.all_gather(shards[13], ("dp", "seq"), axis=0, tiled=True),
            lax.all_gather(shards[14], ("dp", "seq"), axis=0, tiled=True),
        )
        live_rows = (
            (own_positions[None, :] < own_lengths[:, None])
            .astype(jnp.float32)
            .reshape(flat_rows, 1)
        )
        incoming = own_cots.reshape(flat_rows, model_width).astype(jnp.float32) * live_rows
        _, second_pull = jax.vjp(
            layer_norm, resid_two, widen(back_weights[13]), widen(back_weights[14])
        )
        grad_two, grad_gain_two, grad_shift_two = second_pull(incoming)
        feed_low = grad_two.astype(jnp.bfloat16)
        totals[11] = totals[11] + former_product(active_low, feed_low)
        totals[12] = totals[12] + jnp.sum(feed_low.astype(jnp.float32), 0)
        grad_active = latter_product(feed_low, back_weights[11])
        _, gelu_pull = jax.vjp(gelu_exact, hidden)
        up_low = gelu_pull(grad_active)[0].astype(jnp.bfloat16)
        totals[9] = totals[9] + former_product(normed_low, up_low)
        totals[10] = totals[10] + jnp.sum(up_low.astype(jnp.float32), 0)
        grad_normed = latter_product(up_low, back_weights[9]) + grad_two
        _, first_pull = jax.vjp(
            layer_norm, resid_one, widen(back_weights[7]), widen(back_weights[8])
        )
        grad_one, grad_gain_one, grad_shift_one = first_pull(grad_normed)
        branch_low = grad_one.astype(jnp.bfloat16)
        totals[5] = totals[5] + former_product(mixed_low, branch_low)
        totals[6] = totals[6] + jnp.sum(branch_low.astype(jnp.float32), 0)
        dmix_low = latter_product(branch_low, back_weights[5]).astype(jnp.bfloat16)
        dmix_heads = dmix_low.reshape(per_batch, block_rows, head_count, head_size)
        back_keys, backward_value_rows = (gathered_keys, gathered_values)
        chances = jnp.exp(score_block(back_keys) - logarithm_totals)
        back_value_heads = backward_value_rows.reshape(
            per_batch, full_length, head_count, head_size
        )
        back_key_heads = back_keys.reshape(per_batch, full_length, head_count, head_size)
        grad_chances = jnp.einsum(
            "pqhd,pkhd->phqk", dmix_heads, back_value_heads, preferred_element_type=jnp.float32
        )
        row_inner = jnp.sum(grad_chances * chances, -1, keepdims=True)
        dscore_low = (score_scale * (chances * (grad_chances - row_inner))).astype(jnp.bfloat16)
        dquery_low = jnp.einsum(
            "phqk,pkhd->pqhd", dscore_low, back_key_heads, preferred_element_type=jnp.float32
        )
        dquery_low = dquery_low.reshape(flat_rows, model_width).astype(jnp.bfloat16)
        chance_low = chances.astype(jnp.bfloat16)
        value_terms = jnp.einsum(
            "phqk,pqhd->pkhd", chance_low, dmix_heads, preferred_element_type=jnp.float32
        )
        key_terms = jnp.einsum(
            "phqk,pqhd->pkhd", dscore_low, query_heads, preferred_element_type=jnp.float32
        )
        key_sums, value_sums = (
            lax.psum_scatter(
                key_terms.reshape(per_batch, full_length, model_width).astype(jnp.bfloat16),
                "seq",
                scatter_dimension=1,
                tiled=True,
            ).astype(jnp.float32),
            lax.psum_scatter(
                value_terms.reshape(per_batch, full_length, model_width).astype(jnp.bfloat16),
                "seq",
                scatter_dimension=1,
                tiled=True,
            ).astype(jnp.float32),
        )
        dkey_low = key_sums.reshape(flat_rows, model_width).astype(jnp.bfloat16)
        dvalue_low = value_sums.reshape(flat_rows, model_width).astype(jnp.bfloat16)
        totals[0] = totals[0] + former_product(flat_tokens, dquery_low)
        totals[1] = totals[1] + jnp.sum(dquery_low.astype(jnp.float32), 0)
        totals[2] = totals[2] + former_product(flat_tokens, dkey_low)
        totals[3] = totals[3] + former_product(flat_tokens, dvalue_low)
        totals[4] = totals[4] + jnp.sum(dvalue_low.astype(jnp.float32), 0)
        totals[7] = totals[7] + grad_gain_one
        totals[8] = totals[8] + grad_shift_one
        totals[13] = totals[13] + grad_gain_two
        totals[14] = totals[14] + grad_shift_two
        grad_input = (
            latter_product(dquery_low, back_weights[0])
            + latter_product(dkey_low, back_weights[2])
            + latter_product(dvalue_low, back_weights[3])
            + grad_one
        )
        input_grads.append(grad_input.reshape(per_batch, block_rows, model_width))
    owned = lax.psum_scatter(tuple(totals), ("dp", "seq"), scatter_dimension=0, tiled=True)
    output = jnp.concatenate(outputs, 0)
    grad_tokens = jnp.concatenate(input_grads, 0)
    return (
        output,
        grad_tokens,
        owned[0],
        owned[1],
        owned[2],
        owned[3],
        owned[4],
        owned[5],
        owned[6],
        owned[7],
        owned[8],
        owned[9],
        owned[10],
        owned[11],
        owned[12],
        owned[13],
        owned[14],
    )


LOG2E = 1.4426950408889634
PAD = 16
VMEM = 60 << 20
RATE = 1e9


def cost(microseconds):
    return pl.CostEstimate(flops=int(microseconds * RATE), bytes_accessed=0, transcendentals=0)


def contract(former, latter, dim_former, dim_latter):
    return lax.dot_general(
        former,
        latter,
        (((dim_former,), (dim_latter,)), ((), ())),
        preferred_element_type=jnp.float32,
    )


def mix_kernel(scale, chunk, qt, kt, vt, bias, mixed, total, probs, queries, vals):
    size, slots = kt.shape[1], kt.shape[2]
    query = qt[0].astype(jnp.float32) * scale
    high = query.astype(jnp.bfloat16)
    low = (query - high.astype(jnp.float32)).astype(jnp.bfloat16)
    row = lax.broadcasted_iota(jnp.int32, (PAD, slots), 0)
    first = jnp.where(row == 0, 1.0, 0.0).astype(jnp.bfloat16)
    queries[...] = jnp.concatenate([high, low, first], 0).T
    keys = jnp.concatenate([kt[0], kt[0], bias[...]], 0)
    vals[...] = jnp.concatenate([vt[0], jnp.ones((PAD, slots), jnp.bfloat16)], 0).T

    def block(at, seen):
        cut = slice(at, at + chunk)
        scores = matmul(queries[cut], keys)
        top = jnp.max(scores[:, :seen], 1, keepdims=True)
        part = jnp.exp2(scores - top).astype(jnp.bfloat16)
        probs[0, cut] = part
        sums = matmul(part, vals[...]).T
        weight = sums[size : size + 1]
        mixed[0, :, cut] = (sums[:size] / weight).astype(mixed.dtype)
        total[0, :, cut] = weight
        return jnp.max(weight)

    largest = [block(at, 256) for at in range(0, slots, chunk)]

    @pl.when(jnp.logical_not(functools.reduce(jnp.maximum, largest) < 2.0**60))
    def _():
        for at in range(0, slots, chunk):
            block(at, slots)


def mix(qt, kt, vt, bias, scale):
    heads, size, slots = qt.shape
    whole = pl.BlockSpec((1, size, slots), lambda i: (i, 0, 0))
    return pl.pallas_call(
        functools.partial(mix_kernel, scale, 512),
        grid=(heads,),
        in_specs=[whole, whole, whole, pl.BlockSpec((PAD, slots), lambda i: (0, 0))],
        out_specs=[
            whole,
            pl.BlockSpec((1, 1, slots), lambda i: (i, 0, 0)),
            pl.BlockSpec((1, slots, slots), lambda i: (i, 0, 0)),
        ],
        out_shape=[
            jax.ShapeDtypeStruct((heads, size, slots), jnp.bfloat16),
            jax.ShapeDtypeStruct((heads, 1, slots), jnp.float32),
            jax.ShapeDtypeStruct((heads, slots, slots), jnp.bfloat16),
        ],
        scratch_shapes=[
            pltpu.VMEM((slots, 2 * size + PAD), jnp.bfloat16),
            pltpu.VMEM((slots, size + PAD), jnp.bfloat16),
        ],
        compiler_params=pltpu.CompilerParams(vmem_limit_bytes=VMEM),
        cost_estimate=cost(65),
        name="mix",
    )(qt, kt, vt, bias)


def unmix_kernel(scale, chunk, probs, qt, kt, vt, gt, mt, total, out, keys):
    slots = kt.shape[2]
    grad = (gt[0].astype(jnp.float32) / total[0]).astype(jnp.bfloat16)
    inner = jnp.sum(grad.astype(jnp.float32) * mt[0].astype(jnp.float32), 0, keepdims=True)
    inner = jnp.broadcast_to(inner, (8, slots)).T[:, :1]
    turned = grad.T
    keys[...] = kt[0].T
    dk = dv = None
    for at in range(0, slots, chunk):
        cut = slice(at, at + chunk)
        prob = probs[0, cut]
        dprob = matmul(turned[cut], vt[0])
        dscore = (prob.astype(jnp.float32) * (dprob - inner[cut])).astype(jnp.bfloat16)
        out[0, 0, :, cut] = (matmul(dscore, keys[...]) * scale).T.astype(jnp.bfloat16)
        value_term = matmul(grad[:, cut], prob)
        key_term = matmul(qt[0, :, cut], dscore)
        dv = value_term if dv is None else dv + value_term
        dk = key_term if dk is None else dk + key_term
    out[1, 0] = (dk * scale).astype(jnp.bfloat16)
    out[2, 0] = dv.astype(jnp.bfloat16)


def unmix(probs, qt, kt, vt, gt, mt, total, scale):
    heads, size, slots = qt.shape
    whole = pl.BlockSpec((1, size, slots), lambda i: (i, 0, 0))
    return pl.pallas_call(
        functools.partial(unmix_kernel, scale, 256),
        grid=(heads,),
        in_specs=[pl.BlockSpec((1, slots, slots), lambda i: (i, 0, 0))]
        + [whole] * 5
        + [pl.BlockSpec((1, 1, slots), lambda i: (i, 0, 0))],
        out_specs=pl.BlockSpec((3, 1, size, slots), lambda i: (0, i, 0, 0)),
        out_shape=jax.ShapeDtypeStruct((3, heads, size, slots), jnp.bfloat16),
        scratch_shapes=[pltpu.VMEM((slots, size), jnp.bfloat16)],
        compiler_params=pltpu.CompilerParams(vmem_limit_bytes=VMEM),
        cost_estimate=cost(95),
        name="unmix",
    )(probs, qt, kt, vt, gt, mt, total)


def exchange(blocks):
    return lax.all_to_all(blocks, "seq", 0, 0, tiled=True)


def take(array, index):
    return lax.dynamic_index_in_dim(array, index, 0, keepdims=False)


def columns(*vectors):
    rows = vectors[0].shape[0]
    stack = jnp.concatenate(vectors).reshape(-1, rows)
    unit = jnp.eye(stack.shape[0], 128, dtype=stack.dtype)
    return contract(stack, unit, 0, 0).astype(stack.dtype)


def scattered(rows):
    size = lax.axis_size("seq")
    parts = exchange(rows.reshape(size, rows.shape[0] // size, rows.shape[1]))
    return jnp.sum(parts.astype(jnp.float32), 0)


def row_sums(array):
    return jnp.sum(array, 0, keepdims=True)


def project_kernel(x, w, vec, qt, kt, vt):
    width = x.shape[1]
    bias = vec[...].T[:8].astype(jnp.float32)
    outs = matmul(x[...], w[...])
    for i, out in enumerate((qt, kt, vt)):
        part = outs[:, i * width : (i + 1) * width]
        if i != 1:
            part = part + bias[i // 2 : i // 2 + 1]
        out[...] = part.astype(jnp.bfloat16).T


def project(x, first, rows):
    slots, width = x.shape
    flat = pl.BlockSpec((width, rows), lambda i: (0, i))
    one = pl.Buffered(1)
    return pl.pallas_call(
        project_kernel,
        grid=(slots // rows,),
        in_specs=[
            pl.BlockSpec((rows, width), lambda i: (i, 0)),
            pl.BlockSpec((width, 3 * width), lambda i: (0, 0), pipeline_mode=one),
            pl.BlockSpec((width, 128), lambda i: (0, 3 * width // 128)),
        ],
        out_specs=[flat] * 3,
        out_shape=[jax.ShapeDtypeStruct((width, slots), jnp.bfloat16)] * 3,
        compiler_params=pltpu.CompilerParams(vmem_limit_bytes=VMEM),
        cost_estimate=cost(11),
        name="project",
    )(x, first, first)


def norm(rows):
    centre = rows - jnp.mean(rows, -1, keepdims=True)
    rstd = lax.rsqrt(jnp.mean(centre * centre, -1, keepdims=True) + epsilon)
    return centre * rstd, rstd


def norm_back(unit, rstd, grad):
    mean = jnp.mean(grad, -1, keepdims=True)
    inner = jnp.mean(grad * unit, -1, keepdims=True)
    return rstd * (grad - mean - unit * inner)


def feed_kernel(
    x, mt, cot, live, vec, wo, wu, wd, output, grad_one, gt, left, right, sums, slope,
):
    width = x.shape[1]
    wide = wu.shape[1]
    step = pl.program_id(0)
    known = vec[...].T[:16].astype(jnp.float32)
    bo, g1, s1, bd, g2, s2 = (known[i : i + 1] for i in range(6))
    mixed = mt[...].T
    left[:, wide + width :] = mixed
    resid = x[...].astype(jnp.float32) + matmul(mixed, wo[...]) + bo
    unit_one, rstd_one = norm(resid)
    normed = unit_one * g1 + s1
    low = normed.astype(jnp.bfloat16)
    left[:, :width] = low
    resid = normed + bd
    for at in range(0, wide, width):
        cut = slice(at, at + width)
        hidden = matmul(low, wu[:, cut]) + known[6 + at // width : 7 + at // width]
        share = 0.5 + 0.5 * lax.erf(hidden * 0.7071067811865476)
        bell = jnp.exp2(hidden * hidden * -0.7213475204444817) * 0.3989422804014327
        slope[:, cut] = (share + hidden * bell).astype(jnp.bfloat16)
        active = (hidden * share).astype(jnp.bfloat16)
        left[:, width + at : 2 * width + at] = active
        resid = resid + matmul(active, wd[:, cut])
    unit_two, rstd_two = norm(resid)
    output[...] = (unit_two * g2 + s2).astype(jnp.bfloat16)
    incoming = cot[...].astype(jnp.float32) * live[...]
    grad_two = norm_back(unit_two, rstd_two, incoming * g2)
    feed = grad_two.astype(jnp.bfloat16)
    right[:, wide : wide + width] = feed
    grad = grad_two
    up_rows = []
    for at in range(0, wide, width):
        cut = slice(at, at + width)
        part = contract(feed, wd[:, cut], 1, 1) * slope[:, cut].astype(jnp.float32)
        part = part.astype(jnp.bfloat16)
        right[:, cut] = part
        up_rows.append(row_sums(part.astype(jnp.float32)))
        grad = grad + contract(part, wu[:, cut], 1, 1)
    first = norm_back(unit_one, rstd_one, grad * g1)
    grad_one[...] = first
    branch = first.astype(jnp.bfloat16)
    right[:, wide + width :] = branch
    gt[...] = contract(wo[...], branch, 1, 1).astype(jnp.bfloat16)
    rows = [
        row_sums(branch.astype(jnp.float32)),
        row_sums(grad * unit_one),
        row_sums(grad),
        row_sums(feed.astype(jnp.float32)),
        row_sums(incoming * unit_two),
        row_sums(incoming),
    ]
    blank = [jnp.zeros((2, width), jnp.float32)]
    rows = jnp.concatenate(blank + rows + up_rows, 0)

    @pl.when(step == 0)
    def _():
        sums[...] = rows

    @pl.when(step > 0)
    def _():
        sums[...] += rows


def feed(x, mt, cot, live, second, wide, rows):
    slots, width = x.shape
    one = pl.Buffered(1)
    flat = pl.BlockSpec((rows, width), lambda i: (i, 0))
    tall = pl.BlockSpec((width, rows), lambda i: (0, i))
    stack = wide + 2 * width
    broad = pl.BlockSpec((rows, stack), lambda i: (i, 0))
    low = jnp.bfloat16
    return pl.pallas_call(
        feed_kernel,
        grid=(slots // rows,),
        in_specs=[
            flat,
            tall,
            flat,
            pl.BlockSpec((rows, 1), lambda i: (i, 0)),
            pl.BlockSpec((width, 128), lambda i: (0, (2 * wide + width) // 128)),
            pl.BlockSpec((width, width), lambda i: (0, 2 * wide // width), pipeline_mode=one),
            pl.BlockSpec((width, wide), lambda i: (0, 0), pipeline_mode=one),
            pl.BlockSpec((width, wide), lambda i: (0, 1), pipeline_mode=one),
        ],
        out_specs=[
            flat,
            flat,
            tall,
            broad,
            broad,
            pl.BlockSpec((8 + wide // width, width), lambda i: (0, 0)),
        ],
        out_shape=[
            jax.ShapeDtypeStruct((slots, width), low),
            jax.ShapeDtypeStruct((slots, width), jnp.float32),
            jax.ShapeDtypeStruct((width, slots), low),
            jax.ShapeDtypeStruct((slots, stack), low),
            jax.ShapeDtypeStruct((slots, stack), low),
            jax.ShapeDtypeStruct((8 + wide // width, width), jnp.float32),
        ],
        scratch_shapes=[pltpu.VMEM((rows, wide), low)],
        compiler_params=pltpu.CompilerParams(vmem_limit_bytes=VMEM),
        cost_estimate=cost(70),
        name="feed",
    )(x, mt, cot, live, second, second, second, second)


def feed_weights_kernel(left, right, d_w):
    d_w[...] = contract(left[...], right[...], 0, 0).astype(d_w.dtype)


def feed_weights(left, right, width):
    slots, stack = left.shape
    parts = stack // width - 2
    return pl.pallas_call(
        feed_weights_kernel,
        grid=(2 * parts + 1,),
        in_specs=[
            pl.BlockSpec((slots, width), lambda i: (0, jnp.maximum(i - parts + 1, 0))),
            pl.BlockSpec(
                (slots, width), lambda i: (0, jnp.minimum(i, parts) + i // (2 * parts))
            ),
        ],
        out_specs=pl.BlockSpec((width, width), lambda i: (0, i)),
        out_shape=jax.ShapeDtypeStruct((width, (2 * parts + 1) * width), jnp.bfloat16),
        compiler_params=pltpu.CompilerParams(vmem_limit_bytes=VMEM),
        cost_estimate=cost(26),
        name="feed_weights",
    )(left, right)


def inputs_kernel(grads, weights, grad_one, low):
    low[...] = (contract(grads[...], weights[...], 0, 1) + grad_one[...]).astype(low.dtype)


def inputs(grads, first, grad_one, rows):
    depth, slots = grads.shape
    width = first.shape[0]
    flat = pl.BlockSpec((rows, width), lambda i: (i, 0))
    return pl.pallas_call(
        inputs_kernel,
        grid=(slots // rows,),
        in_specs=[
            pl.BlockSpec((depth, rows), lambda i: (0, i)),
            pl.BlockSpec((width, depth), lambda i: (0, 0), pipeline_mode=pl.Buffered(1)),
            flat,
        ],
        out_specs=flat,
        out_shape=jax.ShapeDtypeStruct((slots, width), jnp.bfloat16),
        compiler_params=pltpu.CompilerParams(vmem_limit_bytes=VMEM),
        cost_estimate=cost(12),
        name="inputs",
    )(grads, first, grad_one)


def input_weights_kernel(x, grads, rows, d_w, edges):
    step, last = pl.program_id(0), pl.num_programs(0) - 1
    width = x.shape[1]
    depth = 3 * width
    size = grads.shape[0]
    grad = grads[...]
    product = contract(x[...], grad, 0, 1).astype(d_w.dtype)
    edge = jnp.sum(grad.astype(jnp.float32), 1, keepdims=True)
    for i in range(depth // size):

        @pl.when(step == i)
        def _(i=i):
            d_w[:, i * size : (i + 1) * size] = product
            column, top = i * size // width, i * size % width
            edges[top : top + size, column : column + 1] = edge

    @pl.when(step == last)
    def _():
        known = rows[...]
        tall = jnp.concatenate([known, jnp.zeros((128 - known.shape[0], width), jnp.float32)], 0).T
        column = lax.broadcasted_iota(jnp.int32, (width, 128), 1)
        sums = edges[...]
        columns = jnp.where(column == 0, sums[:, :1], jnp.where(column == 1, sums[:, 2:3], tall))
        d_w[:, depth:] = columns.astype(d_w.dtype)


def input_weights(x, grads, rows, size):
    slots, width = x.shape
    depth = grads.shape[0]
    one = pl.Buffered(1)
    return pl.pallas_call(
        input_weights_kernel,
        grid=(depth // size,),
        in_specs=[
            pl.BlockSpec((slots, width), lambda i: (0, 0), pipeline_mode=one),
            pl.BlockSpec((size, slots), lambda i: (i, 0)),
            pl.BlockSpec(rows.shape, lambda i: (0, 0)),
        ],
        out_specs=pl.BlockSpec((width, depth + 128), lambda i: (0, 0)),
        out_shape=jax.ShapeDtypeStruct((width, depth + 128), jnp.bfloat16),
        scratch_shapes=[pltpu.VMEM((width, 128), jnp.float32)],
        compiler_params=pltpu.CompilerParams(vmem_limit_bytes=VMEM),
        cost_estimate=cost(12),
        name="input_weights",
    )(x, grads, rows)


def whole_body(
    tokens,
    lengths,
    cotangent,
    w_query,
    b_query,
    w_key,
    w_value,
    b_value,
    w_out,
    b_out,
    gain_one,
    shift_one,
    w_up,
    b_up,
    w_down,
    b_down,
    gain_two,
    shift_two,
):
    count, block, width = tokens.shape
    slots = count * block
    wide = w_up.shape[1]
    rows = w_query.shape[0]
    axes = ("dp", "seq")
    me = lax.axis_index("seq")
    heads, size = H, HD
    scale = size ** (-0.5)
    times = wide // width

    x = exchange(tokens).reshape(slots, width)

    first = jnp.concatenate([w_query, w_key, w_value, columns(b_query, b_value)], 1)
    first = lax.all_gather(first, "seq", axis=0, tiled=True)
    first = lax.all_gather(first, "dp", axis=0, tiled=True)
    owners = width // rows
    mixed_up = w_up.reshape(rows, owners, times, rows).transpose(0, 2, 1, 3).reshape(rows, wide)
    downs = [w_down[i * rows : (i + 1) * rows] for i in range(times)]
    vectors = columns(b_out, gain_one, shift_one, b_down, gain_two, shift_two, b_up)
    second = jnp.concatenate([mixed_up] + downs + [w_out, vectors], 1)

    length = take(lengths, me)
    live = jnp.arange(slots, dtype=jnp.int32) < length
    bias = jnp.where(live, 0.0, -1e30).astype(jnp.bfloat16)
    bias = jnp.pad(bias[None, :], ((0, PAD - 1), (0, 0)))
    live = live[:, None].astype(jnp.float32)
    x, live, bias = lax.optimization_barrier((x, live, bias))
    second, first, x = lax.optimization_barrier((second, first, x))
    second = lax.all_gather(second, axes, axis=0, tiled=True)

    def by_head(array):
        return array.reshape(heads, size, slots)

    qt, kt, vt = project(x, first, block)
    qt, cotangent = lax.optimization_barrier((qt, cotangent))
    cot = exchange(cotangent).reshape(slots, width)
    qt, kt, vt = (by_head(a) for a in (qt, kt, vt))
    mt, total, probs = mix(qt, kt, vt, bias, scale * LOG2E)
    result, grad_one, gt, left, right, sums = feed(
        x, mt.reshape(width, slots), cot, live, second, wide, block
    )
    late = feed_weights(left, right, width)
    gt, late = lax.optimization_barrier((gt, late))
    late = lax.psum_scatter(late, "dp", scatter_dimension=0, tiled=True)
    output = exchange(result.reshape(count, block, width))
    grads = unmix(probs, qt, kt, vt, by_head(gt), mt, total, scale)
    grads, output = lax.optimization_barrier((grads, output))
    grads = grads.reshape(3 * width, slots)
    early = input_weights(x, grads, sums, width)
    early, late, grads = lax.optimization_barrier((early, late, grads))
    early = lax.psum_scatter(early, "dp", scatter_dimension=0, tiled=True)
    late = scattered(late)
    low = inputs(grads, first, grad_one, block)
    low, late = lax.optimization_barrier((low, late))
    grad_tokens = exchange(low.reshape(count, block, width))
    early, grad_tokens = lax.optimization_barrier((early, grad_tokens))
    early = scattered(early)
    grad_tokens = grad_tokens.astype(jnp.float32)
    o_wq, o_wk, o_wv = (early[:, i * width : (i + 1) * width] for i in range(3))
    vec = early[:, 3 * width :]
    o_wu = late[:, :wide].reshape(rows, times, owners, rows).transpose(0, 2, 1, 3).reshape(rows, wide)
    o_wd = jnp.concatenate(
        [late[:, wide + i * width : wide + (i + 1) * width] for i in range(times)], 0
    )
    o_wo = late[:, 2 * wide :]
    o_bq, o_bv, o_bo, o_g1, o_s1, o_bd, o_g2, o_s2 = (vec[:, i] for i in range(8))
    o_bu = vec[:, 8 : 8 + times].T.reshape(rows * times)
    return (
        output,
        grad_tokens,
        o_wq,
        o_bq,
        o_wk,
        o_wv,
        o_bv,
        o_wo,
        o_bo,
        o_g1,
        o_s1,
        o_wu,
        o_bu,
        o_wd,
        o_bd,
        o_g2,
        o_s2,
    )


def body(*arrays):
    count = arrays[0].shape[0]
    fits = count == lax.axis_size("seq") and count & (count - 1) == 0
    return whole_body(*arrays) if fits else general_body(*arrays)


def solution(mesh):
    in_specs = (
        P("dp", "seq", None),
        P("dp"),
        P("dp", "seq", None),
        P(("dp", "seq"), None),
        P(("dp", "seq")),
        P(("dp", "seq"), None),
        P(("dp", "seq"), None),
        P(("dp", "seq")),
        P(("dp", "seq"), None),
        P(("dp", "seq")),
        P(("dp", "seq")),
        P(("dp", "seq")),
        P(("dp", "seq"), None),
        P(("dp", "seq")),
        P(("dp", "seq"), None),
        P(("dp", "seq")),
        P(("dp", "seq")),
        P(("dp", "seq")),
    )
    out_specs = (
        P("dp", "seq", None),
        P("dp", "seq", None),
        P(("dp", "seq"), None),
        P(("dp", "seq")),
        P(("dp", "seq"), None),
        P(("dp", "seq"), None),
        P(("dp", "seq")),
        P(("dp", "seq"), None),
        P(("dp", "seq")),
        P(("dp", "seq")),
        P(("dp", "seq")),
        P(("dp", "seq"), None),
        P(("dp", "seq")),
        P(("dp", "seq"), None),
        P(("dp", "seq")),
        P(("dp", "seq")),
        P(("dp", "seq")),
    )
    return jax.shard_map(body, mesh=mesh, in_specs=in_specs, out_specs=out_specs, check_vma=False)
```

```python
import functools

import jax
import jax.numpy as jnp
from jax import lax
from jax.experimental import pallas as pl
from jax.experimental.pallas import tpu as pltpu
from jax.sharding import PartitionSpec as P

H = 12
HD = 64
MB = 4


epsilon = 1e-06


def layer_norm(layer_input_rows, norm_gain, norm_shift):
    centre = layer_input_rows - jnp.mean(layer_input_rows, -1, keepdims=True)
    spread = jnp.mean(centre * centre, -1, keepdims=True)
    return centre * lax.rsqrt(spread + epsilon) * norm_gain + norm_shift


def gelu_exact(values):
    return jax.nn.gelu(values, approximate=False)


def matmul(former, latter):
    return jnp.dot(former, latter, preferred_element_type=jnp.float32)


def former_product(former, latter):
    return lax.dot_general(
        former, latter, (((0,), (0,)), ((), ())), preferred_element_type=jnp.float32
    )


def latter_product(former, latter):
    return lax.dot_general(
        former, latter, (((1,), (1,)), ((), ())), preferred_element_type=jnp.float32
    )


def widen(vector):
    return vector.astype(jnp.float32)


def general_body(
    tokens,
    lengths,
    cotangent,
    w_query,
    b_query,
    w_key,
    w_value,
    b_value,
    w_out,
    b_out,
    gain_one,
    shift_one,
    w_up,
    b_up,
    w_down,
    b_down,
    gain_two,
    shift_two,
):
    shards = (
        w_query,
        b_query,
        w_key,
        w_value,
        b_value,
        w_out,
        b_out,
        gain_one,
        shift_one,
        w_up,
        b_up,
        w_down,
        b_down,
        gain_two,
        shift_two,
    )
    per_batch = tokens.shape[0] // MB
    block_rows = tokens.shape[1]
    model_width = tokens.shape[2]
    head_count = H
    head_size = HD
    flat_rows = per_batch * block_rows
    full_length = block_rows * lax.axis_size("seq")
    offset = lax.axis_index("seq") * block_rows
    positions = jnp.arange(full_length, dtype=jnp.int32)
    own_positions = offset + jnp.arange(block_rows, dtype=jnp.int32)
    score_scale = head_size ** (-0.5)
    owners = lax.axis_size(("dp", "seq"))
    totals = [
        jnp.zeros((shard_piece.shape[0] * owners,) + shard_piece.shape[1:], jnp.float32)
        for shard_piece in shards
    ]
    outputs = []
    input_grads = []
    for micro_batch in range(MB):
        leading_row = micro_batch * per_batch
        own_tokens = tokens[leading_row : leading_row + per_batch]
        own_lengths = lengths[leading_row : leading_row + per_batch]
        own_cots = cotangent[leading_row : leading_row + per_batch]
        fore_weights = (
            lax.all_gather(shards[0], ("dp", "seq"), axis=0, tiled=True),
            lax.all_gather(shards[1], ("dp", "seq"), axis=0, tiled=True),
            lax.all_gather(shards[2], ("dp", "seq"), axis=0, tiled=True),
            lax.all_gather(shards[3], ("dp", "seq"), axis=0, tiled=True),
            lax.all_gather(shards[4], ("dp", "seq"), axis=0, tiled=True),
            lax.all_gather(shards[5], ("dp", "seq"), axis=0, tiled=True),
            lax.all_gather(shards[6], ("dp", "seq"), axis=0, tiled=True),
            lax.all_gather(shards[7], ("dp", "seq"), axis=0, tiled=True),
            lax.all_gather(shards[8], ("dp", "seq"), axis=0, tiled=True),
            lax.all_gather(shards[9], ("dp", "seq"), axis=0, tiled=True),
            lax.all_gather(shards[10], ("dp", "seq"), axis=0, tiled=True),
            lax.all_gather(shards[11], ("dp", "seq"), axis=0, tiled=True),
            lax.all_gather(shards[12], ("dp", "seq"), axis=0, tiled=True),
            lax.all_gather(shards[13], ("dp", "seq"), axis=0, tiled=True),
            lax.all_gather(shards[14], ("dp", "seq"), axis=0, tiled=True),
        )
        flat_tokens = own_tokens.reshape(flat_rows, model_width)
        query_low = (matmul(flat_tokens, fore_weights[0]) + widen(fore_weights[1])).astype(
            jnp.bfloat16
        )
        key_low = matmul(flat_tokens, fore_weights[2]).astype(jnp.bfloat16)
        value_low = (matmul(flat_tokens, fore_weights[3]) + widen(fore_weights[4])).astype(
            jnp.bfloat16
        )
        key_block = key_low.reshape(per_batch, block_rows, model_width)
        value_block = value_low.reshape(per_batch, block_rows, model_width)
        gathered_keys, gathered_values = (
            lax.all_gather(key_block, "seq", axis=1, tiled=True),
            lax.all_gather(value_block, "seq", axis=1, tiled=True),
        )
        query_heads = query_low.reshape(per_batch, block_rows, head_count, head_size)
        visible = (positions[None, :] < own_lengths[:, None])[:, None, None, :]

        def score_block(key_all):
            key_heads = key_all.reshape(per_batch, full_length, head_count, head_size)
            raw_scores = jnp.einsum(
                "pqhd,pkhd->phqk", query_heads, key_heads, preferred_element_type=jnp.float32
            )
            return jnp.where(visible, raw_scores * score_scale, -1e30)

        scores = score_block(gathered_keys)
        logarithm_totals = jax.nn.logsumexp(scores, axis=-1, keepdims=True)
        chances_low = jnp.exp(scores - logarithm_totals).astype(jnp.bfloat16)
        value_heads = gathered_values.reshape(per_batch, full_length, head_count, head_size)
        mixed_heads = jnp.einsum(
            "phqk,pkhd->pqhd", chances_low, value_heads, preferred_element_type=jnp.float32
        )
        mixed_low = mixed_heads.reshape(flat_rows, model_width).astype(jnp.bfloat16)
        branch = matmul(mixed_low, fore_weights[5]) + widen(fore_weights[6])
        resid_one = flat_tokens.astype(jnp.float32) + branch
        normed = layer_norm(resid_one, widen(fore_weights[7]), widen(fore_weights[8]))
        normed_low = normed.astype(jnp.bfloat16)
        hidden = matmul(normed_low, fore_weights[9]) + widen(fore_weights[10])
        active_low = gelu_exact(hidden).astype(jnp.bfloat16)
        feed_out = matmul(active_low, fore_weights[11]) + widen(fore_weights[12])
        resid_two = normed + feed_out
        result = layer_norm(resid_two, widen(fore_weights[13]), widen(fore_weights[14]))
        outputs.append(result.astype(jnp.bfloat16).reshape(per_batch, block_rows, model_width))
        back_weights = (
            lax.all_gather(shards[0], ("dp", "seq"), axis=0, tiled=True),
            lax.all_gather(shards[1], ("dp", "seq"), axis=0, tiled=True),
            lax.all_gather(shards[2], ("dp", "seq"), axis=0, tiled=True),
            lax.all_gather(shards[3], ("dp", "seq"), axis=0, tiled=True),
            lax.all_gather(shards[4], ("dp", "seq"), axis=0, tiled=True),
            lax.all_gather(shards[5], ("dp", "seq"), axis=0, tiled=True),
            lax.all_gather(shards[6], ("dp", "seq"), axis=0, tiled=True),
            lax.all_gather(shards[7], ("dp", "seq"), axis=0, tiled=True),
            lax.all_gather(shards[8], ("dp", "seq"), axis=0, tiled=True),
            lax.all_gather(shards[9], ("dp", "seq"), axis=0, tiled=True),
            lax.all_gather(shards[10], ("dp", "seq"), axis=0, tiled=True),
            lax.all_gather(shards[11], ("dp", "seq"), axis=0, tiled=True),
            lax.all_gather(shards[12], ("dp", "seq"), axis=0, tiled=True),
            lax.all_gather(shards[13], ("dp", "seq"), axis=0, tiled=True),
            lax.all_gather(shards[14], ("dp", "seq"), axis=0, tiled=True),
        )
        live_rows = (
            (own_positions[None, :] < own_lengths[:, None])
            .astype(jnp.float32)
            .reshape(flat_rows, 1)
        )
        incoming = own_cots.reshape(flat_rows, model_width).astype(jnp.float32) * live_rows
        _, second_pull = jax.vjp(
            layer_norm, resid_two, widen(back_weights[13]), widen(back_weights[14])
        )
        grad_two, grad_gain_two, grad_shift_two = second_pull(incoming)
        feed_low = grad_two.astype(jnp.bfloat16)
        totals[11] = totals[11] + former_product(active_low, feed_low)
        totals[12] = totals[12] + jnp.sum(feed_low.astype(jnp.float32), 0)
        grad_active = latter_product(feed_low, back_weights[11])
        _, gelu_pull = jax.vjp(gelu_exact, hidden)
        up_low = gelu_pull(grad_active)[0].astype(jnp.bfloat16)
        totals[9] = totals[9] + former_product(normed_low, up_low)
        totals[10] = totals[10] + jnp.sum(up_low.astype(jnp.float32), 0)
        grad_normed = latter_product(up_low, back_weights[9]) + grad_two
        _, first_pull = jax.vjp(
            layer_norm, resid_one, widen(back_weights[7]), widen(back_weights[8])
        )
        grad_one, grad_gain_one, grad_shift_one = first_pull(grad_normed)
        branch_low = grad_one.astype(jnp.bfloat16)
        totals[5] = totals[5] + former_product(mixed_low, branch_low)
        totals[6] = totals[6] + jnp.sum(branch_low.astype(jnp.float32), 0)
        dmix_low = latter_product(branch_low, back_weights[5]).astype(jnp.bfloat16)
        dmix_heads = dmix_low.reshape(per_batch, block_rows, head_count, head_size)
        back_keys, backward_value_rows = (gathered_keys, gathered_values)
        chances = jnp.exp(score_block(back_keys) - logarithm_totals)
        back_value_heads = backward_value_rows.reshape(
            per_batch, full_length, head_count, head_size
        )
        back_key_heads = back_keys.reshape(per_batch, full_length, head_count, head_size)
        grad_chances = jnp.einsum(
            "pqhd,pkhd->phqk", dmix_heads, back_value_heads, preferred_element_type=jnp.float32
        )
        row_inner = jnp.sum(grad_chances * chances, -1, keepdims=True)
        dscore_low = (score_scale * (chances * (grad_chances - row_inner))).astype(jnp.bfloat16)
        dquery_low = jnp.einsum(
            "phqk,pkhd->pqhd", dscore_low, back_key_heads, preferred_element_type=jnp.float32
        )
        dquery_low = dquery_low.reshape(flat_rows, model_width).astype(jnp.bfloat16)
        chance_low = chances.astype(jnp.bfloat16)
        value_terms = jnp.einsum(
            "phqk,pqhd->pkhd", chance_low, dmix_heads, preferred_element_type=jnp.float32
        )
        key_terms = jnp.einsum(
            "phqk,pqhd->pkhd", dscore_low, query_heads, preferred_element_type=jnp.float32
        )
        key_sums, value_sums = (
            lax.psum_scatter(
                key_terms.reshape(per_batch, full_length, model_width).astype(jnp.bfloat16),
                "seq",
                scatter_dimension=1,
                tiled=True,
            ).astype(jnp.float32),
            lax.psum_scatter(
                value_terms.reshape(per_batch, full_length, model_width).astype(jnp.bfloat16),
                "seq",
                scatter_dimension=1,
                tiled=True,
            ).astype(jnp.float32),
        )
        dkey_low = key_sums.reshape(flat_rows, model_width).astype(jnp.bfloat16)
        dvalue_low = value_sums.reshape(flat_rows, model_width).astype(jnp.bfloat16)
        totals[0] = totals[0] + former_product(flat_tokens, dquery_low)
        totals[1] = totals[1] + jnp.sum(dquery_low.astype(jnp.float32), 0)
        totals[2] = totals[2] + former_product(flat_tokens, dkey_low)
        totals[3] = totals[3] + former_product(flat_tokens, dvalue_low)
        totals[4] = totals[4] + jnp.sum(dvalue_low.astype(jnp.float32), 0)
        totals[7] = totals[7] + grad_gain_one
        totals[8] = totals[8] + grad_shift_one
        totals[13] = totals[13] + grad_gain_two
        totals[14] = totals[14] + grad_shift_two
        grad_input = (
            latter_product(dquery_low, back_weights[0])
            + latter_product(dkey_low, back_weights[2])
            + latter_product(dvalue_low, back_weights[3])
            + grad_one
        )
        input_grads.append(grad_input.reshape(per_batch, block_rows, model_width))
    owned = lax.psum_scatter(tuple(totals), ("dp", "seq"), scatter_dimension=0, tiled=True)
    output = jnp.concatenate(outputs, 0)
    grad_tokens = jnp.concatenate(input_grads, 0)
    return (
        output,
        grad_tokens,
        owned[0],
        owned[1],
        owned[2],
        owned[3],
        owned[4],
        owned[5],
        owned[6],
        owned[7],
        owned[8],
        owned[9],
        owned[10],
        owned[11],
        owned[12],
        owned[13],
        owned[14],
    )


LOG2E = 1.4426950408889634
PAD = 16
VMEM = 60 << 20
RATE = 1e9


def cost(microseconds):
    return pl.CostEstimate(flops=int(microseconds * RATE), bytes_accessed=0, transcendentals=0)


def contract(former, latter, dim_former, dim_latter):
    return lax.dot_general(
        former,
        latter,
        (((dim_former,), (dim_latter,)), ((), ())),
        preferred_element_type=jnp.float32,
    )


def mix_kernel(scale, chunk, qt, kt, vt, bias, mixed, total, probs, queries, vals):
    size, slots = kt.shape[1], kt.shape[2]
    query = qt[0].astype(jnp.float32) * scale
    high = query.astype(jnp.bfloat16)
    low = (query - high.astype(jnp.float32)).astype(jnp.bfloat16)
    row = lax.broadcasted_iota(jnp.int32, (PAD, slots), 0)
    first = jnp.where(row == 0, 1.0, 0.0).astype(jnp.bfloat16)
    queries[...] = jnp.concatenate([high, low, first], 0).T
    keys = jnp.concatenate([kt[0], kt[0], bias[...]], 0)
    vals[...] = jnp.concatenate([vt[0], jnp.ones((PAD, slots), jnp.bfloat16)], 0).T

    def block(at, seen):
        cut = slice(at, at + chunk)
        scores = matmul(queries[cut], keys)
        top = jnp.max(scores[:, :seen], 1, keepdims=True)
        part = jnp.exp2(scores - top).astype(jnp.bfloat16)
        probs[0, cut] = part
        sums = matmul(part, vals[...]).T
        weight = sums[size : size + 1]
        mixed[0, :, cut] = (sums[:size] / weight).astype(mixed.dtype)
        total[0, :, cut] = weight
        return jnp.max(weight)

    largest = [block(at, 256) for at in range(0, slots, chunk)]

    @pl.when(jnp.logical_not(functools.reduce(jnp.maximum, largest) < 2.0**60))
    def _():
        for at in range(0, slots, chunk):
            block(at, slots)


def mix(qt, kt, vt, bias, scale):
    heads, size, slots = qt.shape
    whole = pl.BlockSpec((1, size, slots), lambda i: (i, 0, 0))
    return pl.pallas_call(
        functools.partial(mix_kernel, scale, 512),
        grid=(heads,),
        in_specs=[whole, whole, whole, pl.BlockSpec((PAD, slots), lambda i: (0, 0))],
        out_specs=[
            whole,
            pl.BlockSpec((1, 1, slots), lambda i: (i, 0, 0)),
            pl.BlockSpec((1, slots, slots), lambda i: (i, 0, 0)),
        ],
        out_shape=[
            jax.ShapeDtypeStruct((heads, size, slots), jnp.bfloat16),
            jax.ShapeDtypeStruct((heads, 1, slots), jnp.float32),
            jax.ShapeDtypeStruct((heads, slots, slots), jnp.bfloat16),
        ],
        scratch_shapes=[
            pltpu.VMEM((slots, 2 * size + PAD), jnp.bfloat16),
            pltpu.VMEM((slots, size + PAD), jnp.bfloat16),
        ],
        compiler_params=pltpu.CompilerParams(vmem_limit_bytes=VMEM),
        cost_estimate=cost(65),
        name="mix",
    )(qt, kt, vt, bias)


def unmix_kernel(scale, chunk, probs, qt, kt, vt, gt, mt, total, out, keys):
    slots = kt.shape[2]
    grad = (gt[0].astype(jnp.float32) / total[0]).astype(jnp.bfloat16)
    inner = jnp.sum(grad.astype(jnp.float32) * mt[0].astype(jnp.float32), 0, keepdims=True)
    inner = jnp.broadcast_to(inner, (8, slots)).T[:, :1]
    turned = grad.T
    keys[...] = kt[0].T
    dk = dv = None
    for at in range(0, slots, chunk):
        cut = slice(at, at + chunk)
        prob = probs[0, cut]
        dprob = matmul(turned[cut], vt[0])
        dscore = (prob.astype(jnp.float32) * (dprob - inner[cut])).astype(jnp.bfloat16)
        out[0, 0, :, cut] = (matmul(dscore, keys[...]) * scale).T.astype(jnp.bfloat16)
        value_term = matmul(grad[:, cut], prob)
        key_term = matmul(qt[0, :, cut], dscore)
        dv = value_term if dv is None else dv + value_term
        dk = key_term if dk is None else dk + key_term
    out[1, 0] = (dk * scale).astype(jnp.bfloat16)
    out[2, 0] = dv.astype(jnp.bfloat16)


def unmix(probs, qt, kt, vt, gt, mt, total, scale):
    heads, size, slots = qt.shape
    whole = pl.BlockSpec((1, size, slots), lambda i: (i, 0, 0))
    return pl.pallas_call(
        functools.partial(unmix_kernel, scale, 256),
        grid=(heads,),
        in_specs=[pl.BlockSpec((1, slots, slots), lambda i: (i, 0, 0))]
        + [whole] * 5
        + [pl.BlockSpec((1, 1, slots), lambda i: (i, 0, 0))],
        out_specs=pl.BlockSpec((3, 1, size, slots), lambda i: (0, i, 0, 0)),
        out_shape=jax.ShapeDtypeStruct((3, heads, size, slots), jnp.bfloat16),
        scratch_shapes=[pltpu.VMEM((slots, size), jnp.bfloat16)],
        compiler_params=pltpu.CompilerParams(vmem_limit_bytes=VMEM),
        cost_estimate=cost(95),
        name="unmix",
    )(probs, qt, kt, vt, gt, mt, total)


def exchange(blocks):
    return lax.all_to_all(blocks, "seq", 0, 0, tiled=True)


def take(array, index):
    return lax.dynamic_index_in_dim(array, index, 0, keepdims=False)


def columns(*vectors):
    rows = vectors[0].shape[0]
    stack = jnp.concatenate(vectors).reshape(-1, rows)
    unit = jnp.eye(stack.shape[0], 128, dtype=stack.dtype)
    return contract(stack, unit, 0, 0).astype(stack.dtype)


def scattered(rows):
    me = lax.axis_index("seq")
    size = lax.axis_size("seq")
    parts = rows.reshape(size, rows.shape[0] // size, rows.shape[1])
    total = take(parts, me).astype(jnp.float32)
    for step in range(1, size):
        pairs = [(i, i ^ step) for i in range(size)]
        came = lax.ppermute(take(parts, me ^ step), "seq", pairs)
        total = total + came.astype(jnp.float32)
    return total


def row_sums(array):
    return jnp.sum(array, 0, keepdims=True)


def project_kernel(x, w, vec, qt, kt, vt):
    width = x.shape[1]
    bias = vec[...].T[:8].astype(jnp.float32)
    outs = matmul(x[...], w[...])
    for i, out in enumerate((qt, kt, vt)):
        part = outs[:, i * width : (i + 1) * width]
        if i != 1:
            part = part + bias[i // 2 : i // 2 + 1]
        out[...] = part.astype(jnp.bfloat16).T


def project(x, first, rows):
    slots, width = x.shape
    flat = pl.BlockSpec((width, rows), lambda i: (0, i))
    one = pl.Buffered(1)
    return pl.pallas_call(
        project_kernel,
        grid=(slots // rows,),
        in_specs=[
            pl.BlockSpec((rows, width), lambda i: (i, 0)),
            pl.BlockSpec((width, 3 * width), lambda i: (0, 0), pipeline_mode=one),
            pl.BlockSpec((width, 128), lambda i: (0, 3 * width // 128)),
        ],
        out_specs=[flat] * 3,
        out_shape=[jax.ShapeDtypeStruct((width, slots), jnp.bfloat16)] * 3,
        compiler_params=pltpu.CompilerParams(vmem_limit_bytes=VMEM),
        cost_estimate=cost(11),
        name="project",
    )(x, first, first)


def norm(rows):
    centre = rows - jnp.mean(rows, -1, keepdims=True)
    rstd = lax.rsqrt(jnp.mean(centre * centre, -1, keepdims=True) + epsilon)
    return centre * rstd, rstd


def norm_back(unit, rstd, grad):
    mean = jnp.mean(grad, -1, keepdims=True)
    inner = jnp.mean(grad * unit, -1, keepdims=True)
    return rstd * (grad - mean - unit * inner)


def feed_kernel(
    x, mt, cot, live, vec, wo, wu, wd, output, grad_one, gt, left, right, sums, slope,
):
    width = x.shape[1]
    wide = wu.shape[1]
    step = pl.program_id(0)
    known = vec[...].T[:16].astype(jnp.float32)
    bo, g1, s1, bd, g2, s2 = (known[i : i + 1] for i in range(6))
    mixed = mt[...].T
    left[:, wide + width :] = mixed
    resid = x[...].astype(jnp.float32) + matmul(mixed, wo[...]) + bo
    unit_one, rstd_one = norm(resid)
    normed = unit_one * g1 + s1
    low = normed.astype(jnp.bfloat16)
    left[:, :width] = low
    resid = normed + bd
    for at in range(0, wide, width):
        cut = slice(at, at + width)
        hidden = matmul(low, wu[:, cut]) + known[6 + at // width : 7 + at // width]
        share = 0.5 + 0.5 * lax.erf(hidden * 0.7071067811865476)
        bell = jnp.exp2(hidden * hidden * -0.7213475204444817) * 0.3989422804014327
        slope[:, cut] = (share + hidden * bell).astype(jnp.bfloat16)
        active = (hidden * share).astype(jnp.bfloat16)
        left[:, width + at : 2 * width + at] = active
        resid = resid + matmul(active, wd[:, cut])
    unit_two, rstd_two = norm(resid)
    output[...] = (unit_two * g2 + s2).astype(jnp.bfloat16)
    incoming = cot[...].astype(jnp.float32) * live[...]
    grad_two = norm_back(unit_two, rstd_two, incoming * g2)
    feed = grad_two.astype(jnp.bfloat16)
    right[:, wide : wide + width] = feed
    grad = grad_two
    up_rows = []
    for at in range(0, wide, width):
        cut = slice(at, at + width)
        part = contract(feed, wd[:, cut], 1, 1) * slope[:, cut].astype(jnp.float32)
        part = part.astype(jnp.bfloat16)
        right[:, cut] = part
        up_rows.append(row_sums(part.astype(jnp.float32)))
        grad = grad + contract(part, wu[:, cut], 1, 1)
    first = norm_back(unit_one, rstd_one, grad * g1)
    grad_one[...] = first
    branch = first.astype(jnp.bfloat16)
    right[:, wide + width :] = branch
    gt[...] = contract(wo[...], branch, 1, 1).astype(jnp.bfloat16)
    rows = [
        row_sums(branch.astype(jnp.float32)),
        row_sums(grad * unit_one),
        row_sums(grad),
        row_sums(feed.astype(jnp.float32)),
        row_sums(incoming * unit_two),
        row_sums(incoming),
    ]
    blank = [jnp.zeros((2, width), jnp.float32)]
    rows = jnp.concatenate(blank + rows + up_rows, 0)

    @pl.when(step == 0)
    def _():
        sums[...] = rows

    @pl.when(step > 0)
    def _():
        sums[...] += rows


def feed(x, mt, cot, live, second, wide, rows):
    slots, width = x.shape
    one = pl.Buffered(1)
    flat = pl.BlockSpec((rows, width), lambda i: (i, 0))
    tall = pl.BlockSpec((width, rows), lambda i: (0, i))
    stack = wide + 2 * width
    broad = pl.BlockSpec((rows, stack), lambda i: (i, 0))
    low = jnp.bfloat16
    return pl.pallas_call(
        feed_kernel,
        grid=(slots // rows,),
        in_specs=[
            flat,
            tall,
            flat,
            pl.BlockSpec((rows, 1), lambda i: (i, 0)),
            pl.BlockSpec((width, 128), lambda i: (0, (2 * wide + width) // 128)),
            pl.BlockSpec((width, width), lambda i: (0, 2 * wide // width), pipeline_mode=one),
            pl.BlockSpec((width, wide), lambda i: (0, 0), pipeline_mode=one),
            pl.BlockSpec((width, wide), lambda i: (0, 1), pipeline_mode=one),
        ],
        out_specs=[
            flat,
            flat,
            tall,
            broad,
            broad,
            pl.BlockSpec((8 + wide // width, width), lambda i: (0, 0)),
        ],
        out_shape=[
            jax.ShapeDtypeStruct((slots, width), low),
            jax.ShapeDtypeStruct((slots, width), jnp.float32),
            jax.ShapeDtypeStruct((width, slots), low),
            jax.ShapeDtypeStruct((slots, stack), low),
            jax.ShapeDtypeStruct((slots, stack), low),
            jax.ShapeDtypeStruct((8 + wide // width, width), jnp.float32),
        ],
        scratch_shapes=[pltpu.VMEM((rows, wide), low)],
        compiler_params=pltpu.CompilerParams(vmem_limit_bytes=VMEM),
        cost_estimate=cost(70),
        name="feed",
    )(x, mt, cot, live, second, second, second, second)


def feed_weights_kernel(left, right, d_w):
    d_w[...] = contract(left[...], right[...], 0, 0).astype(d_w.dtype)


def feed_weights(left, right, width):
    slots, stack = left.shape
    parts = stack // width - 2
    return pl.pallas_call(
        feed_weights_kernel,
        grid=(2 * parts + 1,),
        in_specs=[
            pl.BlockSpec((slots, width), lambda i: (0, jnp.maximum(i - parts + 1, 0))),
            pl.BlockSpec(
                (slots, width), lambda i: (0, jnp.minimum(i, parts) + i // (2 * parts))
            ),
        ],
        out_specs=pl.BlockSpec((width, width), lambda i: (0, i)),
        out_shape=jax.ShapeDtypeStruct((width, (2 * parts + 1) * width), jnp.bfloat16),
        compiler_params=pltpu.CompilerParams(vmem_limit_bytes=VMEM),
        cost_estimate=cost(26),
        name="feed_weights",
    )(left, right)


def inputs_kernel(grads, weights, grad_one, low):
    low[...] = (contract(grads[...], weights[...], 0, 1) + grad_one[...]).astype(low.dtype)


def inputs(grads, first, grad_one, rows):
    depth, slots = grads.shape
    width = first.shape[0]
    flat = pl.BlockSpec((rows, width), lambda i: (i, 0))
    return pl.pallas_call(
        inputs_kernel,
        grid=(slots // rows,),
        in_specs=[
            pl.BlockSpec((depth, rows), lambda i: (0, i)),
            pl.BlockSpec((width, depth), lambda i: (0, 0), pipeline_mode=pl.Buffered(1)),
            flat,
        ],
        out_specs=flat,
        out_shape=jax.ShapeDtypeStruct((slots, width), jnp.bfloat16),
        compiler_params=pltpu.CompilerParams(vmem_limit_bytes=VMEM),
        cost_estimate=cost(12),
        name="inputs",
    )(grads, first, grad_one)


def input_weights_kernel(x, grads, rows, d_w, edges):
    step, last = pl.program_id(0), pl.num_programs(0) - 1
    width = x.shape[1]
    depth = 3 * width
    size = grads.shape[0]
    grad = grads[...]
    product = contract(x[...], grad, 0, 1).astype(d_w.dtype)
    edge = jnp.sum(grad.astype(jnp.float32), 1, keepdims=True)
    for i in range(depth // size):

        @pl.when(step == i)
        def _(i=i):
            d_w[:, i * size : (i + 1) * size] = product
            column, top = i * size // width, i * size % width
            edges[top : top + size, column : column + 1] = edge

    @pl.when(step == last)
    def _():
        known = rows[...]
        tall = jnp.concatenate([known, jnp.zeros((128 - known.shape[0], width), jnp.float32)], 0).T
        column = lax.broadcasted_iota(jnp.int32, (width, 128), 1)
        sums = edges[...]
        columns = jnp.where(column == 0, sums[:, :1], jnp.where(column == 1, sums[:, 2:3], tall))
        d_w[:, depth:] = columns.astype(d_w.dtype)


def input_weights(x, grads, rows, size):
    slots, width = x.shape
    depth = grads.shape[0]
    one = pl.Buffered(1)
    return pl.pallas_call(
        input_weights_kernel,
        grid=(depth // size,),
        in_specs=[
            pl.BlockSpec((slots, width), lambda i: (0, 0), pipeline_mode=one),
            pl.BlockSpec((size, slots), lambda i: (i, 0)),
            pl.BlockSpec(rows.shape, lambda i: (0, 0)),
        ],
        out_specs=pl.BlockSpec((width, depth + 128), lambda i: (0, 0)),
        out_shape=jax.ShapeDtypeStruct((width, depth + 128), jnp.bfloat16),
        scratch_shapes=[pltpu.VMEM((width, 128), jnp.float32)],
        compiler_params=pltpu.CompilerParams(vmem_limit_bytes=VMEM),
        cost_estimate=cost(12),
        name="input_weights",
    )(x, grads, rows)


def whole_body(
    tokens,
    lengths,
    cotangent,
    w_query,
    b_query,
    w_key,
    w_value,
    b_value,
    w_out,
    b_out,
    gain_one,
    shift_one,
    w_up,
    b_up,
    w_down,
    b_down,
    gain_two,
    shift_two,
):
    count, block, width = tokens.shape
    slots = count * block
    wide = w_up.shape[1]
    rows = w_query.shape[0]
    axes = ("dp", "seq")
    me = lax.axis_index("seq")
    heads, size = H, HD
    scale = size ** (-0.5)
    times = wide // width

    x = exchange(tokens).reshape(slots, width)

    first = jnp.concatenate([w_query, w_key, w_value, columns(b_query, b_value)], 1)
    first = lax.all_gather(first, "seq", axis=0, tiled=True)
    first = lax.all_gather(first, "dp", axis=0, tiled=True)
    owners = width // rows
    mixed_up = w_up.reshape(rows, owners, times, rows).transpose(0, 2, 1, 3).reshape(rows, wide)
    downs = [w_down[i * rows : (i + 1) * rows] for i in range(times)]
    vectors = columns(b_out, gain_one, shift_one, b_down, gain_two, shift_two, b_up)
    second = jnp.concatenate([mixed_up] + downs + [w_out, vectors], 1)

    length = take(lengths, me)
    live = jnp.arange(slots, dtype=jnp.int32) < length
    bias = jnp.where(live, 0.0, -1e30).astype(jnp.bfloat16)
    bias = jnp.pad(bias[None, :], ((0, PAD - 1), (0, 0)))
    live = live[:, None].astype(jnp.float32)
    x, live, bias = lax.optimization_barrier((x, live, bias))
    second, first, x = lax.optimization_barrier((second, first, x))
    second = lax.all_gather(second, axes, axis=0, tiled=True)

    def by_head(array):
        return array.reshape(heads, size, slots)

    qt, kt, vt = project(x, first, block)
    qt, cotangent = lax.optimization_barrier((qt, cotangent))
    cot = exchange(cotangent).reshape(slots, width)
    qt, kt, vt = (by_head(a) for a in (qt, kt, vt))
    mt, total, probs = mix(qt, kt, vt, bias, scale * LOG2E)
    result, grad_one, gt, left, right, sums = feed(
        x, mt.reshape(width, slots), cot, live, second, wide, block
    )
    late = feed_weights(left, right, width)
    gt, late = lax.optimization_barrier((gt, late))
    late = lax.psum_scatter(late, "dp", scatter_dimension=0, tiled=True)
    output = exchange(result.reshape(count, block, width))
    grads = unmix(probs, qt, kt, vt, by_head(gt), mt, total, scale)
    grads, output = lax.optimization_barrier((grads, output))
    grads = grads.reshape(3 * width, slots)
    early = input_weights(x, grads, sums, width)
    early, late, grads = lax.optimization_barrier((early, late, grads))
    early = lax.psum_scatter(early, "dp", scatter_dimension=0, tiled=True)
    late = scattered(late)
    low = inputs(grads, first, grad_one, block)
    grad_tokens = exchange(low.reshape(count, block, width))
    early, low = lax.optimization_barrier((early, low))
    early = scattered(early)
    grad_tokens, early = lax.optimization_barrier((grad_tokens, early))
    grad_tokens = grad_tokens.astype(jnp.float32)
    o_wq, o_wk, o_wv = (early[:, i * width : (i + 1) * width] for i in range(3))
    vec = early[:, 3 * width :]
    o_wu = late[:, :wide].reshape(rows, times, owners, rows).transpose(0, 2, 1, 3).reshape(rows, wide)
    o_wd = jnp.concatenate(
        [late[:, wide + i * width : wide + (i + 1) * width] for i in range(times)], 0
    )
    o_wo = late[:, 2 * wide :]
    o_bq, o_bv, o_bo, o_g1, o_s1, o_bd, o_g2, o_s2 = (vec[:, i] for i in range(8))
    o_bu = vec[:, 8 : 8 + times].T.reshape(rows * times)
    return (
        output,
        grad_tokens,
        o_wq,
        o_bq,
        o_wk,
        o_wv,
        o_bv,
        o_wo,
        o_bo,
        o_g1,
        o_s1,
        o_wu,
        o_bu,
        o_wd,
        o_bd,
        o_g2,
        o_s2,
    )


def body(*arrays):
    count = arrays[0].shape[0]
    fits = count == lax.axis_size("seq") and count & (count - 1) == 0
    return whole_body(*arrays) if fits else general_body(*arrays)


def solution(mesh):
    in_specs = (
        P("dp", "seq", None),
        P("dp"),
        P("dp", "seq", None),
        P(("dp", "seq"), None),
        P(("dp", "seq")),
        P(("dp", "seq"), None),
        P(("dp", "seq"), None),
        P(("dp", "seq")),
        P(("dp", "seq"), None),
        P(("dp", "seq")),
        P(("dp", "seq")),
        P(("dp", "seq")),
        P(("dp", "seq"), None),
        P(("dp", "seq")),
        P(("dp", "seq"), None),
        P(("dp", "seq")),
        P(("dp", "seq")),
        P(("dp", "seq")),
    )
    out_specs = (
        P("dp", "seq", None),
        P("dp", "seq", None),
        P(("dp", "seq"), None),
        P(("dp", "seq")),
        P(("dp", "seq"), None),
        P(("dp", "seq"), None),
        P(("dp", "seq")),
        P(("dp", "seq"), None),
        P(("dp", "seq")),
        P(("dp", "seq")),
        P(("dp", "seq")),
        P(("dp", "seq"), None),
        P(("dp", "seq")),
        P(("dp", "seq"), None),
        P(("dp", "seq")),
        P(("dp", "seq")),
        P(("dp", "seq")),
    )
    return jax.shard_map(body, mesh=mesh, in_specs=in_specs, out_specs=out_specs, check_vma=False)
```

```python
import functools

import jax
import jax.numpy as jnp
from jax import lax
from jax.experimental import pallas as pl
from jax.experimental.pallas import tpu as pltpu
from jax.sharding import PartitionSpec as P

H = 12
HD = 64
MB = 4


epsilon = 1e-06


def layer_norm(layer_input_rows, norm_gain, norm_shift):
    centre = layer_input_rows - jnp.mean(layer_input_rows, -1, keepdims=True)
    spread = jnp.mean(centre * centre, -1, keepdims=True)
    return centre * lax.rsqrt(spread + epsilon) * norm_gain + norm_shift


def gelu_exact(values):
    return jax.nn.gelu(values, approximate=False)


def matmul(former, latter):
    return jnp.dot(former, latter, preferred_element_type=jnp.float32)


def former_product(former, latter):
    return lax.dot_general(
        former, latter, (((0,), (0,)), ((), ())), preferred_element_type=jnp.float32
    )


def latter_product(former, latter):
    return lax.dot_general(
        former, latter, (((1,), (1,)), ((), ())), preferred_element_type=jnp.float32
    )


def widen(vector):
    return vector.astype(jnp.float32)


def general_body(
    tokens,
    lengths,
    cotangent,
    w_query,
    b_query,
    w_key,
    w_value,
    b_value,
    w_out,
    b_out,
    gain_one,
    shift_one,
    w_up,
    b_up,
    w_down,
    b_down,
    gain_two,
    shift_two,
):
    shards = (
        w_query,
        b_query,
        w_key,
        w_value,
        b_value,
        w_out,
        b_out,
        gain_one,
        shift_one,
        w_up,
        b_up,
        w_down,
        b_down,
        gain_two,
        shift_two,
    )
    per_batch = tokens.shape[0] // MB
    block_rows = tokens.shape[1]
    model_width = tokens.shape[2]
    head_count = H
    head_size = HD
    flat_rows = per_batch * block_rows
    full_length = block_rows * lax.axis_size("seq")
    offset = lax.axis_index("seq") * block_rows
    positions = jnp.arange(full_length, dtype=jnp.int32)
    own_positions = offset + jnp.arange(block_rows, dtype=jnp.int32)
    score_scale = head_size ** (-0.5)
    owners = lax.axis_size(("dp", "seq"))
    totals = [
        jnp.zeros((shard_piece.shape[0] * owners,) + shard_piece.shape[1:], jnp.float32)
        for shard_piece in shards
    ]
    outputs = []
    input_grads = []
    for micro_batch in range(MB):
        leading_row = micro_batch * per_batch
        own_tokens = tokens[leading_row : leading_row + per_batch]
        own_lengths = lengths[leading_row : leading_row + per_batch]
        own_cots = cotangent[leading_row : leading_row + per_batch]
        fore_weights = (
            lax.all_gather(shards[0], ("dp", "seq"), axis=0, tiled=True),
            lax.all_gather(shards[1], ("dp", "seq"), axis=0, tiled=True),
            lax.all_gather(shards[2], ("dp", "seq"), axis=0, tiled=True),
            lax.all_gather(shards[3], ("dp", "seq"), axis=0, tiled=True),
            lax.all_gather(shards[4], ("dp", "seq"), axis=0, tiled=True),
            lax.all_gather(shards[5], ("dp", "seq"), axis=0, tiled=True),
            lax.all_gather(shards[6], ("dp", "seq"), axis=0, tiled=True),
            lax.all_gather(shards[7], ("dp", "seq"), axis=0, tiled=True),
            lax.all_gather(shards[8], ("dp", "seq"), axis=0, tiled=True),
            lax.all_gather(shards[9], ("dp", "seq"), axis=0, tiled=True),
            lax.all_gather(shards[10], ("dp", "seq"), axis=0, tiled=True),
            lax.all_gather(shards[11], ("dp", "seq"), axis=0, tiled=True),
            lax.all_gather(shards[12], ("dp", "seq"), axis=0, tiled=True),
            lax.all_gather(shards[13], ("dp", "seq"), axis=0, tiled=True),
            lax.all_gather(shards[14], ("dp", "seq"), axis=0, tiled=True),
        )
        flat_tokens = own_tokens.reshape(flat_rows, model_width)
        query_low = (matmul(flat_tokens, fore_weights[0]) + widen(fore_weights[1])).astype(
            jnp.bfloat16
        )
        key_low = matmul(flat_tokens, fore_weights[2]).astype(jnp.bfloat16)
        value_low = (matmul(flat_tokens, fore_weights[3]) + widen(fore_weights[4])).astype(
            jnp.bfloat16
        )
        key_block = key_low.reshape(per_batch, block_rows, model_width)
        value_block = value_low.reshape(per_batch, block_rows, model_width)
        gathered_keys, gathered_values = (
            lax.all_gather(key_block, "seq", axis=1, tiled=True),
            lax.all_gather(value_block, "seq", axis=1, tiled=True),
        )
        query_heads = query_low.reshape(per_batch, block_rows, head_count, head_size)
        visible = (positions[None, :] < own_lengths[:, None])[:, None, None, :]

        def score_block(key_all):
            key_heads = key_all.reshape(per_batch, full_length, head_count, head_size)
            raw_scores = jnp.einsum(
                "pqhd,pkhd->phqk", query_heads, key_heads, preferred_element_type=jnp.float32
            )
            return jnp.where(visible, raw_scores * score_scale, -1e30)

        scores = score_block(gathered_keys)
        logarithm_totals = jax.nn.logsumexp(scores, axis=-1, keepdims=True)
        chances_low = jnp.exp(scores - logarithm_totals).astype(jnp.bfloat16)
        value_heads = gathered_values.reshape(per_batch, full_length, head_count, head_size)
        mixed_heads = jnp.einsum(
            "phqk,pkhd->pqhd", chances_low, value_heads, preferred_element_type=jnp.float32
        )
        mixed_low = mixed_heads.reshape(flat_rows, model_width).astype(jnp.bfloat16)
        branch = matmul(mixed_low, fore_weights[5]) + widen(fore_weights[6])
        resid_one = flat_tokens.astype(jnp.float32) + branch
        normed = layer_norm(resid_one, widen(fore_weights[7]), widen(fore_weights[8]))
        normed_low = normed.astype(jnp.bfloat16)
        hidden = matmul(normed_low, fore_weights[9]) + widen(fore_weights[10])
        active_low = gelu_exact(hidden).astype(jnp.bfloat16)
        feed_out = matmul(active_low, fore_weights[11]) + widen(fore_weights[12])
        resid_two = normed + feed_out
        result = layer_norm(resid_two, widen(fore_weights[13]), widen(fore_weights[14]))
        outputs.append(result.astype(jnp.bfloat16).reshape(per_batch, block_rows, model_width))
        back_weights = (
            lax.all_gather(shards[0], ("dp", "seq"), axis=0, tiled=True),
            lax.all_gather(shards[1], ("dp", "seq"), axis=0, tiled=True),
            lax.all_gather(shards[2], ("dp", "seq"), axis=0, tiled=True),
            lax.all_gather(shards[3], ("dp", "seq"), axis=0, tiled=True),
            lax.all_gather(shards[4], ("dp", "seq"), axis=0, tiled=True),
            lax.all_gather(shards[5], ("dp", "seq"), axis=0, tiled=True),
            lax.all_gather(shards[6], ("dp", "seq"), axis=0, tiled=True),
            lax.all_gather(shards[7], ("dp", "seq"), axis=0, tiled=True),
            lax.all_gather(shards[8], ("dp", "seq"), axis=0, tiled=True),
            lax.all_gather(shards[9], ("dp", "seq"), axis=0, tiled=True),
            lax.all_gather(shards[10], ("dp", "seq"), axis=0, tiled=True),
            lax.all_gather(shards[11], ("dp", "seq"), axis=0, tiled=True),
            lax.all_gather(shards[12], ("dp", "seq"), axis=0, tiled=True),
            lax.all_gather(shards[13], ("dp", "seq"), axis=0, tiled=True),
            lax.all_gather(shards[14], ("dp", "seq"), axis=0, tiled=True),
        )
        live_rows = (
            (own_positions[None, :] < own_lengths[:, None])
            .astype(jnp.float32)
            .reshape(flat_rows, 1)
        )
        incoming = own_cots.reshape(flat_rows, model_width).astype(jnp.float32) * live_rows
        _, second_pull = jax.vjp(
            layer_norm, resid_two, widen(back_weights[13]), widen(back_weights[14])
        )
        grad_two, grad_gain_two, grad_shift_two = second_pull(incoming)
        feed_low = grad_two.astype(jnp.bfloat16)
        totals[11] = totals[11] + former_product(active_low, feed_low)
        totals[12] = totals[12] + jnp.sum(feed_low.astype(jnp.float32), 0)
        grad_active = latter_product(feed_low, back_weights[11])
        _, gelu_pull = jax.vjp(gelu_exact, hidden)
        up_low = gelu_pull(grad_active)[0].astype(jnp.bfloat16)
        totals[9] = totals[9] + former_product(normed_low, up_low)
        totals[10] = totals[10] + jnp.sum(up_low.astype(jnp.float32), 0)
        grad_normed = latter_product(up_low, back_weights[9]) + grad_two
        _, first_pull = jax.vjp(
            layer_norm, resid_one, widen(back_weights[7]), widen(back_weights[8])
        )
        grad_one, grad_gain_one, grad_shift_one = first_pull(grad_normed)
        branch_low = grad_one.astype(jnp.bfloat16)
        totals[5] = totals[5] + former_product(mixed_low, branch_low)
        totals[6] = totals[6] + jnp.sum(branch_low.astype(jnp.float32), 0)
        dmix_low = latter_product(branch_low, back_weights[5]).astype(jnp.bfloat16)
        dmix_heads = dmix_low.reshape(per_batch, block_rows, head_count, head_size)
        back_keys, backward_value_rows = (gathered_keys, gathered_values)
        chances = jnp.exp(score_block(back_keys) - logarithm_totals)
        back_value_heads = backward_value_rows.reshape(
            per_batch, full_length, head_count, head_size
        )
        back_key_heads = back_keys.reshape(per_batch, full_length, head_count, head_size)
        grad_chances = jnp.einsum(
            "pqhd,pkhd->phqk", dmix_heads, back_value_heads, preferred_element_type=jnp.float32
        )
        row_inner = jnp.sum(grad_chances * chances, -1, keepdims=True)
        dscore_low = (score_scale * (chances * (grad_chances - row_inner))).astype(jnp.bfloat16)
        dquery_low = jnp.einsum(
            "phqk,pkhd->pqhd", dscore_low, back_key_heads, preferred_element_type=jnp.float32
        )
        dquery_low = dquery_low.reshape(flat_rows, model_width).astype(jnp.bfloat16)
        chance_low = chances.astype(jnp.bfloat16)
        value_terms = jnp.einsum(
            "phqk,pqhd->pkhd", chance_low, dmix_heads, preferred_element_type=jnp.float32
        )
        key_terms = jnp.einsum(
            "phqk,pqhd->pkhd", dscore_low, query_heads, preferred_element_type=jnp.float32
        )
        key_sums, value_sums = (
            lax.psum_scatter(
                key_terms.reshape(per_batch, full_length, model_width).astype(jnp.bfloat16),
                "seq",
                scatter_dimension=1,
                tiled=True,
            ).astype(jnp.float32),
            lax.psum_scatter(
                value_terms.reshape(per_batch, full_length, model_width).astype(jnp.bfloat16),
                "seq",
                scatter_dimension=1,
                tiled=True,
            ).astype(jnp.float32),
        )
        dkey_low = key_sums.reshape(flat_rows, model_width).astype(jnp.bfloat16)
        dvalue_low = value_sums.reshape(flat_rows, model_width).astype(jnp.bfloat16)
        totals[0] = totals[0] + former_product(flat_tokens, dquery_low)
        totals[1] = totals[1] + jnp.sum(dquery_low.astype(jnp.float32), 0)
        totals[2] = totals[2] + former_product(flat_tokens, dkey_low)
        totals[3] = totals[3] + former_product(flat_tokens, dvalue_low)
        totals[4] = totals[4] + jnp.sum(dvalue_low.astype(jnp.float32), 0)
        totals[7] = totals[7] + grad_gain_one
        totals[8] = totals[8] + grad_shift_one
        totals[13] = totals[13] + grad_gain_two
        totals[14] = totals[14] + grad_shift_two
        grad_input = (
            latter_product(dquery_low, back_weights[0])
            + latter_product(dkey_low, back_weights[2])
            + latter_product(dvalue_low, back_weights[3])
            + grad_one
        )
        input_grads.append(grad_input.reshape(per_batch, block_rows, model_width))
    owned = lax.psum_scatter(tuple(totals), ("dp", "seq"), scatter_dimension=0, tiled=True)
    output = jnp.concatenate(outputs, 0)
    grad_tokens = jnp.concatenate(input_grads, 0)
    return (
        output,
        grad_tokens,
        owned[0],
        owned[1],
        owned[2],
        owned[3],
        owned[4],
        owned[5],
        owned[6],
        owned[7],
        owned[8],
        owned[9],
        owned[10],
        owned[11],
        owned[12],
        owned[13],
        owned[14],
    )


LOG2E = 1.4426950408889634
PAD = 16
VMEM = 60 << 20
RATE = 1e9


def cost(microseconds):
    return pl.CostEstimate(flops=int(microseconds * RATE), bytes_accessed=0, transcendentals=0)


def contract(former, latter, dim_former, dim_latter):
    return lax.dot_general(
        former,
        latter,
        (((dim_former,), (dim_latter,)), ((), ())),
        preferred_element_type=jnp.float32,
    )


def mix_kernel(scale, chunk, qt, kt, vt, bias, mixed, total, probs, queries, vals):
    size, slots = kt.shape[1], kt.shape[2]
    query = qt[0].astype(jnp.float32) * scale
    high = query.astype(jnp.bfloat16)
    low = (query - high.astype(jnp.float32)).astype(jnp.bfloat16)
    row = lax.broadcasted_iota(jnp.int32, (PAD, slots), 0)
    first = jnp.where(row == 0, 1.0, 0.0).astype(jnp.bfloat16)
    queries[...] = jnp.concatenate([high, low, first], 0).T
    keys = jnp.concatenate([kt[0], kt[0], bias[...]], 0)
    vals[...] = jnp.concatenate([vt[0], jnp.ones((PAD, slots), jnp.bfloat16)], 0).T

    def block(at, seen):
        cut = slice(at, at + chunk)
        scores = matmul(queries[cut], keys)
        top = jnp.max(scores[:, :seen], 1, keepdims=True)
        part = jnp.exp2(scores - top).astype(jnp.bfloat16)
        probs[0, cut] = part
        sums = matmul(part, vals[...]).T
        weight = sums[size : size + 1]
        mixed[0, :, cut] = (sums[:size] / weight).astype(mixed.dtype)
        total[0, :, cut] = weight
        return jnp.max(weight)

    largest = [block(at, 256) for at in range(0, slots, chunk)]

    @pl.when(jnp.logical_not(functools.reduce(jnp.maximum, largest) < 2.0**60))
    def _():
        for at in range(0, slots, chunk):
            block(at, slots)


def mix(qt, kt, vt, bias, scale):
    heads, size, slots = qt.shape
    whole = pl.BlockSpec((1, size, slots), lambda i: (i, 0, 0))
    return pl.pallas_call(
        functools.partial(mix_kernel, scale, 512),
        grid=(heads,),
        in_specs=[whole, whole, whole, pl.BlockSpec((PAD, slots), lambda i: (0, 0))],
        out_specs=[
            whole,
            pl.BlockSpec((1, 1, slots), lambda i: (i, 0, 0)),
            pl.BlockSpec((1, slots, slots), lambda i: (i, 0, 0)),
        ],
        out_shape=[
            jax.ShapeDtypeStruct((heads, size, slots), jnp.bfloat16),
            jax.ShapeDtypeStruct((heads, 1, slots), jnp.float32),
            jax.ShapeDtypeStruct((heads, slots, slots), jnp.bfloat16),
        ],
        scratch_shapes=[
            pltpu.VMEM((slots, 2 * size + PAD), jnp.bfloat16),
            pltpu.VMEM((slots, size + PAD), jnp.bfloat16),
        ],
        compiler_params=pltpu.CompilerParams(vmem_limit_bytes=VMEM),
        cost_estimate=cost(65),
        name="mix",
    )(qt, kt, vt, bias)


def unmix_kernel(scale, chunk, probs, qt, kt, vt, gt, mt, total, out, keys):
    slots = kt.shape[2]
    grad = (gt[0].astype(jnp.float32) / total[0]).astype(jnp.bfloat16)
    inner = jnp.sum(grad.astype(jnp.float32) * mt[0].astype(jnp.float32), 0, keepdims=True)
    inner = jnp.broadcast_to(inner, (8, slots)).T[:, :1]
    turned = grad.T
    keys[...] = kt[0].T
    dk = dv = None
    for at in range(0, slots, chunk):
        cut = slice(at, at + chunk)
        prob = probs[0, cut]
        dprob = matmul(turned[cut], vt[0])
        dscore = (prob.astype(jnp.float32) * (dprob - inner[cut])).astype(jnp.bfloat16)
        out[0, 0, :, cut] = (matmul(dscore, keys[...]) * scale).T.astype(jnp.bfloat16)
        value_term = matmul(grad[:, cut], prob)
        key_term = matmul(qt[0, :, cut], dscore)
        dv = value_term if dv is None else dv + value_term
        dk = key_term if dk is None else dk + key_term
    out[1, 0] = (dk * scale).astype(jnp.bfloat16)
    out[2, 0] = dv.astype(jnp.bfloat16)


def unmix(probs, qt, kt, vt, gt, mt, total, scale):
    heads, size, slots = qt.shape
    whole = pl.BlockSpec((1, size, slots), lambda i: (i, 0, 0))
    return pl.pallas_call(
        functools.partial(unmix_kernel, scale, 256),
        grid=(heads,),
        in_specs=[pl.BlockSpec((1, slots, slots), lambda i: (i, 0, 0))]
        + [whole] * 5
        + [pl.BlockSpec((1, 1, slots), lambda i: (i, 0, 0))],
        out_specs=pl.BlockSpec((3, 1, size, slots), lambda i: (0, i, 0, 0)),
        out_shape=jax.ShapeDtypeStruct((3, heads, size, slots), jnp.bfloat16),
        scratch_shapes=[pltpu.VMEM((slots, size), jnp.bfloat16)],
        compiler_params=pltpu.CompilerParams(vmem_limit_bytes=VMEM),
        cost_estimate=cost(95),
        name="unmix",
    )(probs, qt, kt, vt, gt, mt, total)


def exchange(blocks):
    return lax.all_to_all(blocks, "seq", 0, 0, tiled=True)


def take(array, index):
    return lax.dynamic_index_in_dim(array, index, 0, keepdims=False)


def columns(*vectors):
    rows = vectors[0].shape[0]
    stack = jnp.concatenate(vectors).reshape(-1, rows)
    unit = jnp.eye(stack.shape[0], 128, dtype=stack.dtype)
    return contract(stack, unit, 0, 0).astype(stack.dtype)


def scattered(rows):
    me = lax.axis_index("seq")
    size = lax.axis_size("seq")
    parts = rows.reshape(size, rows.shape[0] // size, rows.shape[1])
    total = take(parts, me).astype(jnp.float32)
    for step in range(1, size):
        pairs = [(i, i ^ step) for i in range(size)]
        came = lax.ppermute(take(parts, me ^ step), "seq", pairs)
        total = total + came.astype(jnp.float32)
    return total


def row_sums(array):
    return jnp.sum(array, 0, keepdims=True)


def project_kernel(x, w, vec, qt, kt, vt):
    width = x.shape[1]
    bias = vec[...].T[:8].astype(jnp.float32)
    outs = matmul(x[...], w[...])
    for i, out in enumerate((qt, kt, vt)):
        part = outs[:, i * width : (i + 1) * width]
        if i != 1:
            part = part + bias[i // 2 : i // 2 + 1]
        out[...] = part.astype(jnp.bfloat16).T


def project(x, first, rows):
    slots, width = x.shape
    flat = pl.BlockSpec((width, rows), lambda i: (0, i))
    one = pl.Buffered(1)
    return pl.pallas_call(
        project_kernel,
        grid=(slots // rows,),
        in_specs=[
            pl.BlockSpec((rows, width), lambda i: (i, 0)),
            pl.BlockSpec((width, 3 * width), lambda i: (0, 0), pipeline_mode=one),
            pl.BlockSpec((width, 128), lambda i: (0, 3 * width // 128)),
        ],
        out_specs=[flat] * 3,
        out_shape=[jax.ShapeDtypeStruct((width, slots), jnp.bfloat16)] * 3,
        compiler_params=pltpu.CompilerParams(vmem_limit_bytes=VMEM),
        cost_estimate=cost(11),
        name="project",
    )(x, first, first)


def norm(rows):
    centre = rows - jnp.mean(rows, -1, keepdims=True)
    rstd = lax.rsqrt(jnp.mean(centre * centre, -1, keepdims=True) + epsilon)
    return centre * rstd, rstd


def norm_back(unit, rstd, grad):
    mean = jnp.mean(grad, -1, keepdims=True)
    inner = jnp.mean(grad * unit, -1, keepdims=True)
    return rstd * (grad - mean - unit * inner)


def feed_kernel(
    x, mt, cot, live, vec, wo, wu, wd, output, grad_one, gt, left, right, sums, slope,
):
    width = x.shape[1]
    wide = wu.shape[1]
    step = pl.program_id(0)
    known = vec[...].T[:16].astype(jnp.float32)
    bo, g1, s1, bd, g2, s2 = (known[i : i + 1] for i in range(6))
    mixed = mt[...].T
    left[:, wide + width :] = mixed
    resid = x[...].astype(jnp.float32) + matmul(mixed, wo[...]) + bo
    unit_one, rstd_one = norm(resid)
    normed = unit_one * g1 + s1
    low = normed.astype(jnp.bfloat16)
    left[:, :width] = low
    resid = normed + bd
    for at in range(0, wide, width):
        cut = slice(at, at + width)
        hidden = matmul(low, wu[:, cut]) + known[6 + at // width : 7 + at // width]
        share = 0.5 + 0.5 * lax.erf(hidden * 0.7071067811865476)
        bell = jnp.exp2(hidden * hidden * -0.7213475204444817) * 0.3989422804014327
        slope[:, cut] = (share + hidden * bell).astype(jnp.bfloat16)
        active = (hidden * share).astype(jnp.bfloat16)
        left[:, width + at : 2 * width + at] = active
        resid = resid + matmul(active, wd[:, cut])
    unit_two, rstd_two = norm(resid)
    output[...] = (unit_two * g2 + s2).astype(jnp.bfloat16)
    incoming = cot[...].astype(jnp.float32) * live[...]
    grad_two = norm_back(unit_two, rstd_two, incoming * g2)
    feed = grad_two.astype(jnp.bfloat16)
    right[:, wide : wide + width] = feed
    grad = grad_two
    up_rows = []
    for at in range(0, wide, width):
        cut = slice(at, at + width)
        part = contract(feed, wd[:, cut], 1, 1) * slope[:, cut].astype(jnp.float32)
        part = part.astype(jnp.bfloat16)
        right[:, cut] = part
        up_rows.append(row_sums(part.astype(jnp.float32)))
        grad = grad + contract(part, wu[:, cut], 1, 1)
    first = norm_back(unit_one, rstd_one, grad * g1)
    grad_one[...] = first
    branch = first.astype(jnp.bfloat16)
    right[:, wide + width :] = branch
    gt[...] = contract(wo[...], branch, 1, 1).astype(jnp.bfloat16)
    rows = [
        row_sums(branch.astype(jnp.float32)),
        row_sums(grad * unit_one),
        row_sums(grad),
        row_sums(feed.astype(jnp.float32)),
        row_sums(incoming * unit_two),
        row_sums(incoming),
    ]
    blank = [jnp.zeros((2, width), jnp.float32)]
    rows = jnp.concatenate(blank + rows + up_rows, 0)

    @pl.when(step == 0)
    def _():
        sums[...] = rows

    @pl.when(step > 0)
    def _():
        sums[...] += rows


def feed(x, mt, cot, live, second, wide, rows):
    slots, width = x.shape
    one = pl.Buffered(1)
    flat = pl.BlockSpec((rows, width), lambda i: (i, 0))
    tall = pl.BlockSpec((width, rows), lambda i: (0, i))
    stack = wide + 2 * width
    broad = pl.BlockSpec((rows, stack), lambda i: (i, 0))
    low = jnp.bfloat16
    return pl.pallas_call(
        feed_kernel,
        grid=(slots // rows,),
        in_specs=[
            flat,
            tall,
            flat,
            pl.BlockSpec((rows, 1), lambda i: (i, 0)),
            pl.BlockSpec((width, 128), lambda i: (0, (2 * wide + width) // 128)),
            pl.BlockSpec((width, width), lambda i: (0, 2 * wide // width), pipeline_mode=one),
            pl.BlockSpec((width, wide), lambda i: (0, 0), pipeline_mode=one),
            pl.BlockSpec((width, wide), lambda i: (0, 1), pipeline_mode=one),
        ],
        out_specs=[
            flat,
            flat,
            tall,
            broad,
            broad,
            pl.BlockSpec((8 + wide // width, width), lambda i: (0, 0)),
        ],
        out_shape=[
            jax.ShapeDtypeStruct((slots, width), low),
            jax.ShapeDtypeStruct((slots, width), jnp.float32),
            jax.ShapeDtypeStruct((width, slots), low),
            jax.ShapeDtypeStruct((slots, stack), low),
            jax.ShapeDtypeStruct((slots, stack), low),
            jax.ShapeDtypeStruct((8 + wide // width, width), jnp.float32),
        ],
        scratch_shapes=[pltpu.VMEM((rows, wide), low)],
        compiler_params=pltpu.CompilerParams(vmem_limit_bytes=VMEM),
        cost_estimate=cost(70),
        name="feed",
    )(x, mt, cot, live, second, second, second, second)


def feed_weights_kernel(left, right, d_w):
    d_w[...] = contract(left[...], right[...], 0, 0).astype(d_w.dtype)


def feed_weights(left, right, width):
    slots, stack = left.shape
    parts = stack // width - 2
    return pl.pallas_call(
        feed_weights_kernel,
        grid=(2 * parts + 1,),
        in_specs=[
            pl.BlockSpec((slots, width), lambda i: (0, jnp.maximum(i - parts + 1, 0))),
            pl.BlockSpec(
                (slots, width), lambda i: (0, jnp.minimum(i, parts) + i // (2 * parts))
            ),
        ],
        out_specs=pl.BlockSpec((width, width), lambda i: (0, i)),
        out_shape=jax.ShapeDtypeStruct((width, (2 * parts + 1) * width), jnp.bfloat16),
        compiler_params=pltpu.CompilerParams(vmem_limit_bytes=VMEM),
        cost_estimate=cost(26),
        name="feed_weights",
    )(left, right)


def inputs_kernel(grads, weights, grad_one, low):
    low[...] = (contract(grads[...], weights[...], 0, 1) + grad_one[...]).astype(low.dtype)


def inputs(grads, first, grad_one, rows):
    depth, slots = grads.shape
    width = first.shape[0]
    flat = pl.BlockSpec((rows, width), lambda i: (i, 0))
    return pl.pallas_call(
        inputs_kernel,
        grid=(slots // rows,),
        in_specs=[
            pl.BlockSpec((depth, rows), lambda i: (0, i)),
            pl.BlockSpec((width, depth), lambda i: (0, 0), pipeline_mode=pl.Buffered(1)),
            flat,
        ],
        out_specs=flat,
        out_shape=jax.ShapeDtypeStruct((slots, width), jnp.bfloat16),
        compiler_params=pltpu.CompilerParams(vmem_limit_bytes=VMEM),
        cost_estimate=cost(12),
        name="inputs",
    )(grads, first, grad_one)


def input_weights_kernel(x, grads, rows, d_w, edges):
    step, last = pl.program_id(0), pl.num_programs(0) - 1
    width = x.shape[1]
    depth = 3 * width
    size = grads.shape[0]
    grad = grads[...]
    product = contract(x[...], grad, 0, 1).astype(d_w.dtype)
    edge = jnp.sum(grad.astype(jnp.float32), 1, keepdims=True)
    for i in range(depth // size):

        @pl.when(step == i)
        def _(i=i):
            d_w[:, i * size : (i + 1) * size] = product
            column, top = i * size // width, i * size % width
            edges[top : top + size, column : column + 1] = edge

    @pl.when(step == last)
    def _():
        known = rows[...]
        tall = jnp.concatenate([known, jnp.zeros((128 - known.shape[0], width), jnp.float32)], 0).T
        column = lax.broadcasted_iota(jnp.int32, (width, 128), 1)
        sums = edges[...]
        columns = jnp.where(column == 0, sums[:, :1], jnp.where(column == 1, sums[:, 2:3], tall))
        d_w[:, depth:] = columns.astype(d_w.dtype)


def input_weights(x, grads, rows, size):
    slots, width = x.shape
    depth = grads.shape[0]
    one = pl.Buffered(1)
    return pl.pallas_call(
        input_weights_kernel,
        grid=(depth // size,),
        in_specs=[
            pl.BlockSpec((slots, width), lambda i: (0, 0), pipeline_mode=one),
            pl.BlockSpec((size, slots), lambda i: (i, 0)),
            pl.BlockSpec(rows.shape, lambda i: (0, 0)),
        ],
        out_specs=pl.BlockSpec((width, depth + 128), lambda i: (0, 0)),
        out_shape=jax.ShapeDtypeStruct((width, depth + 128), jnp.bfloat16),
        scratch_shapes=[pltpu.VMEM((width, 128), jnp.float32)],
        compiler_params=pltpu.CompilerParams(vmem_limit_bytes=VMEM),
        cost_estimate=cost(12),
        name="input_weights",
    )(x, grads, rows)


def whole_body(
    tokens,
    lengths,
    cotangent,
    w_query,
    b_query,
    w_key,
    w_value,
    b_value,
    w_out,
    b_out,
    gain_one,
    shift_one,
    w_up,
    b_up,
    w_down,
    b_down,
    gain_two,
    shift_two,
):
    count, block, width = tokens.shape
    slots = count * block
    wide = w_up.shape[1]
    rows = w_query.shape[0]
    axes = ("dp", "seq")
    me = lax.axis_index("seq")
    heads, size = H, HD
    scale = size ** (-0.5)
    times = wide // width

    x = exchange(tokens).reshape(slots, width)

    first = jnp.concatenate([w_query, w_key, w_value, columns(b_query, b_value)], 1)
    first = lax.all_gather(first, "seq", axis=0, tiled=True)
    first = lax.all_gather(first, "dp", axis=0, tiled=True)
    owners = width // rows
    mixed_up = w_up.reshape(rows, owners, times, rows).transpose(0, 2, 1, 3).reshape(rows, wide)
    downs = [w_down[i * rows : (i + 1) * rows] for i in range(times)]
    vectors = columns(b_out, gain_one, shift_one, b_down, gain_two, shift_two, b_up)
    second = jnp.concatenate([mixed_up] + downs + [w_out, vectors], 1)

    length = take(lengths, me)
    live = jnp.arange(slots, dtype=jnp.int32) < length
    bias = jnp.where(live, 0.0, -1e30).astype(jnp.bfloat16)
    bias = jnp.pad(bias[None, :], ((0, PAD - 1), (0, 0)))
    live = live[:, None].astype(jnp.float32)
    x, live, bias, cotangent = lax.optimization_barrier((x, live, bias, cotangent))
    second, first, x = lax.optimization_barrier((second, first, x))
    second = lax.all_gather(second, axes, axis=0, tiled=True)

    def by_head(array):
        return array.reshape(heads, size, slots)

    qt, kt, vt = project(x, first, block)
    cot = exchange(cotangent).reshape(slots, width)
    qt, kt, vt = (by_head(a) for a in (qt, kt, vt))
    mt, total, probs = mix(qt, kt, vt, bias, scale * LOG2E)
    result, grad_one, gt, left, right, sums = feed(
        x, mt.reshape(width, slots), cot, live, second, wide, block
    )
    late = feed_weights(left, right, width)
    gt, late = lax.optimization_barrier((gt, late))
    late = lax.psum_scatter(late, "dp", scatter_dimension=0, tiled=True)
    output = exchange(result.reshape(count, block, width))
    grads = unmix(probs, qt, kt, vt, by_head(gt), mt, total, scale)
    grads, output = lax.optimization_barrier((grads, output))
    grads = grads.reshape(3 * width, slots)
    early = input_weights(x, grads, sums, width)
    early, late, grads = lax.optimization_barrier((early, late, grads))
    early = lax.psum_scatter(early, "dp", scatter_dimension=0, tiled=True)
    late = scattered(late)
    low = inputs(grads, first, grad_one, block)
    grad_tokens = exchange(low.reshape(count, block, width))
    early, low = lax.optimization_barrier((early, low))
    early = scattered(early)
    grad_tokens, early = lax.optimization_barrier((grad_tokens, early))
    grad_tokens = grad_tokens.astype(jnp.float32)
    o_wq, o_wk, o_wv = (early[:, i * width : (i + 1) * width] for i in range(3))
    vec = early[:, 3 * width :]
    o_wu = late[:, :wide].reshape(rows, times, owners, rows).transpose(0, 2, 1, 3).reshape(rows, wide)
    o_wd = jnp.concatenate(
        [late[:, wide + i * width : wide + (i + 1) * width] for i in range(times)], 0
    )
    o_wo = late[:, 2 * wide :]
    o_bq, o_bv, o_bo, o_g1, o_s1, o_bd, o_g2, o_s2 = (vec[:, i] for i in range(8))
    o_bu = vec[:, 8 : 8 + times].T.reshape(rows * times)
    return (
        output,
        grad_tokens,
        o_wq,
        o_bq,
        o_wk,
        o_wv,
        o_bv,
        o_wo,
        o_bo,
        o_g1,
        o_s1,
        o_wu,
        o_bu,
        o_wd,
        o_bd,
        o_g2,
        o_s2,
    )


def body(*arrays):
    count = arrays[0].shape[0]
    fits = count == lax.axis_size("seq") and count & (count - 1) == 0
    return whole_body(*arrays) if fits else general_body(*arrays)


def solution(mesh):
    in_specs = (
        P("dp", "seq", None),
        P("dp"),
        P("dp", "seq", None),
        P(("dp", "seq"), None),
        P(("dp", "seq")),
        P(("dp", "seq"), None),
        P(("dp", "seq"), None),
        P(("dp", "seq")),
        P(("dp", "seq"), None),
        P(("dp", "seq")),
        P(("dp", "seq")),
        P(("dp", "seq")),
        P(("dp", "seq"), None),
        P(("dp", "seq")),
        P(("dp", "seq"), None),
        P(("dp", "seq")),
        P(("dp", "seq")),
        P(("dp", "seq")),
    )
    out_specs = (
        P("dp", "seq", None),
        P("dp", "seq", None),
        P(("dp", "seq"), None),
        P(("dp", "seq")),
        P(("dp", "seq"), None),
        P(("dp", "seq"), None),
        P(("dp", "seq")),
        P(("dp", "seq"), None),
        P(("dp", "seq")),
        P(("dp", "seq")),
        P(("dp", "seq")),
        P(("dp", "seq"), None),
        P(("dp", "seq")),
        P(("dp", "seq"), None),
        P(("dp", "seq")),
        P(("dp", "seq")),
        P(("dp", "seq")),
    )
    return jax.shard_map(body, mesh=mesh, in_specs=in_specs, out_specs=out_specs, check_vma=False)
```
